32 devices in a mesh: dp: 16 (over z, y, x), seq: 2 (over core).
Axes of the slice: x: 2, y: 2, z: 4, core: 2. Of those that a mesh axis runs over, the one named last changes fastest.
Arguments:
- inputs: bfloat16 [16, 512, 2048], P('dp', 'seq'), may hold values from -6 to 6
- starts: int32 [16, 512], P('dp', 'seq'), may hold values from 0 to 1, as said below
- norm_attn: bfloat16 [2048], P('dp'), may hold values from 0.5 to 1.5
- w_query: bfloat16 [2048, 2048], P('dp'), may hold values from -0.25 to 0.25
- w_key: bfloat16 [2048, 2048], P('dp'), may hold values from -0.25 to 0.25
- w_value: bfloat16 [2048, 2048], P('dp'), may hold values from -0.125 to 0.125
- w_forget: bfloat16 [2048, 256], P('dp'), may hold values from -0.125 to 0.125
- gate_bias: bfloat16 [256], P('dp'), may hold values from -1 to 6
- w_out: bfloat16 [2048, 2048], P('dp'), may hold values from -0.5 to 0.5
- norm_ffn: bfloat16 [2048], P('dp'), may hold values from 0.5 to 1.5
- w_gate: bfloat16 [2048, 5632], P('dp'), may hold values from -0.125 to 0.125
- w_up: bfloat16 [2048, 5632], P('dp'), may hold values from -0.125 to 0.125
- w_down: bfloat16 [5632, 2048], P('dp'), may hold values from -0.15625 to 0.15625
- cotangent: bfloat16 [16, 512, 2048], P('dp', 'seq'), may hold values from -6 to 6
Outputs:
- output: bfloat16 [16, 512, 2048], P('dp', 'seq')
- grad_input: float32 [16, 512, 2048], P('dp', 'seq')
- grad_norm_attn: float32 [2048], P('dp')
- grad_w_query: float32 [2048, 2048], P('dp')
- grad_w_key: float32 [2048, 2048], P('dp')
- grad_w_value: float32 [2048, 2048], P('dp')
- grad_w_forget: float32 [2048, 256], P('dp')
- grad_gate_bias: float32 [256], P('dp')
- grad_w_out: float32 [2048, 2048], P('dp')
- grad_norm_ffn: float32 [2048], P('dp')
- grad_w_gate: float32 [2048, 5632], P('dp')
- grad_w_up: float32 [2048, 5632], P('dp')
- grad_w_down: float32 [5632, 2048], P('dp')
The draws below stay inside these ranges and needn't reach their ends.
Inputs may be any that keep to these rules, and one draw needn't show every extreme that they name: 1 marks the first position of a document, 0 any other; position 0 of every row is 1, and no document starts at positions 192 to 319 of a row.
All inputs are finite; a program needn't handle non-finite values.
Results may differ from the reference program's by a relative error of at most 0.013.
Values may be sent and summed in bfloat16 or wider, within the bound.
A program may use at most 448 MiB of HBM per device.

```python
import jax
import jax.numpy as jnp
from jax import lax

D = 2048
HEADS = 4
SLOTS = 64
FF = 5632
SEG = 256
BLOCK = 64
SEQ_LEN = 512
ROWS = 16


def draw_starts(key, part):
    key = jax.random.fold_in(key, 7)
    marks = jax.random.randint(key, (ROWS, SEQ_LEN), 0, SEG)
    places = jnp.arange(SEQ_LEN)
    quiet_zone = (places >= SEG - SEG // 4) & (places < SEG + SEG // 4)
    marked = jnp.where((marks < 2) & jnp.logical_not(quiet_zone)[None, :], 1, 0)
    marked = jnp.where((places == 0)[None, :], 1, marked)
    return marked.astype(jnp.int32)


def block_scale(key, dims, split, low, largest):
    level, own = 1.0, jax.random.fold_in(key, 6)
    for position, shards_of in split:
        draws = jnp.exp(jax.random.uniform(jax.random.fold_in(own, position), (shards_of,), jnp.float32, low / len(split), largest / len(split)))
        level = level * jnp.repeat(draws, dims[position] // shards_of).reshape([-1 if axis == position else 1 for axis in range(len(dims))])
    return level


def centred(key, extent, width, most, split=(), held_as=jnp.bfloat16):
    loudness = block_scale(key, extent, split, -0.22, 0.18) if split else 1.0
    array = jax.random.normal(key, extent, jnp.float32) * width * loudness
    return jnp.minimum(jnp.maximum(array, -most), most).astype(held_as)


def setup_inputs(seed: int = 0) -> dict:
    streams_of = jax.random.split(jax.random.key(seed), 15)
    return {
        "inputs": centred(streams_of[0], (ROWS, SEQ_LEN, D), 1.0, 6.0, ((0, 16), (1, 2))),
        "starts": draw_starts(jax.random.fold_in(streams_of[14], 71), 0),
        "norm_attn": jnp.clip(1.0 + 0.1 * jax.random.normal(streams_of[2], (D,), jnp.float32), 0.5, 1.5).astype(jnp.bfloat16),
        "w_query": centred(streams_of[3], (D, D), (D // 4) ** -0.5, 0.25, ((0, 16),)),
        "w_key": centred(streams_of[4], (D, D), (D // 4) ** -0.5, 0.25, ((0, 16),)),
        "w_value": centred(streams_of[5], (D, D), D ** -0.5, 0.125, ((0, 16),)),
        "w_forget": centred(streams_of[6], (D, HEADS * SLOTS), D ** -0.5, 0.125, ((0, 16),)),
        "gate_bias": jnp.clip(-1.0 + 7.0 * jax.random.uniform(streams_of[7], (HEADS * SLOTS,), jnp.float32) ** block_scale(streams_of[7], (HEADS * SLOTS,), ((0, 16),), -0.2, 0.2), -1.0, 6.0).astype(jnp.bfloat16),
        "w_out": centred(streams_of[8], (D, D), (D // 16) ** -0.5, 0.5, ((0, 16),)),
        "norm_ffn": jnp.clip(1.0 + 0.1 * jax.random.normal(streams_of[9], (D,), jnp.float32), 0.5, 1.5).astype(jnp.bfloat16),
        "w_gate": centred(streams_of[10], (D, FF), D ** -0.5, 0.125, ((0, 16),)),
        "w_up": centred(streams_of[11], (D, FF), D ** -0.5, 0.125, ((0, 16),)),
        "w_down": centred(streams_of[12], (FF, D), (FF // 4) ** -0.5, 0.15625, ((0, 16),)),
        "cotangent": centred(streams_of[13], (ROWS, SEQ_LEN, D), 1.0, 6.0, ((0, 16), (1, 2))),
    }


EPSILON = 1e-06
EXACT_PRECISION = lax.Precision.HIGHEST

@jax.custom_vjp
def low(v):
    return lax.optimization_barrier(v.astype(jnp.bfloat16)).astype(jnp.float32)

@jax.custom_vjp
def low_back(v):
    return v

def low_keep(v):
    return (low(v), None)

def low_pass(kept, grad):
    return (grad,)

def back_keep(v):
    return (v, None)

def back_low(kept, grad):
    return (low(grad),)
low.defvjp(low_keep, low_pass)
low_back.defvjp(back_keep, back_low)

def rms_scale(features, scale_gain):
    return features * lax.rsqrt(lax.optimization_barrier(jnp.mean(features * features, axis=-1, keepdims=True)) + EPSILON) * scale_gain

def block_weights(log_forget, begins):
    positions = log_forget.shape[0]
    cumulative = jnp.cumsum(log_forget, axis=0)
    doc_count = jnp.cumsum(begins.astype(jnp.float32))
    places = jnp.arange(positions)
    same_doc = (doc_count[:, None] == doc_count[None, :]) & (places[None, :] <= places[:, None])
    spread = jnp.minimum(cumulative[:, None] - cumulative[None, :], 0.0)
    weight = jnp.where(same_doc[:, :, None, None], jnp.exp(spread), 0.0) * (-jnp.expm1(log_forget))[None]
    incoming_share = jnp.where((doc_count == 0.0)[:, None, None], jnp.exp(cumulative), 0.0)
    return (weight, incoming_share)

def mix_block(carry_state, pieces):
    slot_key_state, slot_value_state = carry_state
    query_rows, key_matrix, value_matrix, log_forget, begins = pieces
    weight, incoming_share = block_weights(log_forget, begins)
    logit_scale = query_rows.shape[-1] ** (-0.5)
    inner_prod = jnp.einsum('thd,shd->tsh', query_rows, key_matrix, precision=EXACT_PRECISION)
    slot_logits = jnp.einsum('tshm,tsh->thm', weight, inner_prod, precision=EXACT_PRECISION)
    slot_logits = logit_scale * (slot_logits + incoming_share * jnp.einsum('ugj,auj->aug', slot_key_state, query_rows, precision=EXACT_PRECISION))
    slot_weights = jax.nn.softmax(slot_logits, axis=-1)
    paired = jnp.einsum('thm,tshm->tsh', slot_weights, weight, precision=EXACT_PRECISION)
    blended_output = jnp.einsum('tsh,shd->thd', paired, value_matrix, precision=EXACT_PRECISION)
    blended_output = blended_output + jnp.einsum('cfx,fxv->cfv', slot_weights * incoming_share, slot_value_state, precision=EXACT_PRECISION)
    closing_row = weight[-1]
    final_incoming = incoming_share[-1][:, :, None]
    slot_key_state = jnp.einsum('xek,xeu->eku', closing_row, key_matrix, precision=EXACT_PRECISION) + final_incoming * slot_key_state
    slot_value_state = jnp.einsum('xek,xeu->eku', closing_row, value_matrix, precision=EXACT_PRECISION) + final_incoming * slot_value_state
    return ((slot_key_state, slot_value_state), blended_output)

def run_blocks(carry_state, query_rows, key_matrix, value_matrix, log_forget, begins):
    block_count = query_rows.shape[0] // BLOCK
    pieces = tuple((member.reshape((block_count, BLOCK) + member.shape[1:]) for member in (query_rows, key_matrix, value_matrix, log_forget, begins)))
    carry_state, blended_output = lax.scan(jax.checkpoint(mix_block), carry_state, pieces)
    return (carry_state, blended_output.reshape(query_rows.shape))

def layer(row_input, row_starts, params):
    gain_attn, full_query, full_key, full_value, full_forget, full_bias, full_out, gain_ffn, full_gate, full_up, full_down = params
    length = row_input.shape[0]
    head_dim = D // HEADS
    normed_attn = low(rms_scale(row_input, gain_attn))
    query_pre = low_back(jnp.dot(normed_attn, full_query, precision=EXACT_PRECISION))
    key_pre = low_back(jnp.dot(normed_attn, full_key, precision=EXACT_PRECISION))
    value_pre = low_back(jnp.dot(normed_attn, full_value, precision=EXACT_PRECISION))
    z_pre = low_back(jnp.dot(normed_attn, full_forget, precision=EXACT_PRECISION))
    query_rows = low(jax.nn.silu(query_pre)).reshape(length, HEADS, head_dim)
    key_matrix = low(jax.nn.silu(key_pre)).reshape(length, HEADS, head_dim)
    value_matrix = low(value_pre).reshape(length, HEADS, head_dim)
    log_forget = (jax.nn.log_sigmoid(z_pre + full_bias) / 8.0).reshape(length, HEADS, SLOTS)
    zero_state = jnp.zeros((HEADS, SLOTS, head_dim), jnp.float32)
    ignored, mixed_rows = run_blocks((zero_state, zero_state), query_rows, key_matrix, value_matrix, log_forget, row_starts)
    mixed = low(mixed_rows.reshape(length, D))
    attended = row_input + low_back(jnp.dot(mixed, full_out, precision=EXACT_PRECISION))
    normed_ffn = low(rms_scale(attended, gain_ffn))
    gate_pre = low_back(jnp.dot(normed_ffn, full_gate, precision=EXACT_PRECISION))
    up_pre = low_back(jnp.dot(normed_ffn, full_up, precision=EXACT_PRECISION))
    hidden = low(jax.nn.silu(gate_pre) * up_pre)
    return attended + low_back(jnp.dot(hidden, full_down, precision=EXACT_PRECISION))

def reference(inputs, starts, norm_attn, w_query, w_key, w_value, w_forget, gate_bias, w_out, norm_ffn, w_gate, w_up, w_down, cotangent):
    params = tuple((member.astype(jnp.float32) for member in (norm_attn, w_query, w_key, w_value, w_forget, gate_bias, w_out, norm_ffn, w_gate, w_up, w_down)))

    def one_row(totals, row_data):
        row_input, row_starts, row_grad = row_data

        def forward(features, weights_all):
            return layer(features, row_starts, weights_all)
        row_out, pull_back = jax.vjp(forward, row_input.astype(jnp.float32), params)
        grad_row, grad_params = pull_back(row_grad.astype(jnp.float32))
        totals = tuple((accum + extra for accum, extra in zip(totals, grad_params)))
        return (totals, (row_out.astype(jnp.bfloat16), grad_row))
    zeros_all = tuple((jnp.zeros_like(member) for member in params))
    totals, outs_rows = lax.scan(one_row, zeros_all, (inputs, starts, cotangent))
    output, grad_input = outs_rows
    return (output, grad_input, totals[0], totals[1], totals[2], totals[3], totals[4], totals[5], totals[6], totals[7], totals[8], totals[9], totals[10])
```

```python
import functools

import jax
import jax.numpy as jnp
from jax import lax
from jax.sharding import Mesh
from jax.sharding import PartitionSpec as P
from jax.experimental import pallas as pl
from jax.experimental.pallas import tpu as pltpu

SLOTS = 64
TILE = 128
F32, BF16 = jnp.float32, jnp.bfloat16
NN = (((1,), (0,)), ((), ()))
NT = (((1,), (1,)), ((), ()))
TN = (((0,), (0,)), ((), ()))
HALVES = (64, 32, 16, 8, 4, 2, 1)


def dot(a, b, dims):
    return lax.dot_general(a, b, dims, preferred_element_type=F32)


def parts_of(a):
    high = a.astype(BF16)
    return high, (a - high.astype(F32)).astype(BF16)


def dot_parts(a, b, dims):
    return dot(a[0], b[0], dims) + (dot(a[1], b[0], dims) + dot(a[0], b[1], dims))


def dot_ones(ones, a):
    high = a.astype(BF16)
    rest = a - high.astype(F32)
    middle = rest.astype(BF16)
    low = (rest - middle.astype(F32)).astype(BF16)
    return dot(ones, high, NN) + (dot(ones, middle, NN) + dot(ones, low, NN))


def places():
    shape = (TILE, TILE)
    return lax.broadcasted_iota(jnp.int32, shape, 0), lax.broadcasted_iota(jnp.int32, shape, 1)


def ones_where(mask):
    return jnp.where(mask, 1.0, 0.0).astype(BF16)


def steps_to_middle(half):
    t, s = places()
    block = 2 * half
    same = (t // block) == (s // block)
    t_right, s_right = (t % block) >= half, (s % block) >= half
    right = t_right & s_right & (s <= t)
    left = jnp.logical_not(t_right | s_right) & (s > t)
    return ones_where(same & (right | left))


def pair_mask(half, turned=False):
    t, s = places()
    if turned:
        t, s = s, t
    block = 2 * half
    return ((t // block) == (s // block)) & ((t % block) >= half) & ((s % block) < half)


def first_row(rows):
    return lax.broadcasted_iota(jnp.int32, (rows, 2 * SLOTS), 1) < SLOTS


def row_sums(a, first):
    return (
        jnp.sum(jnp.where(first, a, 0.0), axis=1, keepdims=True),
        jnp.sum(jnp.where(first, 0.0, a), axis=1, keepdims=True),
    )


def tile_rows(j):
    return pl.ds(pl.multiple_of(j * TILE, TILE), TILE)


def prepare(lf_ref, decay_ref, reach_ref, e_ref, tiles):
    t, s = places()

    @pl.loop(0, tiles)
    def _(j):
        rows = tile_rows(j)
        lf = lf_ref[rows, :]
        decay_ref[rows, :] = dot_ones(ones_where(s <= t), lf)
        reach_ref[rows, :] = dot_ones(ones_where(s > t), lf)
        for level, half in enumerate(HALVES):
            e_ref[level, rows, :] = jnp.exp(dot_ones(steps_to_middle(half), lf))


def far_pairs(tiles):
    out, half = [], tiles // 2
    while half >= 1:
        for start in range(0, tiles, 2 * half):
            out.append((start + half, start, half))
        half //= 2
    return out


def far_decays(right, left, half, decay_ref, reach_ref):
    after, total = [], None
    for j in range(right, right + half):
        part = decay_ref[j * TILE:(j + 1) * TILE, :]
        after.append(jnp.exp(part if total is None else part + total))
        last = part[TILE - 1:TILE, :]
        total = last if total is None else total + last
    before, total = [], None
    for j in range(left + half - 1, left - 1, -1):
        part = reach_ref[j * TILE:(j + 1) * TILE, :]
        before.append(jnp.exp(part if total is None else part + total))
        whole = decay_ref[(j + 1) * TILE - 1:(j + 1) * TILE, :]
        total = whole if total is None else total + whole
    if half == 1:
        return after[0], before[0]
    return jnp.concatenate(after, axis=0), jnp.concatenate(before[::-1], axis=0)


def diagonal_of(block):
    t, s = places()
    return jnp.sum(jnp.where(t == s, block, 0.0), axis=1, keepdims=True)


def weighted_sums(a_ref, out_ref, gain_ref, decay_ref, reach_ref, e_ref, tiles):
    first = first_row(TILE)

    @pl.loop(0, tiles)
    def _(j):
        rows = tile_rows(j)
        gain = gain_ref[rows, :]
        blocks = [a_ref[r, rows, rows] for r in range(2)]
        total = jnp.where(first, diagonal_of(blocks[0]), diagonal_of(blocks[1])) * gain
        for level, half in enumerate(HALVES):
            e = e_ref[level, rows, :]
            x = parts_of(e * gain)
            pairs = pair_mask(half)
            y = [dot_parts(parts_of(jnp.where(pairs, a, 0.0)), x, NN) for a in blocks]
            total = total + e * jnp.where(first, y[0], y[1])
        out_ref[rows, :] = total

    for right, left, half in far_pairs(tiles):
        after, before = far_decays(right, left, half, decay_ref, reach_ref)
        here = slice(right * TILE, (right + half) * TILE)
        there = slice(left * TILE, (left + half) * TILE)
        x = parts_of(before * gain_ref[there, :])
        y = [dot_parts(parts_of(a_ref[r, here, there]), x, NN) for r in range(2)]
        out_ref[here, :] += after * jnp.where(first_row(half * TILE), y[0], y[1])


def split_rows(a, first):
    return parts_of(jnp.where(first, a, 0.0)), parts_of(jnp.where(first, 0.0, a))


def paired_weights(p_ref, out_ref, gain_ref, decay_ref, reach_ref, e_ref, tiles):
    first = first_row(TILE)
    t, s = places()

    @pl.loop(0, tiles)
    def _(j):
        rows = tile_rows(j)
        gain, p = gain_ref[rows, :], p_ref[rows, :]
        sums = row_sums(p * gain, first)
        total = [jnp.where(t == s, sums[r], 0.0) for r in range(2)]
        for level, half in enumerate(HALVES):
            e = e_ref[level, rows, :]
            x = parts_of(e * gain)
            pairs = pair_mask(half)
            pe = split_rows(p * e, first)
            total = [total[r] + jnp.where(pairs, dot_parts(pe[r], x, NT), 0.0) for r in range(2)]
        for r in range(2):
            out_ref[r, rows, rows] = total[r]

    for right, left, half in far_pairs(tiles):
        after, before = far_decays(right, left, half, decay_ref, reach_ref)
        here = slice(right * TILE, (right + half) * TILE)
        there = slice(left * TILE, (left + half) * TILE)
        x = parts_of(before * gain_ref[there, :])
        pe = split_rows(p_ref[here, :] * after, first_row(half * TILE))
        for r in range(2):
            out_ref[r, here, there] = dot_parts(pe[r], x, NT)
            out_ref[r, there, here] = jnp.zeros((half * TILE, half * TILE), F32)


def inner(a_ref, b_ref, r):
    return dot(a_ref[0, r], b_ref[0, r], NT) + dot(a_ref[1, r], b_ref[1, r], NT)


def forward_kernel(q_ref, k_ref, v_ref, lf_ref, gain_ref, dcol_ref, drow_ref,
                   mixed_ref, s_ref, p_ref, b_ref, a_ref, decay_ref, reach_ref, e_ref):
    length, depth = q_ref.shape[2:]
    tiles = length // TILE
    scale = (2 * depth) ** -0.5
    for r in range(2):
        same = dcol_ref[r] == drow_ref[r]
        a_ref[r] = jnp.where(same, inner(q_ref, k_ref, r), 0.0)
    prepare(lf_ref, decay_ref, reach_ref, e_ref, tiles)
    weighted_sums(a_ref, s_ref, gain_ref, decay_ref, reach_ref, e_ref, tiles)
    first = first_row(length)
    logits = s_ref[...] * scale
    low = -jnp.inf
    top = jnp.where(
        first,
        jnp.max(jnp.where(first, logits, low), axis=1, keepdims=True),
        jnp.max(jnp.where(first, low, logits), axis=1, keepdims=True),
    )
    grown = jnp.exp(logits - top)
    sums = row_sums(grown, first)
    p_ref[...] = grown / jnp.where(first, sums[0], sums[1])
    paired_weights(p_ref, b_ref, gain_ref, decay_ref, reach_ref, e_ref, tiles)
    for r in range(2):
        b = jnp.where(dcol_ref[r] == drow_ref[r], b_ref[r], 0.0)
        b_ref[r] = b
        high, rest = parts_of(b)
        for f in range(2):
            mixed = (dot(high, v_ref[f, r], NN) + dot(rest, v_ref[f, r], NN)).astype(BF16)
            for place in range(2):
                mixed_ref[r, place, f] = mixed[place * length // 2:(place + 1) * length // 2]


def backward_kernel(q_ref, k_ref, v_ref, g_ref, lf_ref, gain_ref, dcol_ref, drow_ref, s_ref, p_ref, b_ref,
                    gq_ref, gk_ref, gv_ref, gl_ref,
                    a_ref, at_ref, dot_ref, h_ref, back_ref, decay_ref, reach_ref, e_ref):
    length, depth = q_ref.shape[2:]
    tiles = length // TILE
    scale = (2 * depth) ** -0.5
    first_all, first = first_row(length), first_row(TILE)
    t, s = places()
    grads = [[g_ref[r, :, f].reshape(length, depth) for r in range(2)] for f in range(2)]
    for r in range(2):
        same = dcol_ref[r] == drow_ref[r]
        by_t = dot(grads[0][r], v_ref[0, r], NT) + dot(grads[1][r], v_ref[1, r], NT)
        by_s = dot(v_ref[0, r], grads[0][r], NT) + dot(v_ref[1, r], grads[1][r], NT)
        a_ref[r] = jnp.where(same, by_t, 0.0)
        at_ref[0, r] = jnp.where(same, inner(k_ref, q_ref, r), 0.0)
        at_ref[1, r] = jnp.where(same, by_s, 0.0)
    prepare(lf_ref, decay_ref, reach_ref, e_ref, tiles)
    weighted_sums(a_ref, dot_ref, gain_ref, decay_ref, reach_ref, e_ref, tiles)
    p, dots = p_ref[...], dot_ref[...]
    sums = row_sums(p * dots, first_all)
    h = scale * (p * (dots - jnp.where(first_all, sums[0], sums[1])))
    h_ref[...] = h
    dot_ref[...] = h * s_ref[...] + p * dots
    paired_weights(h_ref, a_ref, gain_ref, decay_ref, reach_ref, e_ref, tiles)
    @pl.loop(0, tiles)
    def _(j):
        rows = tile_rows(j)
        h, p = h_ref[rows, :], p_ref[rows, :]
        keys = [at_ref[0, r, rows, rows] for r in range(2)]
        values = [at_ref[1, r, rows, rows] for r in range(2)]
        total = (
            jnp.where(first, diagonal_of(keys[0]), diagonal_of(keys[1])) * h
            + jnp.where(first, diagonal_of(values[0]), diagonal_of(values[1])) * p
        )
        for level, half in enumerate(HALVES):
            e = e_ref[level, rows, :]
            he, pe = parts_of(h * e), parts_of(p * e)
            pairs = pair_mask(half, turned=True)
            y = [
                dot_parts(parts_of(jnp.where(pairs, keys[r], 0.0)), he, NN)
                + dot_parts(parts_of(jnp.where(pairs, values[r], 0.0)), pe, NN)
                for r in range(2)
            ]
            total = total + e * jnp.where(first, y[0], y[1])
        back_ref[rows, :] = total

    for right, left, half in far_pairs(tiles):
        after, before = far_decays(right, left, half, decay_ref, reach_ref)
        here = slice(right * TILE, (right + half) * TILE)
        there = slice(left * TILE, (left + half) * TILE)
        he, pe = parts_of(h_ref[here, :] * after), parts_of(p_ref[here, :] * after)
        y = [
            dot_parts(parts_of(at_ref[0, r, there, here]), he, NN)
            + dot_parts(parts_of(at_ref[1, r, there, here]), pe, NN)
            for r in range(2)
        ]
        back_ref[there, :] += before * jnp.where(first_row(half * TILE), y[0], y[1])

    for r in range(2):
        c = jnp.where(dcol_ref[r] == drow_ref[r], a_ref[r], 0.0)
        high, rest = parts_of(c)
        for f in range(2):
            gq_ref[f, r] = dot(high, k_ref[f, r], NN) + dot(rest, k_ref[f, r], NN)
            gk_ref[f, r] = dot(high, q_ref[f, r], TN) + dot(rest, q_ref[f, r], TN)
        high, rest = parts_of(b_ref[r])
        for f in range(2):
            gv_ref[f, r] = dot(high, grads[f][r], TN) + dot(rest, grads[f][r], TN)
    carried = jnp.zeros((1, 2 * SLOTS), F32)
    for j in range(tiles - 1, -1, -1):
        rows = slice(j * TILE, (j + 1) * TILE)
        back = back_ref[rows, :]
        change = dot_ref[rows, :] - gain_ref[rows, :] * back
        upward = dot_ones(ones_where(s >= t), change) + carried
        gl_ref[rows, :] = upward - jnp.exp(lf_ref[rows, :]) * back
        carried = upward[0:1, :]


def mix_forward(q, k, v, lf, gain, doc):
    rows, length, depth = q.shape[1:]
    lanes = (length, 2 * SLOTS)
    whole = jax.ShapeDtypeStruct((rows, length, length), F32)
    return pl.pallas_call(
        forward_kernel,
        name="mix_forward",
        out_shape=(
            jax.ShapeDtypeStruct((rows, 2, 2, length // 2, depth), BF16), jax.ShapeDtypeStruct(lanes, F32),
            jax.ShapeDtypeStruct(lanes, F32), whole,
        ),
        scratch_shapes=[
            pltpu.VMEM((2, length, length), F32), pltpu.VMEM(lanes, F32), pltpu.VMEM(lanes, F32),
            pltpu.VMEM((len(HALVES),) + lanes, F32),
        ],
        compiler_params=pltpu.CompilerParams(vmem_limit_bytes=40 << 20),
    )(q, k, v, lf, gain, doc[:, :, None], doc[:, None, :])


def mix_backward(q, k, v, g, lf, gain, doc, s, p, b):
    length = q.shape[2]
    lanes = (length, 2 * SLOTS)
    square = (2, length, length)
    return pl.pallas_call(
        backward_kernel,
        name="mix_backward",
        out_shape=(jax.ShapeDtypeStruct(q.shape, F32),) * 3 + (jax.ShapeDtypeStruct(lanes, F32),),
        scratch_shapes=[
            pltpu.VMEM(square, F32), pltpu.VMEM((2,) + square, F32),
            pltpu.VMEM(lanes, F32), pltpu.VMEM(lanes, F32), pltpu.VMEM(lanes, F32),
            pltpu.VMEM(lanes, F32), pltpu.VMEM(lanes, F32), pltpu.VMEM((len(HALVES),) + lanes, F32),
        ],
        compiler_params=pltpu.CompilerParams(vmem_limit_bytes=48 << 20),
    )(q, k, v, g, lf, gain, doc[:, :, None], doc[:, None, :], s, p, b)


HEADS = 4
EPSILON = 1e-06
PLANE = ("y", "x")
MESH = pl.DeviceIdType.MESH


def exchange_kernel(to_homes, same, a_ref, out_ref, send, recv, local):
    y, x, c = (lax.axis_index(name) for name in ("y", "x", "c"))
    barrier = pltpu.get_barrier_semaphore()
    for flip in range(1, 8):
        peer = {
            "y": lax.rem(y + flip // 4, 2), "x": lax.rem(x + (flip // 2) % 2, 2), "c": lax.rem(c + flip % 2, 2)
        }
        pl.semaphore_signal(barrier, inc=1, device_id=peer, device_id_type=MESH)
    pl.semaphore_wait(barrier, 7)
    slot = y * 2 + x if to_homes else x * 2 + c
    for i in range(4):
        if to_homes:
            peer = {"y": c, "x": i // 2, "c": i % 2}
        else:
            peer = {"y": i // 2, "x": i % 2, "c": y}
        mine = (peer["y"] == y) & (peer["x"] == x) & (peer["c"] == c)
        source = a_ref if same else a_ref.at[i]

        @pl.when(mine)
        def _():
            pltpu.make_async_copy(source, out_ref.at[slot], local).start()

        @pl.when(jnp.logical_not(mine))
        def _():
            pltpu.make_async_remote_copy(
                src_ref=source, dst_ref=out_ref.at[slot], send_sem=send.at[i], recv_sem=recv.at[slot],
                device_id=peer, device_id_type=MESH,
            ).start()

    for i in range(4):
        if to_homes:
            peer = {"y": c, "x": i // 2, "c": i % 2}
            giver = {"y": i // 2, "x": i % 2, "c": y}
        else:
            peer = {"y": i // 2, "x": i % 2, "c": y}
            giver = {"y": c, "x": i // 2, "c": i % 2}
        source = a_ref if same else a_ref.at[i]
        sent_here = (peer["y"] == y) & (peer["x"] == x) & (peer["c"] == c)
        from_here = (giver["y"] == y) & (giver["x"] == x) & (giver["c"] == c)

        def whole(device):
            return pltpu.make_async_remote_copy(
                src_ref=source, dst_ref=out_ref.at[i], send_sem=send.at[i], recv_sem=recv.at[i],
                device_id=device, device_id_type=MESH,
            )

        @pl.when(jnp.logical_not(sent_here))
        def _():
            whole(peer).wait_send()

        @pl.when(jnp.logical_not(from_here))
        def _():
            whole(peer).wait_recv()

        @pl.when(from_here)
        def _():
            pltpu.make_async_copy(source, out_ref.at[i], local).wait()


def exchange(a, collective, to_homes, same=False):
    block = a.shape if same else a.shape[1:]
    return pl.pallas_call(
        functools.partial(exchange_kernel, to_homes, same),
        name="to_homes" if to_homes else "from_homes",
        out_shape=jax.ShapeDtypeStruct((4,) + block, a.dtype),
        in_specs=[pl.BlockSpec(memory_space=pl.ANY)],
        out_specs=pl.BlockSpec(memory_space=pl.ANY),
        scratch_shapes=[pltpu.SemaphoreType.DMA((4,)), pltpu.SemaphoreType.DMA((4,)), pltpu.SemaphoreType.DMA],
        compiler_params=pltpu.CompilerParams(collective_id=collective, has_side_effects=True),
    )(a)


def share(a):
    mine = lax.all_to_all(a, PLANE, split_axis=0, concat_axis=0, tiled=True)
    mine = mine.reshape((-1,) + a.shape[2:])
    return lax.all_gather(mine, ("c", "z"), axis=0, tiled=True).reshape((2, -1) + a.shape[2:])


def sum_over(a, axes):
    return lax.psum_scatter(a.astype(BF16), axes, scatter_dimension=0, tiled=True)


def slope(v):
    s = jax.nn.sigmoid(v)
    return s * (1.0 + v * (1.0 - s))


def scaled(features):
    return lax.rsqrt(jnp.mean(features * features, axis=-1, keepdims=True) + EPSILON)


def norm_back(grad, gain, features, ratio):
    u, xh = grad * gain, features * ratio
    return ratio * (u - xh * jnp.mean(u * xh, axis=-1, keepdims=True))


def body(inputs, starts, norm_attn, w_query, w_key, w_value, w_forget, gate_bias, w_out, norm_ffn, w_gate, w_up,
         w_down, cotangent):
    positions, features = inputs.shape[1:]
    depth = features // HEADS
    y, x, c, z = (lax.axis_index(name) for name in ("y", "x", "c", "z"))
    planes = lax.axis_size("z")
    head = y * 2 + x
    rows_here = w_query.shape[0]
    hidden_here = w_down.shape[0]

    def own_half(a, axis):
        return lax.dynamic_index_in_dim(a, c, axis, keepdims=False)

    bias_here = gate_bias.shape[0]
    small = jnp.concatenate([norm_attn, norm_ffn, gate_bias, starts[0].astype(BF16)])
    small = lax.all_gather(small, ("z", "y", "x", "c"), axis=0)
    small = small.reshape((planes, 2, 2, 2, small.shape[-1]))
    cuts = [rows_here, 2 * rows_here, 2 * rows_here + bias_here]
    gain_attn, gain_ffn, bias = (
        part[:, :, :, 0].reshape(-1).astype(F32) for part in jnp.split(small[..., :cuts[2]], cuts[:2], axis=-1)
    )
    begins = lax.dynamic_index_in_dim(small[..., cuts[2]:], z, 0, keepdims=False)
    begins = lax.dynamic_index_in_dim(begins, c, 0, keepdims=False).reshape(2, 2 * positions).astype(F32)
    doc = jnp.cumsum(begins, axis=1)
    bias = lax.dynamic_slice_in_dim(bias, head * SLOTS, SLOTS)

    def columns(w):
        w = w.reshape(rows_here, HEADS, 2, -1)
        return own_half(w, 2).transpose(1, 0, 2)

    mixer_w = share(jnp.concatenate([columns(w) for w in (w_query, w_key, w_value, w_forget)], axis=-1))

    def hidden_columns(w):
        w = own_half(w.reshape(rows_here, planes, 4, 2, hidden_here // 2), 3)
        return w.transpose(2, 0, 1, 3).reshape(4, rows_here, -1)

    full_gate, full_up = share(hidden_columns(w_gate)), share(hidden_columns(w_up))
    down_half = own_half(w_down.reshape(2, hidden_here // 2, features), 0)
    full_down = lax.all_gather(down_half, ("c", "z"), axis=0, tiled=True).reshape(2, -1, features)
    out_half = own_half(w_out.reshape(2, rows_here // 2, features), 0)
    full_out = lax.all_gather(out_half, ("z", "y", "x", "c"), axis=0, tiled=True)

    x_here = inputs.reshape(positions, features)
    cot_here = cotangent.reshape(positions, features)
    x_rows = exchange(x_here, 1, False, same=True).reshape(4 * positions, features).astype(F32)
    cot = exchange(cot_here, 2, False, same=True).reshape(4 * positions, features)
    normed = (x_rows * scaled(x_rows) * gain_attn).astype(BF16)
    pre = jnp.einsum("td,cdf->ctf", normed, mixer_w, preferred_element_type=F32)
    by_row = (2, 2, 2 * positions, depth // 2)
    query_pre, key_pre, value_pre = (
        pre[:, :, i * depth // 2:(i + 1) * depth // 2].reshape(by_row) for i in range(3)
    )
    z_total = pre[:, :, 3 * depth // 2:].reshape(2, 2, 2 * positions, SLOTS // 2)
    z_total = z_total.transpose(2, 1, 0, 3).reshape(2 * positions, 2 * SLOTS) + jnp.tile(bias, 2)
    log_forget = jax.nn.log_sigmoid(z_total) / 8.0
    gain = -jnp.expm1(log_forget)
    queries, keys, values = jax.nn.silu(query_pre).astype(BF16), jax.nn.silu(key_pre).astype(BF16), value_pre.astype(BF16)
    mixed, scores, probs, paired = mix_forward(queries, keys, values, log_forget, gain, doc)
    mixed = exchange(mixed.reshape(4, 2 * positions, depth // 2), 3, True)
    mixed = mixed.reshape(2 * HEADS, positions, depth // 2).transpose(1, 0, 2).reshape(positions, features)
    attended = x_here.astype(F32) + jnp.dot(mixed, full_out, preferred_element_type=F32)

    ratio_f = scaled(attended)
    normed_ffn = exchange((attended * ratio_f * gain_ffn).astype(BF16), 4, False, same=True)
    normed_ffn = normed_ffn.reshape(4 * positions, features)
    gate_pre = jnp.einsum("td,cdf->ctf", normed_ffn, full_gate, preferred_element_type=F32)
    up_pre = jnp.einsum("td,cdf->ctf", normed_ffn, full_up, preferred_element_type=F32)
    silu_gate = jax.nn.silu(gate_pre)
    hidden = (silu_gate * up_pre).astype(BF16)
    grad_hidden = jnp.einsum("td,cfd->ctf", cot, full_down, preferred_element_type=F32)
    grad_gate = (grad_hidden * up_pre * slope(gate_pre)).astype(BF16)
    grad_up = (grad_hidden * silu_gate).astype(BF16)
    grad_down_w = jnp.einsum("ctf,td->cfd", hidden, cot, preferred_element_type=F32)
    grad_down_w = sum_over(grad_down_w.reshape(-1, features), ("c", "z"))
    grad_normed_ffn = (
        jnp.einsum("ctf,cdf->td", grad_gate, full_gate, preferred_element_type=F32)
        + jnp.einsum("ctf,cdf->td", grad_up, full_up, preferred_element_type=F32)
    ).astype(BF16)
    grad_normed_ffn = exchange(grad_normed_ffn.reshape(4, positions, features), 5, True)
    grad_normed_ffn = jnp.sum(grad_normed_ffn.astype(F32), axis=0)
    grad_gate_w = jnp.einsum("td,ctf->cdf", normed_ffn, grad_gate, preferred_element_type=F32)
    grad_gate_w = sum_over(grad_gate_w.reshape(2 * features, -1), ("c", "z"))
    grad_up_w = jnp.einsum("td,ctf->cdf", normed_ffn, grad_up, preferred_element_type=F32)
    grad_up_w = sum_over(grad_up_w.reshape(2 * features, -1), ("c", "z"))
    block_out = jnp.einsum("ctf,cfd->td", hidden, full_down, preferred_element_type=F32).astype(BF16)
    block_out = exchange(block_out.reshape(4, positions, features), 6, True)
    output = (attended + jnp.sum(block_out.astype(F32), axis=0)).astype(BF16)
    grad_gain_ffn = jnp.sum(grad_normed_ffn * attended * ratio_f, axis=0)
    grad_attended = cot_here.astype(F32) + norm_back(grad_normed_ffn, gain_ffn, attended, ratio_f)

    grad_branch = grad_attended.astype(BF16)
    grad_out_w = jnp.einsum("td,te->de", mixed, grad_branch, preferred_element_type=F32)
    grad_out_w = sum_over(grad_out_w, ("z", "y", "x", "c"))
    grad_mixed = jnp.einsum("te,de->td", grad_branch, full_out, preferred_element_type=F32).astype(BF16)
    grad_mixed = grad_mixed.reshape(positions, HEADS, 2, depth // 2).transpose(1, 2, 0, 3)
    grad_mixed = exchange(grad_mixed.reshape(4, 2 * positions, depth // 2), 7, False)
    grad_mixed = grad_mixed.reshape(2, 2, 2, positions, depth // 2)
    grad_queries, grad_keys, grad_values, grad_log = mix_backward(
        queries, keys, values, grad_mixed, log_forget, gain, doc, scores, probs, paired
    )
    grad_z = grad_log * jax.nn.sigmoid(-z_total) / 8.0
    grad_bias = jnp.sum(jnp.sum(grad_z, axis=0).reshape(2, SLOTS), axis=0)
    grad_z = grad_z.reshape(2 * positions, 2, 2, SLOTS // 2).transpose(2, 1, 0, 3)
    tokens = (2, 4 * positions, -1)
    grad_pre = jnp.concatenate([
        (grad_queries * slope(query_pre)).astype(BF16).reshape(tokens),
        (grad_keys * slope(key_pre)).astype(BF16).reshape(tokens),
        grad_values.astype(BF16).reshape(tokens),
        grad_z.astype(BF16).reshape(tokens),
    ], axis=-1)
    grad_mixer_w = jnp.einsum("td,ctf->cdf", normed, grad_pre, preferred_element_type=F32)
    grad_mixer_w = sum_over(grad_mixer_w.reshape(2 * features, -1), ("c", "z"))
    grad_normed = jnp.einsum("ctf,cdf->td", grad_pre, mixer_w, preferred_element_type=F32).astype(BF16)
    grad_normed = exchange(grad_normed.reshape(4, positions, features), 8, True)
    grad_normed = jnp.sum(grad_normed.astype(F32), axis=0)
    x_here = x_here.astype(F32)
    ratio_a = scaled(x_here)
    grad_gain_attn = jnp.sum(grad_normed * x_here * ratio_a, axis=0)
    grad_input = grad_attended + norm_back(grad_normed, gain_attn, x_here, ratio_a)

    bias_all = lax.dynamic_update_slice_in_dim(jnp.zeros((HEADS * SLOTS,), F32), grad_bias, head * SLOTS, 0)
    small = lax.psum(jnp.concatenate([grad_gain_attn, grad_gain_ffn, bias_all]), ("z", "y", "x", "c"))
    block = z * 4 + head
    grad_gain_attn = lax.dynamic_slice_in_dim(small, block * rows_here, rows_here)
    grad_gain_ffn = lax.dynamic_slice_in_dim(small, features + block * rows_here, rows_here)
    grad_bias = lax.dynamic_slice_in_dim(small, 2 * features + block * bias_here, bias_here)

    def to_rows(a):
        a = lax.all_to_all(a.reshape(4, rows_here, -1), PLANE, split_axis=0, concat_axis=0, tiled=True)
        return lax.all_gather(a, "c", axis=0)

    grad_mixer_w = to_rows(grad_mixer_w).transpose(2, 1, 0, 3)
    grad_w = [
        grad_mixer_w[..., i * depth // 2:(i + 1) * depth // 2].reshape(rows_here, features).astype(F32) for i in range(3)
    ]
    grad_forget_w = grad_mixer_w[..., 3 * depth // 2:].reshape(rows_here, HEADS * SLOTS).astype(F32)

    def from_hidden(a):
        a = to_rows(a).reshape(2, 4, rows_here, planes, hidden_here // 2)
        return a.transpose(2, 3, 1, 0, 4).reshape(rows_here, -1).astype(F32)

    def both_halves(a):
        return lax.all_gather(a, "c", axis=0, tiled=True).astype(F32)

    return (
        output.reshape(inputs.shape), grad_input.reshape(inputs.shape), grad_gain_attn, grad_w[0], grad_w[1], grad_w[2],
        grad_forget_w, grad_bias, both_halves(grad_out_w), grad_gain_ffn, from_hidden(grad_gate_w),
        from_hidden(grad_up_w), both_halves(grad_down_w),
    )


def solution(mesh):
    planes = mesh.shape["dp"] // 4
    fine = Mesh(mesh.devices.reshape(planes, 2, 2, 2), ("z", "y", "x", "c"))
    dp = ("z", "y", "x")
    tokens, vector, matrix = P(dp, "c", None), P(dp), P(dp, None)
    in_specs = (
        tokens, P(dp, "c"), vector, matrix, matrix, matrix, matrix, vector, matrix, vector, matrix, matrix, matrix, tokens
    )
    out_specs = (
        tokens, tokens, vector, matrix, matrix, matrix, matrix, vector, matrix, vector, matrix, matrix, matrix
    )
    return jax.shard_map(body, mesh=fine, in_specs=in_specs, out_specs=out_specs, check_vma=False)
```

```python
import functools

import jax
import jax.numpy as jnp
from jax import lax
from jax.sharding import Mesh
from jax.sharding import PartitionSpec as P
from jax.experimental import pallas as pl
from jax.experimental.pallas import tpu as pltpu

HEADS = 4
SLOTS = 64
DEPTH = 512
TILE = 128
EPSILON = 1e-06
F32, BF16 = jnp.float32, jnp.bfloat16
NN = (((1,), (0,)), ((), ()))
NT = (((1,), (1,)), ((), ()))
TN = (((0,), (0,)), ((), ()))
HALVES = (64, 32, 16, 8, 4, 2, 1)


def dot(a, b, dims):
    return lax.dot_general(a, b, dims, preferred_element_type=F32)


def parts_of(a):
    high = a.astype(BF16)
    return high, (a - high.astype(F32)).astype(BF16)


def dot_parts(a, b, dims):
    return dot(a[0], b[0], dims) + (dot(a[1], b[0], dims) + dot(a[0], b[1], dims))


def dot_ones(ones, a):
    high = a.astype(BF16)
    rest = a - high.astype(F32)
    middle = rest.astype(BF16)
    low = (rest - middle.astype(F32)).astype(BF16)
    return dot(ones, high, NN) + (dot(ones, middle, NN) + dot(ones, low, NN))


def places():
    shape = (TILE, TILE)
    return lax.broadcasted_iota(jnp.int32, shape, 0), lax.broadcasted_iota(jnp.int32, shape, 1)


def ones_where(mask):
    return jnp.where(mask, 1.0, 0.0).astype(BF16)


def steps_to_middle(half):
    t, s = places()
    block = 2 * half
    same = (t // block) == (s // block)
    t_right, s_right = (t % block) >= half, (s % block) >= half
    right = t_right & s_right & (s <= t)
    left = jnp.logical_not(t_right | s_right) & (s > t)
    return ones_where(same & (right | left))


def pair_mask(half, turned=False):
    t, s = places()
    if turned:
        t, s = s, t
    block = 2 * half
    return ((t // block) == (s // block)) & ((t % block) >= half) & ((s % block) < half)


def first_row(rows):
    return lax.broadcasted_iota(jnp.int32, (rows, 2 * SLOTS), 1) < SLOTS


def row_sums(a, first):
    return (
        jnp.sum(jnp.where(first, a, 0.0), axis=1, keepdims=True),
        jnp.sum(jnp.where(first, 0.0, a), axis=1, keepdims=True),
    )


def tile_rows(j):
    return pl.ds(pl.multiple_of(j * TILE, TILE), TILE)


def prepare(lf_ref, decay_ref, reach_ref, e_ref, tiles):
    t, s = places()

    @pl.loop(0, tiles)
    def _(j):
        rows = tile_rows(j)
        lf = lf_ref[rows, :]
        decay_ref[rows, :] = dot_ones(ones_where(s <= t), lf)
        reach_ref[rows, :] = dot_ones(ones_where(s > t), lf)
        for level, half in enumerate(HALVES):
            e_ref[level, rows, :] = jnp.exp(dot_ones(steps_to_middle(half), lf))


def far_pairs(tiles):
    out, half = [], tiles // 2
    while half >= 1:
        for start in range(0, tiles, 2 * half):
            out.append((start + half, start, half))
        half //= 2
    return out


def far_decays(right, left, half, decay_ref, reach_ref):
    after, total = [], None
    for j in range(right, right + half):
        part = decay_ref[j * TILE:(j + 1) * TILE, :]
        after.append(jnp.exp(part if total is None else part + total))
        last = part[TILE - 1:TILE, :]
        total = last if total is None else total + last
    before, total = [], None
    for j in range(left + half - 1, left - 1, -1):
        part = reach_ref[j * TILE:(j + 1) * TILE, :]
        before.append(jnp.exp(part if total is None else part + total))
        whole = decay_ref[(j + 1) * TILE - 1:(j + 1) * TILE, :]
        total = whole if total is None else total + whole
    if half == 1:
        return after[0], before[0]
    return jnp.concatenate(after, axis=0), jnp.concatenate(before[::-1], axis=0)


def diagonal_of(block):
    t, s = places()
    return jnp.sum(jnp.where(t == s, block, 0.0), axis=1, keepdims=True)


def weighted_sums(a_ref, out_ref, gain_ref, decay_ref, reach_ref, e_ref, tiles):
    first = first_row(TILE)

    @pl.loop(0, tiles)
    def _(j):
        rows = tile_rows(j)
        gain = gain_ref[rows, :]
        blocks = [a_ref[r, rows, rows] for r in range(2)]
        total = jnp.where(first, diagonal_of(blocks[0]), diagonal_of(blocks[1])) * gain
        for level, half in enumerate(HALVES):
            e = e_ref[level, rows, :]
            x = parts_of(e * gain)
            pairs = pair_mask(half)
            y = [dot_parts(parts_of(jnp.where(pairs, a, 0.0)), x, NN) for a in blocks]
            total = total + e * jnp.where(first, y[0], y[1])
        out_ref[rows, :] = total

    for right, left, half in far_pairs(tiles):
        after, before = far_decays(right, left, half, decay_ref, reach_ref)
        here = slice(right * TILE, (right + half) * TILE)
        there = slice(left * TILE, (left + half) * TILE)
        x = parts_of(before * gain_ref[there, :])
        y = [dot_parts(parts_of(a_ref[r, here, there]), x, NN) for r in range(2)]
        out_ref[here, :] += after * jnp.where(first_row(half * TILE), y[0], y[1])


def split_rows(a, first):
    return parts_of(jnp.where(first, a, 0.0)), parts_of(jnp.where(first, 0.0, a))


def paired_weights(p_ref, out_ref, gain_ref, decay_ref, reach_ref, e_ref, tiles):
    first = first_row(TILE)
    t, s = places()

    @pl.loop(0, tiles)
    def _(j):
        rows = tile_rows(j)
        gain, p = gain_ref[rows, :], p_ref[rows, :]
        sums = row_sums(p * gain, first)
        total = [jnp.where(t == s, sums[r], 0.0) for r in range(2)]
        for level, half in enumerate(HALVES):
            e = e_ref[level, rows, :]
            x = parts_of(e * gain)
            pairs = pair_mask(half)
            pe = split_rows(p * e, first)
            total = [total[r] + jnp.where(pairs, dot_parts(pe[r], x, NT), 0.0) for r in range(2)]
        for r in range(2):
            out_ref[r, rows, rows] = total[r]

    for right, left, half in far_pairs(tiles):
        after, before = far_decays(right, left, half, decay_ref, reach_ref)
        here = slice(right * TILE, (right + half) * TILE)
        there = slice(left * TILE, (left + half) * TILE)
        x = parts_of(before * gain_ref[there, :])
        pe = split_rows(p_ref[here, :] * after, first_row(half * TILE))
        for r in range(2):
            out_ref[r, here, there] = dot_parts(pe[r], x, NT)
            out_ref[r, there, here] = jnp.zeros((half * TILE, half * TILE), F32)


def inner(a, b, r):
    return dot(a[0][r], b[0][r], NT) + dot(a[1][r], b[1][r], NT)


def sigmoid(v):
    return 1.0 / (1.0 + jnp.exp(-v))


def projections(pre_ref, which, length, act):
    depth = DEPTH // 2
    return [
        [act(pre_ref[f, r * length:(r + 1) * length, which * depth:(which + 1) * depth]) for r in range(2)]
        for f in range(2)
    ]


def silu_low(v):
    return (v * sigmoid(v)).astype(BF16)


def low(v):
    return v.astype(BF16)


def forward_kernel(pre_ref, lf_ref, gain_ref, dcol_ref, drow_ref,
                   mixed_ref, s_ref, p_ref, b_ref, a_ref, decay_ref, reach_ref, e_ref):
    length = lf_ref.shape[0]
    tiles = length // TILE
    scale = DEPTH ** -0.5
    q, k = projections(pre_ref, 0, length, silu_low), projections(pre_ref, 1, length, silu_low)
    for r in range(2):
        same = dcol_ref[r] == drow_ref[r]
        a_ref[r] = jnp.where(same, inner(q, k, r), 0.0)
    prepare(lf_ref, decay_ref, reach_ref, e_ref, tiles)
    weighted_sums(a_ref, s_ref, gain_ref, decay_ref, reach_ref, e_ref, tiles)
    first = first_row(length)
    logits = s_ref[...] * scale
    least = -jnp.inf
    top = jnp.where(
        first,
        jnp.max(jnp.where(first, logits, least), axis=1, keepdims=True),
        jnp.max(jnp.where(first, least, logits), axis=1, keepdims=True),
    )
    grown = jnp.exp(logits - top)
    sums = row_sums(grown, first)
    p_ref[...] = grown / jnp.where(first, sums[0], sums[1])
    paired_weights(p_ref, b_ref, gain_ref, decay_ref, reach_ref, e_ref, tiles)
    v = projections(pre_ref, 2, length, low)
    for r in range(2):
        b = jnp.where(dcol_ref[r] == drow_ref[r], b_ref[r], 0.0)
        b_ref[r] = b
        high, rest = parts_of(b)
        for f in range(2):
            mixed = (dot(high, v[f][r], NN) + dot(rest, v[f][r], NN)).astype(BF16)
            for place in range(2):
                mixed_ref[r, place, f] = mixed[place * length // 2:(place + 1) * length // 2]


def to_columns(r, f):
    t, s = places()
    half = SLOTS // 2
    return ones_where((s < half) & (t == s + r * SLOTS + f * half))


def backward_kernel(pre_ref, g_ref, lf_ref, gain_ref, rate_ref, dcol_ref, drow_ref, s_ref, p_ref, b_ref,
                    out_ref, bias_ref, a_ref, at_ref, dot_ref, h_ref, back_ref, decay_ref, reach_ref, e_ref):
    length = lf_ref.shape[0]
    tiles, depth = length // TILE, DEPTH // 2
    scale = DEPTH ** -0.5
    first_all, first = first_row(length), first_row(TILE)
    t, s = places()
    q, k = projections(pre_ref, 0, length, silu_low), projections(pre_ref, 1, length, silu_low)
    v = projections(pre_ref, 2, length, low)
    grads = [[g_ref[r, :, f].reshape(length, depth) for r in range(2)] for f in range(2)]
    for r in range(2):
        same = dcol_ref[r] == drow_ref[r]
        a_ref[r] = jnp.where(same, inner(grads, v, r), 0.0)
        at_ref[0, r] = jnp.where(same, inner(k, q, r), 0.0)
        at_ref[1, r] = jnp.where(same, inner(v, grads, r), 0.0)
    prepare(lf_ref, decay_ref, reach_ref, e_ref, tiles)
    weighted_sums(a_ref, dot_ref, gain_ref, decay_ref, reach_ref, e_ref, tiles)
    p, dots = p_ref[...], dot_ref[...]
    sums = row_sums(p * dots, first_all)
    h = scale * (p * (dots - jnp.where(first_all, sums[0], sums[1])))
    h_ref[...] = h
    dot_ref[...] = h * s_ref[...] + p * dots
    paired_weights(h_ref, a_ref, gain_ref, decay_ref, reach_ref, e_ref, tiles)
    @pl.loop(0, tiles)
    def _(j):
        rows = tile_rows(j)
        h, p = h_ref[rows, :], p_ref[rows, :]
        keys = [at_ref[0, r, rows, rows] for r in range(2)]
        values = [at_ref[1, r, rows, rows] for r in range(2)]
        total = (
            jnp.where(first, diagonal_of(keys[0]), diagonal_of(keys[1])) * h
            + jnp.where(first, diagonal_of(values[0]), diagonal_of(values[1])) * p
        )
        for level, half in enumerate(HALVES):
            e = e_ref[level, rows, :]
            he, pe = parts_of(h * e), parts_of(p * e)
            pairs = pair_mask(half, turned=True)
            y = [
                dot_parts(parts_of(jnp.where(pairs, keys[r], 0.0)), he, NN)
                + dot_parts(parts_of(jnp.where(pairs, values[r], 0.0)), pe, NN)
                for r in range(2)
            ]
            total = total + e * jnp.where(first, y[0], y[1])
        back_ref[rows, :] = total

    for right, left, half in far_pairs(tiles):
        after, before = far_decays(right, left, half, decay_ref, reach_ref)
        here = slice(right * TILE, (right + half) * TILE)
        there = slice(left * TILE, (left + half) * TILE)
        he, pe = parts_of(h_ref[here, :] * after), parts_of(p_ref[here, :] * after)
        y = [
            dot_parts(parts_of(at_ref[0, r, there, here]), he, NN)
            + dot_parts(parts_of(at_ref[1, r, there, here]), pe, NN)
            for r in range(2)
        ]
        back_ref[there, :] += before * jnp.where(first_row(half * TILE), y[0], y[1])

    for r in range(2):
        rows = slice(r * length, (r + 1) * length)
        c = parts_of(jnp.where(dcol_ref[r] == drow_ref[r], a_ref[r], 0.0))
        w = parts_of(b_ref[r])
        for f in range(2):
            gq = dot(c[0], k[f][r], NN) + dot(c[1], k[f][r], NN)
            out_ref[f, rows, :depth] = (gq * slope(pre_ref[f, rows, :depth])).astype(BF16)
            gk = dot(c[0], q[f][r], TN) + dot(c[1], q[f][r], TN)
            out_ref[f, rows, depth:2 * depth] = (gk * slope(pre_ref[f, rows, depth:2 * depth])).astype(BF16)
            gv = dot(w[0], grads[f][r], TN) + dot(w[1], grads[f][r], TN)
            out_ref[f, rows, 2 * depth:3 * depth] = gv.astype(BF16)
    carried = jnp.zeros((1, 2 * SLOTS), F32)
    for j in range(tiles - 1, -1, -1):
        rows = slice(j * TILE, (j + 1) * TILE)
        back = back_ref[rows, :]
        change = dot_ref[rows, :] - gain_ref[rows, :] * back
        upward = dot_ones(ones_where(s >= t), change) + carried
        h_ref[rows, :] = (upward - jnp.exp(lf_ref[rows, :]) * back) * rate_ref[rows, :]
        carried = upward[0:1, :]
    grad_z = h_ref[...]
    bias_ref[...] = jnp.broadcast_to(jnp.sum(grad_z, axis=0, keepdims=True), bias_ref.shape)
    for r in range(2):
        for f in range(2):
            out_ref[f, r * length:(r + 1) * length, 3 * depth:] = dot(grad_z.astype(BF16), to_columns(r, f), NN).astype(BF16)


def slope(v):
    s = sigmoid(v)
    return s * (1.0 + v * (1.0 - s))


def cost(us):
    return pl.CostEstimate(flops=0, bytes_accessed=us * 3_000_000, transcendentals=0)


def mix_forward(pre, lf, gain, doc):
    length = lf.shape[0]
    lanes = (length, 2 * SLOTS)
    square = (2, length, length)
    return pl.pallas_call(
        forward_kernel,
        name="mix_forward",
        out_shape=(
            jax.ShapeDtypeStruct((2, 2, 2, length // 2, DEPTH // 2), BF16), jax.ShapeDtypeStruct(lanes, F32),
            jax.ShapeDtypeStruct(lanes, F32), jax.ShapeDtypeStruct(square, F32),
        ),
        scratch_shapes=[
            pltpu.VMEM(square, F32), pltpu.VMEM(lanes, F32), pltpu.VMEM(lanes, F32),
            pltpu.VMEM((len(HALVES),) + lanes, F32),
        ],
        compiler_params=pltpu.CompilerParams(vmem_limit_bytes=50 << 20),
        cost_estimate=cost(16),
    )(pre, lf, gain, doc[:, :, None], doc[:, None, :])


def mix_backward(pre, g, lf, gain, rate, doc, s, p, b):
    length = lf.shape[0]
    lanes = (length, 2 * SLOTS)
    square = (2, length, length)
    return pl.pallas_call(
        backward_kernel,
        name="mix_backward",
        out_shape=(jax.ShapeDtypeStruct(pre.shape, BF16), jax.ShapeDtypeStruct((8, 2 * SLOTS), F32)),
        scratch_shapes=[
            pltpu.VMEM(square, F32), pltpu.VMEM((2,) + square, F32),
            pltpu.VMEM(lanes, F32), pltpu.VMEM(lanes, F32), pltpu.VMEM(lanes, F32),
            pltpu.VMEM(lanes, F32), pltpu.VMEM(lanes, F32), pltpu.VMEM((len(HALVES),) + lanes, F32),
        ],
        compiler_params=pltpu.CompilerParams(vmem_limit_bytes=60 << 20),
        cost_estimate=cost(28),
    )(pre, g, lf, gain, rate, doc[:, :, None], doc[:, None, :], s, p, b)


def hidden_kernel(nf_ref, wg_ref, wu_ref, hidden_ref, slope_ref, silu_ref):
    nf = nf_ref[...]
    gate, up = dot(nf, wg_ref[0], NN), dot(nf, wu_ref[0], NN)
    s = sigmoid(gate)
    silu = gate * s
    hidden_ref[0] = (silu * up).astype(BF16)
    slope_ref[0] = (up * (s * (1.0 + gate * (1.0 - s)))).astype(BF16)
    silu_ref[0] = silu.astype(BF16)


def unit_specs(tokens, features, units):
    rows = tokens // 2
    return (
        pl.BlockSpec((rows, features), lambda h, t: (t, 0)),
        pl.BlockSpec((1, features, units), lambda h, t: (h, 0, 0)),
        pl.BlockSpec((1, rows, units), lambda h, t: (h, t, 0)),
        jax.ShapeDtypeStruct((2, tokens, units), BF16),
    )


def hidden_units(nf, wg, wu):
    some, weight, unit, units_all = unit_specs(*nf.shape, wg.shape[2])
    return pl.pallas_call(
        hidden_kernel,
        name="hidden_units",
        grid=(2, 2),
        in_specs=[some, weight, weight],
        out_specs=[unit] * 3,
        out_shape=[units_all] * 3,
        compiler_params=pltpu.CompilerParams(vmem_limit_bytes=60 << 20),
        cost_estimate=cost(20),
    )(nf, wg, wu)


def hidden_grads_kernel(cot_ref, slope_ref, silu_ref, wg_ref, wu_ref, wd_ref, gg_ref, gu_ref, back_ref, total_ref):
    half, tile = pl.program_id(0), pl.program_id(1)
    rows = cot_ref.shape[0]
    here = pl.ds(pl.multiple_of(tile * rows, rows), rows)
    grad = dot(cot_ref[...], wd_ref[0], NT)
    gg = (grad * slope_ref[0].astype(F32)).astype(BF16)
    gu = (grad * silu_ref[0].astype(F32)).astype(BF16)
    gg_ref[0], gu_ref[0] = gg, gu
    back = dot(gg, wg_ref[0], NT) + dot(gu, wu_ref[0], NT)

    @pl.when(half == 0)
    def _():
        total_ref[here, :] = back

    @pl.when(half == 1)
    def _():
        back_ref[...] = (total_ref[here, :] + back).astype(BF16)


def hidden_grads(cot, slopes, silus, wg, wu, wd):
    tokens, features = cot.shape
    units = wg.shape[2]
    some, weight, unit, units_all = unit_specs(tokens, features, units)
    return pl.pallas_call(
        hidden_grads_kernel,
        name="hidden_grads",
        grid=(2, 2),
        in_specs=[some, unit, unit, weight, weight, pl.BlockSpec((1, units, features), lambda h, t: (h, 0, 0))],
        out_specs=[unit, unit, pl.BlockSpec((tokens // 2, features), lambda h, t: (h * t, 0))],
        out_shape=[units_all, units_all, jax.ShapeDtypeStruct(cot.shape, BF16)],
        scratch_shapes=[pltpu.VMEM((tokens, features), F32)],
        compiler_params=pltpu.CompilerParams(vmem_limit_bytes=60 << 20),
        cost_estimate=cost(32),
    )(cot, slopes, silus, wg, wu, wd)


def later(count, waits, body, *refs):
    body(*refs[:count], *refs[count + waits:])


def out_kernel(a_ref, b_ref, out_ref):
    grads = dot(a_ref[...], b_ref[0], TN).astype(BF16)
    wide = grads.shape[1] // 2
    for f in range(2):
        out_ref[0, f] = grads[:, f * wide:(f + 1) * wide]


def out_grads(a, b):
    planes = lax.axis_size("z")
    tokens, depth = a.shape
    features = b.shape[2]
    rows = max(depth // planes, TILE)
    grads = pl.pallas_call(
        out_kernel,
        name="out_grads",
        grid=(depth // rows,),
        in_specs=[
            pl.BlockSpec((tokens, rows), lambda i: (0, i)), pl.BlockSpec((1, tokens, features), lambda i: (0, 0, 0)),
        ],
        out_specs=pl.BlockSpec((1, 2, rows, features // 2), lambda i: (i, 0, 0, 0)),
        out_shape=jax.ShapeDtypeStruct((depth // rows, 2, rows, features // 2), BF16),
        compiler_params=pltpu.CompilerParams(vmem_limit_bytes=60 << 20),
        cost_estimate=cost(8),
    )(a, b)
    if rows * planes > depth:
        grads = grads.reshape(-1, 2, rows * planes // depth, depth // planes, features // 2).transpose(0, 2, 1, 3, 4)
    return grads.reshape(planes, 2, depth // planes, features // 2)


def weight_kernel(a_ref, *refs):
    for i, b_ref in enumerate(refs[:-1]):
        refs[-1][0, 0, i] = dot(a_ref[...], b_ref[0], TN).astype(BF16)


def weight_sums_kernel(a_ref, b_ref, sums_ref, out_ref):
    grads = dot(a_ref[...], b_ref[0], TN)
    wide = grads.shape[1]
    out_ref[0, 0, 0, :, :wide - TILE] = grads[:, :wide - TILE].astype(BF16)
    once = jnp.where(pl.program_id(0) == 0, 1.0, 0.0)
    out_ref[0, 0, 0, :, wide - TILE:] = (grads[:, wide - TILE:] + once * sums_ref[...]).astype(BF16)


def weight_grads(a, *others, sums=None, after=()):
    planes = lax.axis_size("z")
    tokens, features = a.shape
    rows = features // planes
    specs = [pl.BlockSpec((tokens, rows), lambda h, z: (0, z))]
    specs += [pl.BlockSpec((1,) + b.shape[1:], lambda h, z: (h, 0, 0)) for b in others]
    body, operands = weight_kernel, (a,) + others
    count, columns = len(others), others[0].shape[2]
    if sums is not None:
        body, operands = weight_sums_kernel, operands + (sums,)
        specs.append(pl.BlockSpec((rows, TILE), lambda h, z: (z, 0)))
    if after:
        body = functools.partial(later, len(operands), len(after), body)
        specs += [pl.BlockSpec(memory_space=pl.ANY)] * len(after)
    return pl.pallas_call(
        body,
        name="weight_grads",
        grid=(2, planes),
        in_specs=specs,
        out_specs=pl.BlockSpec((1, 1, count, rows, columns), lambda h, z: (z, h, 0, 0, 0)),
        out_shape=jax.ShapeDtypeStruct((planes, 2, count, rows, columns), BF16),
        compiler_params=pltpu.CompilerParams(vmem_limit_bytes=60 << 20),
        cost_estimate=cost(12 * len(others)),
    )(*operands, *after)


def down_kernel(hidden_ref, cot_ref, out_ref):
    grads = dot(hidden_ref[0], cot_ref[...], TN)
    rows = out_ref.shape[2]
    for z in range(out_ref.shape[0]):
        out_ref[z, 0] = grads[z * rows:(z + 1) * rows].astype(BF16)


def down_grads(hidden, cot):
    planes = lax.axis_size("z")
    tokens, features = cot.shape
    units = hidden.shape[2]
    wide = features // 2
    return pl.pallas_call(
        down_kernel,
        name="down_grads",
        grid=(2, 2),
        in_specs=[
            pl.BlockSpec((1, tokens, units), lambda h, i: (h, 0, 0)),
            pl.BlockSpec((tokens, wide), lambda h, i: (0, i)),
        ],
        out_specs=pl.BlockSpec((planes, 1, units // planes, wide), lambda h, i: (0, h, 0, i)),
        out_shape=jax.ShapeDtypeStruct((planes, 2, units // planes, features), BF16),
        compiler_params=pltpu.CompilerParams(vmem_limit_bytes=60 << 20),
        cost_estimate=cost(12),
    )(hidden, cot)


def input_kernel(grad_ref, w_ref, x_ref, out_ref, sums_ref):
    tile = pl.program_id(0)
    back = dot(grad_ref[0], w_ref[0], NT) + dot(grad_ref[1], w_ref[1], NT)
    out_ref[...] = back.astype(BF16)
    x = x_ref[...].astype(F32)
    xh = x * lax.rsqrt(jnp.mean(x * x, axis=1, keepdims=True) + EPSILON)
    sums = jnp.sum((back * xh).reshape(-1, 8, back.shape[1]), axis=0)
    sums_ref[...] = jnp.where(tile == 0, sums, sums_ref[...] + sums)


def input_grads(grad, w, x):
    tokens, features = x.shape
    rows = tokens // 4
    return pl.pallas_call(
        input_kernel,
        name="input_grads",
        grid=(4,),
        in_specs=[
            pl.BlockSpec((2, rows, grad.shape[2]), lambda t: (0, t, 0)), pl.BlockSpec(w.shape, lambda t: (0, 0, 0)),
            pl.BlockSpec((rows, features), lambda t: (t, 0)),
        ],
        out_specs=[pl.BlockSpec((rows, features), lambda t: (t, 0)), pl.BlockSpec((8, features), lambda t: (0, 0))],
        out_shape=[jax.ShapeDtypeStruct(x.shape, BF16), jax.ShapeDtypeStruct((8, features), F32)],
        compiler_params=pltpu.CompilerParams(vmem_limit_bytes=60 << 20),
        cost_estimate=cost(12),
    )(grad, w, x)


MESH = pl.DeviceIdType.MESH


def routes(kind, i, y, x, c):
    chip = {"y": i // 2 % 2, "x": i % 2}
    if kind == "to_homes":
        return {"y": c, "x": i // 2, "c": i % 2}, {**chip, "c": y}, y * 2 + x
    if kind in ("from_homes", "copy_homes"):
        return {**chip, "c": y}, {"y": c, "x": i // 2, "c": i % 2}, x * 2 + c
    if kind == "columns":
        return {**chip, "c": c}, {**chip, "c": c}, y * 2 + x
    return {**chip, "c": i // 4}, {**chip, "c": i // 4}, c * 4 + y * 2 + x


def enter_plane(y, x, c, more=()):
    barrier = pltpu.get_barrier_semaphore()
    peers = list(more)
    for flip in range(1, 8):
        peers.append({
            "y": lax.rem(y + flip // 4, 2), "x": lax.rem(x + (flip // 2) % 2, 2), "c": lax.rem(c + flip % 2, 2)
        })
    for peer in peers:
        pl.semaphore_signal(barrier, inc=1, device_id=peer, device_id_type=MESH)
    pl.semaphore_wait(barrier, len(peers))


def swap_kernel_sems(count):
    return [pltpu.SemaphoreType.DMA((count,)), pltpu.SemaphoreType.DMA((count,))]


def enter_pairs(y, x):
    barrier = pltpu.get_barrier_semaphore()
    for peer in ({"y": 1 - y}, {"x": 1 - x}):
        pl.semaphore_signal(barrier, inc=1, device_id=peer, device_id_type=MESH)
    pl.semaphore_wait(barrier, 2)


def remote(source, target, send, recv, peer):
    return pltpu.make_async_remote_copy(
        src_ref=source, dst_ref=target, send_sem=send, recv_sem=recv, device_id=peer, device_id_type=MESH
    )


class Gather:
    def __init__(self, a_ref, out_ref, y, x, send, recv, local):
        to_x, to_y = {"x": 1 - x}, {"y": 1 - y}
        self.places = here, at_x, at_y, _ = y * 2 + x, y * 2 + 1 - x, (1 - y) * 2 + x, (1 - y) * 2 + 1 - x
        half = a_ref.shape[0] // 2
        parts = [pl.ds(0, half), pl.ds(half, half)]

        def copy(source, place, part, n, peer):
            return remote(source.at[parts[part]], out_ref.at[place, parts[part]], send.at[n], recv.at[n], peer)

        self.own = pltpu.make_async_copy(a_ref, out_ref.at[here], local)
        self.first = [copy(a_ref, here, 0, 0, to_x), copy(a_ref, here, 1, 1, to_y)]
        self.second = [copy(a_ref, here, 1, 2, to_x), copy(a_ref, here, 0, 3, to_y)]
        self.passed = [copy(out_ref.at[at_x], at_x, 0, 4, to_y), copy(out_ref.at[at_y], at_y, 1, 5, to_x)]

    def start(self):
        for copy in [self.own] + self.first + self.second:
            copy.start()

    def go_on(self):
        for copy, onward in zip(self.first, self.passed):
            copy.wait_recv()
            onward.start()

    def wait(self):
        for copy in self.second + self.passed:
            copy.wait_recv()
        for copy in self.first + self.second + self.passed:
            copy.wait_send()
        self.own.wait()


def gather_kernel(count, *refs):
    outs, sems = refs[-4 * count:-3 * count], refs[-3 * count:]
    y, x = lax.axis_index("y"), lax.axis_index("x")
    enter_pairs(y, x)
    gathers = [Gather(refs[n], outs[n], y, x, *sems[3 * n:3 * n + 3]) for n in range(count)]
    for gather in gathers:
        gather.start()
    for gather in gathers:
        gather.go_on()
    for gather in gathers:
        gather.wait()


def gather_sems():
    return swap_kernel_sems(6) + [pltpu.SemaphoreType.DMA]


def gather_plane(collective, *arrays, after=()):
    any_place, count = pl.BlockSpec(memory_space=pl.ANY), len(arrays)
    return pl.pallas_call(
        functools.partial(gather_kernel, count),
        name="gather_plane",
        out_shape=[jax.ShapeDtypeStruct((4,) + a.shape, a.dtype) for a in arrays],
        in_specs=[any_place] * (count + len(after)),
        out_specs=[any_place] * count,
        scratch_shapes=gather_sems() * count,
        compiler_params=pltpu.CompilerParams(collective_id=collective, has_side_effects=True),
        cost_estimate=cost(38 * count),
    )(*arrays, *after)


class Moves:
    def __init__(self, kind, a_ref, out_ref, y, x, c, send, recv, local):
        self.copies = []
        for i in range(out_ref.shape[0]):
            peer, giver, slot = routes(kind, i, y, x, c)
            source = a_ref if kind == "copy_homes" else a_ref.at[:, i % 4] if kind == "spread" else a_ref.at[i]
            to_me, from_me = (
                (at["y"] == y) & (at["x"] == x) & (at["c"] == c) for at in (peer, giver)
            )
            self.copies.append((
                to_me, from_me,
                pltpu.make_async_copy(source, out_ref.at[slot], local),
                remote(source, out_ref.at[slot], send.at[i], recv.at[slot], peer),
                pltpu.make_async_copy(source, out_ref.at[i], local),
                remote(source, out_ref.at[i], send.at[i], recv.at[i], peer),
            ))

    def start(self):
        for to_me, _, here, there, _, _ in self.copies:
            pl.when(to_me)(here.start)
            pl.when(jnp.logical_not(to_me))(there.start)

    def wait(self):
        for to_me, from_me, _, _, here, there in self.copies:
            pl.when(jnp.logical_not(to_me))(there.wait_send)
            pl.when(jnp.logical_not(from_me))(there.wait_recv)
            pl.when(from_me)(here.wait)


def move_sems(kind):
    slots = 8 if kind == "spread" else 4
    return swap_kernel_sems(slots) + [pltpu.SemaphoreType.DMA]


def moved(kind, a):
    block = a.shape if kind == "copy_homes" else (a.shape[0],) + a.shape[2:] if kind == "spread" else a.shape[1:]
    return jax.ShapeDtypeStruct((8 if kind == "spread" else 4,) + block, a.dtype)


def move_kernel(kinds, waits, *refs):
    count = len(kinds)
    sources, results, sems = refs[:count], refs[count + waits:2 * count + waits], refs[2 * count + waits:]
    y, x, c = (lax.axis_index(name) for name in ("y", "x", "c"))
    enter_plane(y, x, c)
    moves = [
        Moves(kind, sources[n], results[n], y, x, c, *sems[3 * n:3 * n + 3]) for n, kind in enumerate(kinds)
    ]
    for one in moves:
        one.start()
    for one in moves:
        one.wait()


def move(collective, *items, after=(), us=48):
    kinds = tuple(kind for kind, _ in items)
    any_place = pl.BlockSpec(memory_space=pl.ANY)
    return pl.pallas_call(
        functools.partial(move_kernel, kinds, len(after)),
        name=kinds[0],
        out_shape=[moved(kind, a) for kind, a in items],
        in_specs=[any_place] * (len(items) + len(after)),
        out_specs=[any_place] * len(items),
        scratch_shapes=[sem for kind in kinds for sem in move_sems(kind)],
        compiler_params=pltpu.CompilerParams(collective_id=collective, has_side_effects=True),
        cost_estimate=cost(us),
    )(*(a for _, a in items), *after)


def start_kernel(kinds, planes, *refs):
    count = len(kinds)
    sources, w_ref, m_ref = refs[:count], refs[count], refs[count + 1]
    results, w_out_ref, m_out_ref = refs[count + 2:2 * count + 2], refs[2 * count + 2], refs[2 * count + 3]
    sems = refs[2 * count + 4:]
    y, x, c, z = (lax.axis_index(name) for name in ("y", "x", "c", "z"))
    up, down = lax.rem(z + 1, planes), lax.rem(z + planes - 1, planes)
    enter_plane(y, x, c, [{"z": up}, {"z": down}])
    moves = [
        Moves(kind, sources[n], results[n], y, x, c, *sems[3 * n:3 * n + 3]) for n, kind in enumerate(kinds)
    ]
    sems = sems[3 * count:]
    rows = Gather(w_ref, w_out_ref.at[c], y, x, *sems[:3])
    m_send, m_recv, core_send, core_recv, pass_send, pass_recv, local = sems[3:]
    other = {"c": 1 - c}

    def block(step):
        at = lax.rem(z + planes - step, planes)
        return m_ref if step == 0 else m_out_ref.at[c, at], m_out_ref.at[c, at]

    ring = [remote(*block(step), m_send.at[step], m_recv.at[step], {"z": up}) for step in range(planes - 1)]
    across = [remote(*block(step), core_send.at[step], core_recv.at[step], other) for step in range(planes)]
    own = pltpu.make_async_copy(m_ref, m_out_ref.at[c, z], local)
    passed = [
        remote(w_ref if n == 0 else w_out_ref.at[c, at], w_out_ref.at[c, at], pass_send.at[n], pass_recv.at[n], other)
        for n, at in enumerate(rows.places)
    ]
    ring[0].start()
    across[0].start()
    own.start()
    for one in moves:
        one.start()
    rows.start()
    passed[0].start()
    rows.go_on()
    for step in range(planes - 1):
        ring[step].wait_recv()
        if step < planes - 2:
            ring[step + 1].start()
        across[step + 1].start()
    for one in moves:
        one.wait()
    rows.wait()
    for copy in passed[1:]:
        copy.start()
    for copy in across + passed:
        copy.wait()
    for copy in ring:
        copy.wait_send()
    own.wait()


def start_moves(collective, items, w_half, mixer_part):
    planes = lax.axis_size("z")
    kinds = tuple(kind for kind, _ in items)
    any_place = pl.BlockSpec(memory_space=pl.ANY)
    shapes = [moved(kind, a) for kind, a in items]
    shapes.append(jax.ShapeDtypeStruct((2, 4) + w_half.shape, w_half.dtype))
    shapes.append(jax.ShapeDtypeStruct((2, planes) + mixer_part.shape, mixer_part.dtype))
    sems = [sem for kind in kinds for sem in move_sems(kind)] + gather_sems()
    sems += swap_kernel_sems(planes) + swap_kernel_sems(planes) + swap_kernel_sems(4) + [pltpu.SemaphoreType.DMA]
    return pl.pallas_call(
        functools.partial(start_kernel, kinds, planes),
        name="start_moves",
        out_shape=shapes,
        in_specs=[any_place] * (len(items) + 2),
        out_specs=[any_place] * len(shapes),
        scratch_shapes=sems,
        compiler_params=pltpu.CompilerParams(collective_id=collective, has_side_effects=True),
        cost_estimate=cost(85),
    )(*(a for _, a in items), w_half, mixer_part)


def reduce_kernel(a_ref, *refs):
    out_ref, got_ref, sum_ref, last_ref, send, recv = refs[-6:]
    y, x = lax.axis_index("y"), lax.axis_index("x")
    enter_pairs(y, x)
    half = out_ref.shape[0] // 2
    parts = [pl.ds(0, half), pl.ds(half, half)]
    places = [(1 - y, y), (1 - x, x)]
    peers = [{"x": 1 - x}, {"y": 1 - y}]

    def block(part, place, other):
        if part == 0:
            return place * 2 + (1 - x if other else x)
        return (1 - y if other else y) * 2 + place

    def copy(source, target, n, peer):
        return remote(source, target, send.at[n], recv.at[n], peer)

    first = [
        [copy(a_ref.at[block(part, places[part][i], True), parts[part]], got_ref.at[part, i], 2 * part + i, peers[part])
         for i in range(2)] for part in range(2)
    ]
    for i in range(2):
        for part in range(2):
            first[part][i].start()
    onward = [copy(sum_ref.at[part], last_ref.at[part], 4 + part, peers[1 - part]) for part in range(2)]

    def total(part, i):
        own = a_ref[block(part, places[part][i], False), parts[part], :]
        return own.astype(F32) + got_ref[part, i].astype(F32)

    for part in range(2):
        first[part][0].wait_recv()
        sum_ref[part] = total(part, 0).astype(BF16)
        onward[part].start()
    for part in range(2):
        first[part][1].wait_recv()
        out_ref[parts[part], :] = total(part, 1)
    for part in range(2):
        onward[part].wait_recv()
        out_ref[parts[part], :] += last_ref[part].astype(F32)
    for one in first[0] + first[1] + onward:
        one.wait_send()


def reduce_plane(collective, a, after=()):
    rows, features = a.shape[1:]
    half = (rows // 2, features)
    return pl.pallas_call(
        reduce_kernel,
        name="reduce_plane",
        out_shape=jax.ShapeDtypeStruct((rows, features), F32),
        in_specs=[pl.BlockSpec(memory_space=pltpu.VMEM)] + [pl.BlockSpec(memory_space=pl.ANY)] * len(after),
        out_specs=pl.BlockSpec(memory_space=pltpu.VMEM),
        scratch_shapes=[pltpu.VMEM((2, 2) + half, BF16), pltpu.VMEM((2,) + half, BF16), pltpu.VMEM((2,) + half, BF16)]
        + swap_kernel_sems(6),
        compiler_params=pltpu.CompilerParams(collective_id=collective, has_side_effects=True),
        cost_estimate=cost(38),
    )(a, *after)


def add_other(a, other):
    return (a.astype(F32) + other.astype(F32)).astype(BF16)


def halves_of(a, place, axis):
    here = lax.axis_index(axis)
    return [lax.dynamic_index_in_dim(a, at, place, keepdims=False) for at in (here, 1 - here)]


def gather_planes(a):
    return lax.all_gather(a, ("c", "z"), axis=0, tiled=True).reshape((2, -1) + a.shape[1:])


def sum_planes(a):
    return lax.psum_scatter(a.reshape((-1,) + a.shape[2:]), ("z", "c"), scatter_dimension=0, tiled=True)[0]


def swap(a, axis):
    return lax.ppermute(a, axis, [(0, 1), (1, 0)])


def both_of(a, axis):
    other = swap(a, axis)
    return jnp.where(lax.axis_index(axis) == 0, jnp.stack([a, other]), jnp.stack([other, a]))


def scaled(features):
    return lax.rsqrt(jnp.mean(features * features, axis=-1, keepdims=True) + EPSILON)


def norm_back(grad, gain, features, ratio):
    u, xh = grad * gain, features * ratio
    return ratio * (u - xh * jnp.mean(u * xh, axis=-1, keepdims=True))


def body(inputs, starts, norm_attn, w_query, w_key, w_value, w_forget, gate_bias, w_out, norm_ffn, w_gate, w_up,
         w_down, cotangent):
    positions, features = inputs.shape[1:]
    depth = features // HEADS
    y, x, c, z = (lax.axis_index(name) for name in ("y", "x", "c", "z"))
    planes = lax.axis_size("z")
    head = y * 2 + x
    rows_here = w_query.shape[0]
    hidden_here = w_down.shape[0]

    def own_half(a, axis):
        return lax.dynamic_index_in_dim(a, c, axis, keepdims=False)

    bias_here = gate_bias.shape[0]

    def columns(w):
        w = w.reshape(rows_here, HEADS, 2, -1)
        return own_half(w, 2).transpose(1, 0, 2)

    def column(v):
        v = jnp.pad(v, (0, rows_here - v.shape[0]))
        return jnp.broadcast_to(v[None, :, None], (HEADS, rows_here, 1))

    parts = [columns(w) for w in (w_query, w_key, w_value, w_forget)]
    parts += [column(v) for v in (norm_attn, norm_ffn, gate_bias)]
    width = sum(part.shape[-1] for part in parts)
    parts.append(jnp.zeros((HEADS, rows_here, -width % TILE), BF16))
    vectors = width - 3
    def hidden_columns(w):
        w = own_half(w.reshape(rows_here, planes, 4, 2, hidden_here // 2), 3)
        return w.transpose(2, 0, 1, 3).reshape(4, rows_here, -1)

    x_here = inputs.reshape(positions, features)
    cot_here = cotangent.reshape(positions, features)
    out_half = own_half(w_out.reshape(2, rows_here // 2, features), 0)
    out_half = lax.all_gather(out_half, "z", axis=0)
    (mine,) = move(1, ("columns", jnp.concatenate(parts, axis=-1)), us=14)
    full_down = gather_planes(own_half(w_down.reshape(2, hidden_here // 2, features), 0))
    begins, x_rows, gate_mine, up_mine, full_out, mixer_w = start_moves(
        2, (
            ("copy_homes", jnp.broadcast_to(starts, (8, positions))), ("copy_homes", x_here),
            ("columns", hidden_columns(w_gate)), ("columns", hidden_columns(w_up)),
        ), out_half, mine.reshape(4 * rows_here, -1),
    )
    full_gate = gather_planes(gate_mine.reshape(4 * rows_here, -1))
    full_up = gather_planes(up_mine.reshape(4 * rows_here, -1))
    full_out = full_out.reshape(2, 4, planes, rows_here // 2, features)
    full_out = full_out.transpose(2, 1, 0, 3, 4).reshape(features, features)
    mixer_w = mixer_w.reshape(2, features, -1)
    gain_attn, gain_ffn = (mixer_w[0, :, vectors + i].astype(F32) for i in range(2))
    bias = mixer_w[0, :, vectors + 2].reshape(4 * planes, rows_here)[:, :bias_here].reshape(-1).astype(F32)
    bias = lax.dynamic_slice_in_dim(bias, head * SLOTS, SLOTS)
    doc = jnp.cumsum(begins[:, 0].reshape(2, 2 * positions).astype(F32), axis=1)

    x_rows = x_rows.reshape(4 * positions, features)
    x_wide = x_rows.astype(F32)
    normed = (x_wide * scaled(x_wide) * gain_attn).astype(BF16)
    pre = jnp.einsum("td,cdf->ctf", normed, mixer_w, preferred_element_type=F32)
    z_total = pre[:, :, 3 * depth // 2:vectors].reshape(2, 2, 2 * positions, SLOTS // 2)
    z_total = z_total.transpose(2, 1, 0, 3).reshape(2 * positions, 2 * SLOTS) + jnp.tile(bias, 2)
    log_forget = jax.nn.log_sigmoid(z_total) / 8.0
    gain = -jnp.expm1(log_forget)
    mixed, scores, probs, paired = mix_forward(pre, log_forget, gain, doc)
    mixed_rows = mixed.reshape(4, 2, positions, depth // 2).transpose(0, 2, 1, 3).reshape(4 * positions, depth)
    (mixed,) = move(4, ("to_homes", mixed.reshape(4, 2 * positions, depth // 2)), us=14)
    mixed = mixed.reshape(2 * HEADS, positions, depth // 2).transpose(1, 0, 2).reshape(positions, features)
    attended = x_here.astype(F32) + jnp.dot(mixed, full_out, preferred_element_type=F32)

    ratio_f = scaled(attended)
    normed_ffn, cot = gather_plane(5, (attended * ratio_f * gain_ffn).astype(BF16), cot_here)
    cot = cot.reshape(4 * positions, features)
    normed_ffn = normed_ffn.reshape(4 * positions, features)
    hidden, slopes, silus = hidden_units(normed_ffn, full_gate, full_up)
    grad_down_w = down_grads(hidden, cot)
    grad_gate, grad_up, grad_normed_ffn = hidden_grads(cot, slopes, silus, full_gate, full_up, full_down)
    grad_hidden_w = weight_grads(normed_ffn, grad_gate, grad_up)
    grad_normed_ffn = reduce_plane(
        6, grad_normed_ffn.reshape(4, positions, features), after=(grad_down_w, grad_hidden_w)
    )
    grad_down_w, grad_hidden_w = sum_planes(grad_down_w), sum_planes(grad_hidden_w)
    block_out = jnp.einsum("ctf,cfd->td", hidden, full_down, preferred_element_type=F32).astype(BF16)
    grad_gain_ffn = jnp.sum(grad_normed_ffn * attended * ratio_f, axis=0)
    grad_attended = cot_here.astype(F32) + norm_back(grad_normed_ffn, gain_ffn, attended, ratio_f)

    grad_branch = grad_attended.astype(BF16)
    grad_mixed = jnp.einsum("te,de->td", grad_branch, full_out, preferred_element_type=F32).astype(BF16)
    grad_mixed = grad_mixed.reshape(positions, HEADS, 2, depth // 2).transpose(1, 2, 0, 3)
    grad_mixed, branch_rows = move(
        8, ("from_homes", grad_mixed.reshape(4, 2 * positions, depth // 2)), ("copy_homes", grad_branch),
        after=(grad_down_w,), us=60,
    )
    branch_rows = branch_rows.reshape(1, 4 * positions, features)
    grad_mixed = grad_mixed.reshape(2, 2, 2, positions, depth // 2)
    rate = jax.nn.sigmoid(-z_total) / 8.0
    grad_pre, grad_bias = mix_backward(pre, grad_mixed, log_forget, gain, rate, doc, scores, probs, paired)
    grad_bias = jnp.sum(grad_bias[0].reshape(2, SLOTS), axis=0)
    grad_out_w = out_grads(mixed_rows, branch_rows)
    grad_normed, sums = input_grads(grad_pre, mixer_w, x_rows)
    grad_bias = jnp.zeros((HEADS, SLOTS), F32).at[head].set(grad_bias).reshape(4 * planes, bias_here)
    grad_bias = jnp.pad(grad_bias, ((0, 0), (0, rows_here - bias_here))).reshape(-1)
    sums = jnp.stack([jnp.sum(sums, axis=0), grad_gain_ffn, grad_bias], axis=-1)
    first_sum = vectors + TILE - mixer_w.shape[-1]
    sums = jnp.pad(sums, ((0, 0), (first_sum, TILE - first_sum - 3)))
    grad_mixer_w = weight_grads(normed, grad_pre, sums=sums, after=(grad_hidden_w,))
    grad_out_w = sum_planes(grad_out_w)
    grad_normed, grad_hidden_w = move(
        9, ("to_homes", grad_normed.reshape(4, positions, features)),
        ("spread", grad_hidden_w.reshape(2, 4, rows_here, -1)), after=(grad_mixer_w, grad_out_w), us=75,
    )
    grad_mixer_w = sum_planes(grad_mixer_w)
    grad_normed_here = jnp.sum(grad_normed.astype(F32), axis=0)
    x_here = x_here.astype(F32)
    ratio_a = scaled(x_here)
    grad_input = grad_attended + norm_back(grad_normed_here, gain_attn, x_here, ratio_a)

    block_out = reduce_plane(7, block_out.reshape(4, positions, features), after=(grad_normed,))
    output = (attended + block_out).astype(BF16)

    def to_rows(collective, a):
        (a,) = move(collective, ("spread", a.reshape(a.shape[0], 4, rows_here, -1)), us=18)
        return a.reshape((2, 4) + a.shape[1:])

    def from_hidden(a):
        a = a.reshape(2, 4, rows_here, planes, hidden_here // 2)
        return a.transpose(2, 3, 1, 0, 4).reshape(rows_here, -1).astype(F32)

    grad_hidden_w = grad_hidden_w.reshape((2, 4) + grad_hidden_w.shape[1:])
    grad_gate_w, grad_up_w = from_hidden(grad_hidden_w[:, :, 0]), from_hidden(grad_hidden_w[:, :, 1])
    blocks = 4 * planes
    grad_out_w = lax.ppermute(
        grad_out_w, ("z", "y", "x"), [(at, at % 4 * planes + at // 4) for at in range(blocks)]
    )
    grad_out_w = both_of(grad_out_w, "c").transpose(1, 0, 2).reshape(rows_here, features).astype(F32)
    grad_down_w = both_of(grad_down_w, "c").reshape(hidden_here, features).astype(F32)
    grad_mixer_w = to_rows(12, grad_mixer_w)[:, :, 0]
    sums = jnp.sum(grad_mixer_w[0, :, :, vectors:width].astype(F32), axis=0)
    grad_mixer_w = grad_mixer_w.transpose(2, 1, 0, 3)
    grad_w = [
        grad_mixer_w[..., i * depth // 2:(i + 1) * depth // 2].reshape(rows_here, features).astype(F32) for i in range(3)
    ]
    grad_forget_w = grad_mixer_w[..., 3 * depth // 2:vectors].reshape(rows_here, HEADS * SLOTS).astype(F32)
    return (
        output.reshape(inputs.shape), grad_input.reshape(inputs.shape), sums[:, 0], grad_w[0], grad_w[1], grad_w[2],
        grad_forget_w, sums[:bias_here, 2], grad_out_w, sums[:, 1], grad_gate_w, grad_up_w, grad_down_w,
    )


def solution(mesh):
    planes = mesh.shape["dp"] // 4
    fine = Mesh(mesh.devices.reshape(planes, 2, 2, 2), ("z", "y", "x", "c"))
    dp = ("z", "y", "x")
    tokens, vector, matrix = P(dp, "c", None), P(dp), P(dp, None)
    in_specs = (
        tokens, P(dp, "c"), vector, matrix, matrix, matrix, matrix, vector, matrix, vector, matrix, matrix, matrix, tokens
    )
    out_specs = (
        tokens, tokens, vector, matrix, matrix, matrix, matrix, vector, matrix, vector, matrix, matrix, matrix
    )
    return jax.shard_map(body, mesh=fine, in_specs=in_specs, out_specs=out_specs, check_vma=False)
```

```python
import functools

import jax
import jax.numpy as jnp
from jax import lax
from jax.sharding import Mesh
from jax.sharding import PartitionSpec as P
from jax.experimental import pallas as pl
from jax.experimental.pallas import tpu as pltpu

HEADS = 4
SLOTS = 64
DEPTH = 512
TILE = 128
EPSILON = 1e-06
F32, BF16 = jnp.float32, jnp.bfloat16
NN = (((1,), (0,)), ((), ()))
NT = (((1,), (1,)), ((), ()))
TN = (((0,), (0,)), ((), ()))
HALVES = (64, 32, 16, 8, 4, 2, 1)
MESH = pl.DeviceIdType.MESH


def cost(us):
    return pl.CostEstimate(flops=0, bytes_accessed=us * 3_000_000, transcendentals=0)


def routes(kind, i, y, x, c):
    chip = {"y": i // 2 % 2, "x": i % 2}
    if kind == "to_homes":
        return {"y": c, "x": i // 2, "c": i % 2}, {**chip, "c": y}, y * 2 + x
    if kind in ("from_homes", "copy_homes"):
        return {**chip, "c": y}, {"y": c, "x": i // 2, "c": i % 2}, x * 2 + c
    return {**chip, "c": c}, {**chip, "c": c}, y * 2 + x


def enter_plane(y, x, c, more=()):
    barrier = pltpu.get_barrier_semaphore()
    peers = list(more)
    for flip in range(1, 8):
        peers.append({
            "y": lax.rem(y + flip // 4, 2), "x": lax.rem(x + (flip // 2) % 2, 2), "c": lax.rem(c + flip % 2, 2)
        })
    for peer in peers:
        pl.semaphore_signal(barrier, inc=1, device_id=peer, device_id_type=MESH)
    pl.semaphore_wait(barrier, len(peers))


def swap_kernel_sems(count):
    return [pltpu.SemaphoreType.DMA((count,)), pltpu.SemaphoreType.DMA((count,))]


def enter_pairs(y, x):
    barrier = pltpu.get_barrier_semaphore()
    for peer in ({"y": 1 - y}, {"x": 1 - x}):
        pl.semaphore_signal(barrier, inc=1, device_id=peer, device_id_type=MESH)
    pl.semaphore_wait(barrier, 2)


def remote(source, target, send, recv, peer):
    return pltpu.make_async_remote_copy(
        src_ref=source, dst_ref=target, send_sem=send, recv_sem=recv, device_id=peer, device_id_type=MESH
    )


class Stay:
    def __init__(self, source, target, sem, buffer):
        self.load = pltpu.make_async_copy(source, buffer, sem)
        self.store = pltpu.make_async_copy(buffer, target, sem)

    def start(self):
        self.load.start()
        self.load.wait()
        self.store.start()

    def wait(self):
        self.store.wait()


class GatherNear:
    def __init__(self, a_ref, out_ref, y, x, send, recv, *local):
        to_x, to_y = {"x": 1 - x}, {"y": 1 - y}
        here = y * 2 + x
        parts = halves_at(a_ref.shape[0])

        def copy(part, n, peer):
            return remote(a_ref.at[parts[part]], out_ref.at[here, parts[part]], send.at[n], recv.at[n], peer)

        self.own = Stay(a_ref, out_ref.at[here], *local)
        self.first, self.second = [copy(0, 0, to_x), copy(1, 1, to_y)], [copy(1, 2, to_x), copy(0, 3, to_y)]
        self.all = self.first + self.second

    def start(self):
        for copy in self.all + [self.own]:
            copy.start()

    def wait(self):
        for copy in self.all:
            copy.wait()
        self.own.wait()


class GatherFar:
    def __init__(self, out_ref, y, x, send, recv):
        at_x, at_y = y * 2 + 1 - x, (1 - y) * 2 + x
        parts = halves_at(out_ref.shape[1])

        def copy(place, part, n, peer):
            block = out_ref.at[place, parts[part]]
            return remote(block, block, send.at[n], recv.at[n], peer)

        self.all = [copy(at_x, 0, 0, {"y": 1 - y}), copy(at_y, 1, 1, {"x": 1 - x})]

    def start(self):
        for copy in self.all:
            copy.start()

    def wait(self):
        for copy in self.all:
            copy.wait()


def halves_at(rows):
    return [pl.ds(0, rows // 2), pl.ds(rows // 2, rows // 2)]


class Gather:
    def __init__(self, a_ref, out_ref, y, x, send, recv, *local):
        self.near = GatherNear(a_ref, out_ref, y, x, send, recv, *local)
        self.far = GatherFar(out_ref, y, x, send.at[pl.ds(4, 2)], recv.at[pl.ds(4, 2)])

    def start(self):
        self.near.start()

    def wait(self):
        for copy, onward in zip(self.near.first, self.far.all):
            copy.wait_recv()
            onward.start()
        for copy in self.near.second + self.far.all:
            copy.wait_recv()
        for copy in self.near.all + self.far.all:
            copy.wait_send()
        self.near.own.wait()


class ReduceNear:
    def __init__(self, a_ref, out_ref, y, x, send, recv):
        parts = halves_at(a_ref.shape[1])
        self.all = []
        for i, (at_y, at_x) in enumerate(((1 - y, 1 - x), (y, x))):
            blocks = (at_y * 2 + 1 - x, (1 - y) * 2 + at_x)
            for part, peer in enumerate(({"x": 1 - x}, {"y": 1 - y})):
                n = 2 * part + i
                self.all.append(
                    remote(a_ref.at[blocks[part], parts[part]], out_ref.at[part, i], send.at[n], recv.at[n], peer)
                )

    def start(self):
        for copy in self.all:
            copy.start()

    def wait(self):
        for copy in self.all:
            copy.wait()


class ReduceFar:
    def __init__(self, a_ref, out_ref, y, x, send, recv):
        self.all = [
            remote(a_ref.at[n], out_ref.at[n], send.at[n], recv.at[n], peer)
            for n, peer in enumerate(({"y": 1 - y}, {"x": 1 - x}))
        ]

    def start(self):
        for copy in self.all:
            copy.start()

    def wait(self):
        for copy in self.all:
            copy.wait()


class Swap:
    def __init__(self, a_ref, out_ref, c, send, recv):
        self.copy = remote(a_ref, out_ref, send.at[0], recv.at[0], {"c": 1 - c})

    def start(self):
        self.copy.start()

    def wait(self):
        self.copy.wait()


class Moves:
    def __init__(self, kind, source, target, y, x, c, send, recv, *local):
        self.copies = []
        for i in range(4):
            peer, giver, slot = routes(kind, i, y, x, c)
            to_me, from_me = (
                (at["y"] == y) & (at["x"] == x) & (at["c"] == c) for at in (peer, giver)
            )
            self.copies.append((
                to_me, from_me,
                Stay(source(i), target(slot), *local),
                remote(source(i), target(slot), send.at[i], recv.at[slot], peer),
                Stay(source(i), target(i), *local),
                remote(source(i), target(i), send.at[i], recv.at[i], peer),
            ))

    def start(self):
        for to_me, _, _, there, _, _ in self.copies:
            pl.when(jnp.logical_not(to_me))(there.start)
        for to_me, _, here, _, _, _ in self.copies:
            pl.when(to_me)(here.start)

    def wait(self):
        for to_me, from_me, _, _, here, there in self.copies:
            pl.when(jnp.logical_not(to_me))(there.wait_send)
            pl.when(jnp.logical_not(from_me))(there.wait_recv)
            pl.when(from_me)(here.wait)


class Spread:
    def __init__(self, a_ref, out_ref, y, x, c, send, recv, *local):
        here, other = y * 2 + x, {"c": 1 - c}
        self.own = Stay(a_ref.at[:, here], out_ref.at[c, here], *local)
        self.across = [remote(a_ref.at[:, here], out_ref.at[c, here], send.at[0], recv.at[0], other)]
        self.sent = []
        for flip in (1, 2, 3):
            peer = {"y": lax.rem(y + flip // 2, 2), "x": lax.rem(x + flip % 2, 2)}
            chip = peer["y"] * 2 + peer["x"]
            self.sent.append(remote(a_ref.at[:, chip], out_ref.at[c, here], send.at[flip], recv.at[flip], peer))
            self.across.append(
                remote(out_ref.at[c, chip], out_ref.at[c, chip], send.at[3 + flip], recv.at[3 + flip], other)
            )

    def start(self):
        for copy in self.sent + [self.across[0], self.own]:
            copy.start()

    def wait(self):
        for copy, onward in zip(self.sent, self.across[1:]):
            copy.wait_recv()
            onward.start()
        for copy in self.across:
            copy.wait()
        for copy in self.sent:
            copy.wait_send()
        self.own.wait()


def move_scratch(kind, a):
    sems = swap_kernel_sems({"spread": 7, "copy_chips": 6}.get(kind, 4)) + [pltpu.SemaphoreType.DMA]
    if kind in ("copy_homes", "copy_chips", "gather_near", "keep"):
        block = a.shape
    elif kind == "spread":
        block = a.shape[:1] + a.shape[2:]
    else:
        block = a.shape[1:] if kind in ("to_homes", "from_homes", "columns") else (16, TILE)
    return sems + [pltpu.VMEM(block, a.dtype)]


def moved(kind, a):
    if kind == "spread":
        return jax.ShapeDtypeStruct((2, 4, a.shape[0]) + a.shape[2:], a.dtype)
    if kind == "reduce_near":
        return jax.ShapeDtypeStruct((2, 2, a.shape[1] // 2) + a.shape[2:], a.dtype)
    if kind in ("swap_core", "keep", "gather_far", "reduce_far"):
        return jax.ShapeDtypeStruct(a.shape, a.dtype)
    block = a.shape if kind in ("copy_homes", "copy_chips", "gather_near") else a.shape[1:]
    return jax.ShapeDtypeStruct((4,) + block, a.dtype)


def one_move(kind, a_ref, out_ref, y, x, c, *sems):
    if kind == "spread":
        return Spread(a_ref, out_ref, y, x, c, *sems)
    if kind == "copy_chips":
        return Gather(a_ref, out_ref, y, x, *sems)
    if kind == "gather_near":
        return GatherNear(a_ref, out_ref, y, x, *sems)
    if kind == "gather_far":
        return GatherFar(out_ref, y, x, *sems[:2])
    if kind in ("reduce_near", "reduce_far"):
        return (ReduceNear if kind == "reduce_near" else ReduceFar)(a_ref, out_ref, y, x, *sems[:2])
    if kind == "swap_core":
        return Swap(a_ref, out_ref, c, *sems[:2])
    if kind == "keep":
        return Stay(a_ref, out_ref, *sems[2:])

    def source(i):
        return a_ref if kind == "copy_homes" else a_ref.at[i]

    return Moves(kind, source, lambda slot: out_ref.at[slot], y, x, c, *sems)


def all_moves(kinds, sources, results, sems, y, x, c):
    return [one_move(kind, sources[n], results[n], y, x, c, *sems[4 * n:4 * n + 4]) for n, kind in enumerate(kinds)]


def compute_body(counts, kinds, grid, body, *refs):
    refs, parts = list(refs), []
    for count in counts:
        parts.append(refs[:count])
        refs = refs[count:]
    operands, sources, _, outs, results, scratch, sems = parts
    if kinds:
        y, x, c = (lax.axis_index(name) for name in ("y", "x", "c"))
        moves = all_moves(kinds, sources, results, sems, y, x, c)
        first, last = True, True
        for axis, size in enumerate(grid):
            first, last = first & (pl.program_id(axis) == 0), last & (pl.program_id(axis) == size - 1)

        def start():
            enter_plane(y, x, c)
            for one in moves:
                one.start()

        def finish():
            for one in moves:
                one.wait()

        pl.when(first)(start) if grid else start()
    body(*operands, *outs, *scratch)
    if kinds:
        pl.when(last)(finish) if grid else finish()


def compute(body, name, operands, in_specs, out_specs, out_shape, us, grid=(), scratch=(), moves=(), collective=None, after=()):
    any_place = pl.BlockSpec(memory_space=pl.ANY)
    kinds = tuple(kind for kind, _ in moves)
    sems = [sem for kind, a in moves for sem in move_scratch(kind, a)]
    counts = (len(operands), len(moves), len(after), len(out_shape), len(moves), len(scratch), len(sems))
    params = {"collective_id": collective, "has_side_effects": True} if moves else {}
    aliases = {len(operands) + n: len(out_shape) + n for n, kind in enumerate(kinds) if kind == "gather_far"}
    return pl.pallas_call(
        functools.partial(compute_body, counts, kinds, grid, body),
        name=name,
        grid=grid,
        in_specs=list(in_specs) + [any_place] * (len(moves) + len(after)),
        out_specs=list(out_specs) + [any_place] * len(moves),
        out_shape=list(out_shape) + [moved(kind, a) for kind, a in moves],
        scratch_shapes=list(scratch) + sems,
        input_output_aliases=aliases,
        compiler_params=pltpu.CompilerParams(vmem_limit_bytes=60 << 20, **params),
        cost_estimate=cost(us),
    )(*operands, *(a for _, a in moves), *after)


def move_kernel(kinds, waits, *refs):
    count = len(kinds)
    sources, results, sems = refs[:count], refs[count + waits:2 * count + waits], refs[2 * count + waits:]
    y, x, c = (lax.axis_index(name) for name in ("y", "x", "c"))
    enter_plane(y, x, c)
    moves = all_moves(kinds, sources, results, sems, y, x, c)
    for one in moves:
        one.start()
    for one in moves:
        one.wait()


def move(collective, *items, after=(), us=48):
    kinds = tuple(kind for kind, _ in items)
    any_place = pl.BlockSpec(memory_space=pl.ANY)
    return pl.pallas_call(
        functools.partial(move_kernel, kinds, len(after)),
        name=kinds[0],
        out_shape=[moved(kind, a) for kind, a in items],
        in_specs=[any_place] * (len(items) + len(after)),
        out_specs=[any_place] * len(items),
        scratch_shapes=[sem for kind, a in items for sem in move_scratch(kind, a)],
        compiler_params=pltpu.CompilerParams(collective_id=collective, has_side_effects=True),
        cost_estimate=cost(us),
    )(*(a for _, a in items), *after)


def start_kernel(kinds, planes, *refs):
    count = len(kinds)
    projections, rest_ref, sources = refs[:3], refs[3], refs[4:4 + count]
    results, m_ref, sems = refs[4 + count:4 + 2 * count], refs[4 + 2 * count], refs[5 + 2 * count:]
    y, x, c, z = (lax.axis_index(name) for name in ("y", "x", "c", "z"))
    up, down = lax.rem(z + 1, planes), lax.rem(z + planes - 1, planes)
    wide = DEPTH // 2
    enter_plane(y, x, c, [{"z": up}, {"z": down}])
    moves = all_moves(kinds, sources, results, sems, y, x, c)
    sems = sems[4 * count:]

    def part(n, source, columns):
        return Moves(
            "columns", source, lambda slot: m_ref.at[c, z, slot, :, columns], y, x, c, *sems[4 * n:4 * n + 4]
        )

    def columns_of(w_ref):
        return lambda i: w_ref.at[:, pl.ds(pl.multiple_of((2 * i + c) * wide, wide), wide)]

    parts = [part(n, columns_of(w_ref), pl.ds(n * wide, wide)) for n, w_ref in enumerate(projections)]
    parts.append(part(3, lambda i: rest_ref.at[i], pl.ds(3 * wide, TILE)))
    m_send, m_recv, core_send, core_recv = sems[16:]

    def block(step):
        return m_ref.at[c, lax.rem(z + planes - step, planes)]

    ring = [
        remote(block(step), block(step), m_send.at[step], m_recv.at[step], {"z": up}) for step in range(planes - 1)
    ]
    across = [
        remote(block(step), block(step), core_send.at[step], core_recv.at[step], {"c": 1 - c}) for step in range(planes)
    ]
    for one in parts:
        one.start()
    for one in parts:
        one.wait()
    ring[0].start()
    across[0].start()
    for one in moves:
        one.start()
    for step in range(planes - 1):
        ring[step].wait_recv()
        if step < planes - 2:
            ring[step + 1].start()
        across[step + 1].start()
    for one in moves:
        one.wait()
    for copy in across:
        copy.wait()
    for copy in ring:
        copy.wait_send()


def start_moves(collective, projections, rest, items):
    planes = lax.axis_size("z")
    kinds = tuple(kind for kind, _ in items)
    any_place = pl.BlockSpec(memory_space=pl.ANY)
    shapes = [moved(kind, a) for kind, a in items]
    shapes.append(jax.ShapeDtypeStruct((2, planes, 4, rest.shape[1], 3 * DEPTH // 2 + TILE), BF16))
    sems = [sem for kind, a in items for sem in move_scratch(kind, a)]
    part = jax.ShapeDtypeStruct((4, rest.shape[1], DEPTH // 2), BF16)
    sems += [sem for a in (part, part, part, rest) for sem in move_scratch("columns", a)]
    sems += swap_kernel_sems(planes) + swap_kernel_sems(planes)
    return pl.pallas_call(
        functools.partial(start_kernel, kinds, planes),
        name="start_moves",
        out_shape=shapes,
        in_specs=[any_place] * (len(items) + 4),
        out_specs=[any_place] * len(shapes),
        scratch_shapes=sems,
        compiler_params=pltpu.CompilerParams(collective_id=collective, has_side_effects=True),
        cost_estimate=cost(85),
    )(*projections, rest, *(a for _, a in items))


def reduce_kernel(a_ref, *refs):
    out_ref, got_ref, sum_ref, last_ref, send, recv = refs[-6:]
    y, x = lax.axis_index("y"), lax.axis_index("x")
    enter_pairs(y, x)
    half = out_ref.shape[0] // 2
    parts = [pl.ds(0, half), pl.ds(half, half)]
    places = [(1 - y, y), (1 - x, x)]
    peers = [{"x": 1 - x}, {"y": 1 - y}]

    def block(part, place, other):
        if part == 0:
            return place * 2 + (1 - x if other else x)
        return (1 - y if other else y) * 2 + place

    def copy(source, target, n, peer):
        return remote(source, target, send.at[n], recv.at[n], peer)

    first = [
        [copy(a_ref.at[block(part, places[part][i], True), parts[part]], got_ref.at[part, i], 2 * part + i, peers[part])
         for i in range(2)] for part in range(2)
    ]
    for i in range(2):
        for part in range(2):
            first[part][i].start()
    onward = [copy(sum_ref.at[part], last_ref.at[part], 4 + part, peers[1 - part]) for part in range(2)]

    def total(part, i):
        own = a_ref[block(part, places[part][i], False), parts[part], :]
        return own.astype(F32) + got_ref[part, i].astype(F32)

    for part in range(2):
        first[part][0].wait_recv()
        sum_ref[part] = total(part, 0).astype(BF16)
        onward[part].start()
    for part in range(2):
        first[part][1].wait_recv()
        out_ref[parts[part], :] = total(part, 1)
    for part in range(2):
        onward[part].wait_recv()
        out_ref[parts[part], :] += last_ref[part].astype(F32)
    for one in first[0] + first[1] + onward:
        one.wait_send()


def reduce_plane(collective, a, after=()):
    rows, features = a.shape[1:]
    half = (rows // 2, features)
    return pl.pallas_call(
        reduce_kernel,
        name="reduce_plane",
        out_shape=jax.ShapeDtypeStruct((rows, features), F32),
        in_specs=[pl.BlockSpec(memory_space=pltpu.VMEM)] + [pl.BlockSpec(memory_space=pl.ANY)] * len(after),
        out_specs=pl.BlockSpec(memory_space=pltpu.VMEM),
        scratch_shapes=[pltpu.VMEM((2, 2) + half, BF16), pltpu.VMEM((2,) + half, BF16), pltpu.VMEM((2,) + half, BF16)]
        + swap_kernel_sems(6),
        compiler_params=pltpu.CompilerParams(collective_id=collective, has_side_effects=True),
        cost_estimate=cost(38),
    )(a, *after)


def add_other(a, other):
    return (a.astype(F32) + other.astype(F32)).astype(BF16)


def halves_of(a, place, axis):
    here = lax.axis_index(axis)
    return [lax.dynamic_index_in_dim(a, at, place, keepdims=False) for at in (here, 1 - here)]


def dot(a, b, dims):
    return lax.dot_general(a, b, dims, preferred_element_type=F32)


def parts_of(a):
    high = a.astype(BF16)
    return high, (a - high.astype(F32)).astype(BF16)


def dot_parts(a, b, dims):
    return dot(a[0], b[0], dims) + (dot(a[1], b[0], dims) + dot(a[0], b[1], dims))


def dot_ones(ones, a):
    high = a.astype(BF16)
    rest = a - high.astype(F32)
    middle = rest.astype(BF16)
    low = (rest - middle.astype(F32)).astype(BF16)
    return dot(ones, high, NN) + (dot(ones, middle, NN) + dot(ones, low, NN))


def places():
    shape = (TILE, TILE)
    return lax.broadcasted_iota(jnp.int32, shape, 0), lax.broadcasted_iota(jnp.int32, shape, 1)


def ones_where(mask):
    return jnp.where(mask, 1.0, 0.0).astype(BF16)


def steps_to_middle(half):
    t, s = places()
    block = 2 * half
    same = (t // block) == (s // block)
    t_right, s_right = (t % block) >= half, (s % block) >= half
    right = t_right & s_right & (s <= t)
    left = jnp.logical_not(t_right | s_right) & (s > t)
    return ones_where(same & (right | left))


def pair_mask(half, turned=False):
    t, s = places()
    if turned:
        t, s = s, t
    block = 2 * half
    return ((t // block) == (s // block)) & ((t % block) >= half) & ((s % block) < half)


def first_row(rows):
    return lax.broadcasted_iota(jnp.int32, (rows, 2 * SLOTS), 1) < SLOTS


def row_sums(a, first):
    return (
        jnp.sum(jnp.where(first, a, 0.0), axis=1, keepdims=True),
        jnp.sum(jnp.where(first, 0.0, a), axis=1, keepdims=True),
    )


def tile_rows(j):
    return pl.ds(pl.multiple_of(j * TILE, TILE), TILE)


def prepare(lf_ref, decay_ref, reach_ref, e_ref, tiles):
    t, s = places()

    @pl.loop(0, tiles)
    def _(j):
        rows = tile_rows(j)
        lf = lf_ref[rows, :]
        decay_ref[rows, :] = dot_ones(ones_where(s <= t), lf)
        reach_ref[rows, :] = dot_ones(ones_where(s > t), lf)
        for level, half in enumerate(HALVES):
            e_ref[level, rows, :] = jnp.exp(dot_ones(steps_to_middle(half), lf))


def far_pairs(tiles):
    out, half = [], tiles // 2
    while half >= 1:
        for start in range(0, tiles, 2 * half):
            out.append((start + half, start, half))
        half //= 2
    return out


def far_decays(right, left, half, decay_ref, reach_ref):
    after, total = [], None
    for j in range(right, right + half):
        part = decay_ref[j * TILE:(j + 1) * TILE, :]
        after.append(jnp.exp(part if total is None else part + total))
        last = part[TILE - 1:TILE, :]
        total = last if total is None else total + last
    before, total = [], None
    for j in range(left + half - 1, left - 1, -1):
        part = reach_ref[j * TILE:(j + 1) * TILE, :]
        before.append(jnp.exp(part if total is None else part + total))
        whole = decay_ref[(j + 1) * TILE - 1:(j + 1) * TILE, :]
        total = whole if total is None else total + whole
    if half == 1:
        return after[0], before[0]
    return jnp.concatenate(after, axis=0), jnp.concatenate(before[::-1], axis=0)


def diagonal_of(block):
    t, s = places()
    return jnp.sum(jnp.where(t == s, block, 0.0), axis=1, keepdims=True)


def weighted_sums(a_ref, out_ref, gain_ref, decay_ref, reach_ref, e_ref, tiles):
    first = first_row(TILE)

    @pl.loop(0, tiles)
    def _(j):
        rows = tile_rows(j)
        gain = gain_ref[rows, :]
        blocks = [a_ref[r, rows, rows] for r in range(2)]
        total = jnp.where(first, diagonal_of(blocks[0]), diagonal_of(blocks[1])) * gain
        for level, half in enumerate(HALVES):
            e = e_ref[level, rows, :]
            x = parts_of(e * gain)
            pairs = pair_mask(half)
            y = [dot_parts(parts_of(jnp.where(pairs, a, 0.0)), x, NN) for a in blocks]
            total = total + e * jnp.where(first, y[0], y[1])
        out_ref[rows, :] = total

    for right, left, half in far_pairs(tiles):
        after, before = far_decays(right, left, half, decay_ref, reach_ref)
        here = slice(right * TILE, (right + half) * TILE)
        there = slice(left * TILE, (left + half) * TILE)
        x = parts_of(before * gain_ref[there, :])
        y = [dot_parts(parts_of(a_ref[r, here, there]), x, NN) for r in range(2)]
        out_ref[here, :] += after * jnp.where(first_row(half * TILE), y[0], y[1])


def split_rows(a, first):
    return parts_of(jnp.where(first, a, 0.0)), parts_of(jnp.where(first, 0.0, a))


def paired_weights(p_ref, out_ref, gain_ref, decay_ref, reach_ref, e_ref, tiles):
    first = first_row(TILE)
    t, s = places()

    @pl.loop(0, tiles)
    def _(j):
        rows = tile_rows(j)
        gain, p = gain_ref[rows, :], p_ref[rows, :]
        sums = row_sums(p * gain, first)
        total = [jnp.where(t == s, sums[r], 0.0) for r in range(2)]
        for level, half in enumerate(HALVES):
            e = e_ref[level, rows, :]
            x = parts_of(e * gain)
            pairs = pair_mask(half)
            pe = split_rows(p * e, first)
            total = [total[r] + jnp.where(pairs, dot_parts(pe[r], x, NT), 0.0) for r in range(2)]
        for r in range(2):
            out_ref[r, rows, rows] = total[r]

    for right, left, half in far_pairs(tiles):
        after, before = far_decays(right, left, half, decay_ref, reach_ref)
        here = slice(right * TILE, (right + half) * TILE)
        there = slice(left * TILE, (left + half) * TILE)
        x = parts_of(before * gain_ref[there, :])
        pe = split_rows(p_ref[here, :] * after, first_row(half * TILE))
        for r in range(2):
            out_ref[r, here, there] = dot_parts(pe[r], x, NT)
            out_ref[r, there, here] = jnp.zeros((half * TILE, half * TILE), F32)


def inner(a, b, r):
    return dot(a[0][r], b[0][r], NT) + dot(a[1][r], b[1][r], NT)


def sigmoid(v):
    return 1.0 / (1.0 + jnp.exp(-v))


def projections(pre_ref, which, length, act):
    depth = DEPTH // 2
    return [
        [act(pre_ref[f, r * length:(r + 1) * length, which * depth:(which + 1) * depth]) for r in range(2)]
        for f in range(2)
    ]


def silu_low(v):
    return (v * sigmoid(v)).astype(BF16)


def low(v):
    return v.astype(BF16)


def forward_kernel(pre_ref, lf_ref, gain_ref, dcol_ref, drow_ref,
                   mixed_ref, s_ref, p_ref, b_ref, a_ref, decay_ref, reach_ref, e_ref):
    length = lf_ref.shape[0]
    tiles = length // TILE
    scale = DEPTH ** -0.5
    q, k = projections(pre_ref, 0, length, silu_low), projections(pre_ref, 1, length, silu_low)
    for r in range(2):
        same = dcol_ref[r] == drow_ref[r]
        a_ref[r] = jnp.where(same, inner(q, k, r), 0.0)
    prepare(lf_ref, decay_ref, reach_ref, e_ref, tiles)
    weighted_sums(a_ref, s_ref, gain_ref, decay_ref, reach_ref, e_ref, tiles)
    first = first_row(length)
    logits = s_ref[...] * scale
    least = -jnp.inf
    top = jnp.where(
        first,
        jnp.max(jnp.where(first, logits, least), axis=1, keepdims=True),
        jnp.max(jnp.where(first, least, logits), axis=1, keepdims=True),
    )
    grown = jnp.exp(logits - top)
    sums = row_sums(grown, first)
    p_ref[...] = grown / jnp.where(first, sums[0], sums[1])
    paired_weights(p_ref, b_ref, gain_ref, decay_ref, reach_ref, e_ref, tiles)
    v = projections(pre_ref, 2, length, low)
    for r in range(2):
        b = jnp.where(dcol_ref[r] == drow_ref[r], b_ref[r], 0.0)
        b_ref[r] = b
        high, rest = parts_of(b)
        for f in range(2):
            mixed = (dot(high, v[f][r], NN) + dot(rest, v[f][r], NN)).astype(BF16)
            for place in range(2):
                mixed_ref[r, place, f] = mixed[place * length // 2:(place + 1) * length // 2]


def to_columns(r, f):
    t, s = places()
    half = SLOTS // 2
    return ones_where((s < half) & (t == s + r * SLOTS + f * half))


def backward_kernel(pre_ref, g_ref, lf_ref, gain_ref, rate_ref, dcol_ref, drow_ref, s_ref, p_ref, b_ref,
                    out_ref, bias_ref, a_ref, at_ref, dot_ref, h_ref, back_ref, decay_ref, reach_ref, e_ref):
    length = lf_ref.shape[0]
    tiles, depth = length // TILE, DEPTH // 2
    scale = DEPTH ** -0.5
    first_all, first = first_row(length), first_row(TILE)
    t, s = places()
    q, k = projections(pre_ref, 0, length, silu_low), projections(pre_ref, 1, length, silu_low)
    v = projections(pre_ref, 2, length, low)
    grads = [[g_ref[r, :, f].reshape(length, depth) for r in range(2)] for f in range(2)]
    for r in range(2):
        same = dcol_ref[r] == drow_ref[r]
        a_ref[r] = jnp.where(same, inner(grads, v, r), 0.0)
        at_ref[0, r] = jnp.where(same, inner(k, q, r), 0.0)
        at_ref[1, r] = jnp.where(same, inner(v, grads, r), 0.0)
    prepare(lf_ref, decay_ref, reach_ref, e_ref, tiles)
    weighted_sums(a_ref, dot_ref, gain_ref, decay_ref, reach_ref, e_ref, tiles)
    p, dots = p_ref[...], dot_ref[...]
    sums = row_sums(p * dots, first_all)
    h = scale * (p * (dots - jnp.where(first_all, sums[0], sums[1])))
    h_ref[...] = h
    dot_ref[...] = h * s_ref[...] + p * dots
    paired_weights(h_ref, a_ref, gain_ref, decay_ref, reach_ref, e_ref, tiles)
    @pl.loop(0, tiles)
    def _(j):
        rows = tile_rows(j)
        h, p = h_ref[rows, :], p_ref[rows, :]
        keys = [at_ref[0, r, rows, rows] for r in range(2)]
        values = [at_ref[1, r, rows, rows] for r in range(2)]
        total = (
            jnp.where(first, diagonal_of(keys[0]), diagonal_of(keys[1])) * h
            + jnp.where(first, diagonal_of(values[0]), diagonal_of(values[1])) * p
        )
        for level, half in enumerate(HALVES):
            e = e_ref[level, rows, :]
            he, pe = parts_of(h * e), parts_of(p * e)
            pairs = pair_mask(half, turned=True)
            y = [
                dot_parts(parts_of(jnp.where(pairs, keys[r], 0.0)), he, NN)
                + dot_parts(parts_of(jnp.where(pairs, values[r], 0.0)), pe, NN)
                for r in range(2)
            ]
            total = total + e * jnp.where(first, y[0], y[1])
        back_ref[rows, :] = total

    for right, left, half in far_pairs(tiles):
        after, before = far_decays(right, left, half, decay_ref, reach_ref)
        here = slice(right * TILE, (right + half) * TILE)
        there = slice(left * TILE, (left + half) * TILE)
        he, pe = parts_of(h_ref[here, :] * after), parts_of(p_ref[here, :] * after)
        y = [
            dot_parts(parts_of(at_ref[0, r, there, here]), he, NN)
            + dot_parts(parts_of(at_ref[1, r, there, here]), pe, NN)
            for r in range(2)
        ]
        back_ref[there, :] += before * jnp.where(first_row(half * TILE), y[0], y[1])

    for r in range(2):
        rows = slice(r * length, (r + 1) * length)
        c = parts_of(jnp.where(dcol_ref[r] == drow_ref[r], a_ref[r], 0.0))
        w = parts_of(b_ref[r])
        for f in range(2):
            gq = dot(c[0], k[f][r], NN) + dot(c[1], k[f][r], NN)
            out_ref[f, rows, :depth] = (gq * slope(pre_ref[f, rows, :depth])).astype(BF16)
            gk = dot(c[0], q[f][r], TN) + dot(c[1], q[f][r], TN)
            out_ref[f, rows, depth:2 * depth] = (gk * slope(pre_ref[f, rows, depth:2 * depth])).astype(BF16)
            gv = dot(w[0], grads[f][r], TN) + dot(w[1], grads[f][r], TN)
            out_ref[f, rows, 2 * depth:3 * depth] = gv.astype(BF16)
    carried = jnp.zeros((1, 2 * SLOTS), F32)
    for j in range(tiles - 1, -1, -1):
        rows = slice(j * TILE, (j + 1) * TILE)
        back = back_ref[rows, :]
        change = dot_ref[rows, :] - gain_ref[rows, :] * back
        upward = dot_ones(ones_where(s >= t), change) + carried
        h_ref[rows, :] = (upward - jnp.exp(lf_ref[rows, :]) * back) * rate_ref[rows, :]
        carried = upward[0:1, :]
    grad_z = h_ref[...]
    bias_ref[...] = jnp.broadcast_to(jnp.sum(grad_z, axis=0, keepdims=True), bias_ref.shape)
    for r in range(2):
        for f in range(2):
            out_ref[f, r * length:(r + 1) * length, 3 * depth:] = dot(grad_z.astype(BF16), to_columns(r, f), NN).astype(BF16)


def slope(v):
    s = sigmoid(v)
    return s * (1.0 + v * (1.0 - s))


def mix_forward(pre, lf, gain, doc, moves, collective):
    length = lf.shape[0]
    lanes = (length, 2 * SLOTS)
    square = (2, length, length)
    in_vmem = pl.BlockSpec(memory_space=pltpu.VMEM)
    return compute(
        forward_kernel, "mix_forward", (pre, lf, gain, doc[:, :, None], doc[:, None, :]), [in_vmem] * 5, [in_vmem] * 4,
        (
            jax.ShapeDtypeStruct((2, 2, 2, length // 2, DEPTH // 2), BF16), jax.ShapeDtypeStruct(lanes, F32),
            jax.ShapeDtypeStruct(lanes, F32), jax.ShapeDtypeStruct(square, F32),
        ),
        24, scratch=[
            pltpu.VMEM(square, F32), pltpu.VMEM(lanes, F32), pltpu.VMEM(lanes, F32),
            pltpu.VMEM((len(HALVES),) + lanes, F32),
        ],
        moves=moves, collective=collective,
    )


def mix_backward(pre, g, lf, gain, rate, doc, s, p, b, moves, collective):
    length = lf.shape[0]
    lanes = (length, 2 * SLOTS)
    square = (2, length, length)
    in_vmem = pl.BlockSpec(memory_space=pltpu.VMEM)
    return compute(
        backward_kernel, "mix_backward", (pre, g, lf, gain, rate, doc[:, :, None], doc[:, None, :], s, p, b),
        [in_vmem] * 10, [in_vmem] * 2,
        (jax.ShapeDtypeStruct(pre.shape, BF16), jax.ShapeDtypeStruct((8, 2 * SLOTS), F32)), 30,
        scratch=[pltpu.VMEM(square, F32), pltpu.VMEM((2,) + square, F32)] + [pltpu.VMEM(lanes, F32)] * 5
        + [pltpu.VMEM((len(HALVES),) + lanes, F32)],
        moves=moves, collective=collective,
    )


def hidden_kernel(nf_ref, w_ref, hidden_ref, slope_ref, silu_ref):
    units = hidden_ref.shape[2]
    both = dot(nf_ref[...], w_ref[0], NN)
    gate, up = both[:, :units], both[:, units:]
    s = sigmoid(gate)
    silu = gate * s
    hidden_ref[0] = (silu * up).astype(BF16)
    slope_ref[0] = (up * (s * (1.0 + gate * (1.0 - s)))).astype(BF16)
    silu_ref[0] = silu.astype(BF16)


def unit_specs(tokens, features, units):
    rows = tokens // 2
    return (
        pl.BlockSpec((rows, features), lambda h, t: (t, 0)),
        pl.BlockSpec((1, features, 2 * units), lambda h, t: (h, 0, 0)),
        pl.BlockSpec((1, rows, units), lambda h, t: (h, t, 0)),
        jax.ShapeDtypeStruct((2, tokens, units), BF16),
    )


def hidden_units(nf, w, moves, collective):
    some, weight, unit, units_all = unit_specs(*nf.shape, w.shape[2] // 2)
    return compute(
        hidden_kernel, "hidden_units", (nf, w), [some, weight], [unit] * 3, [units_all] * 3, 22, grid=(2, 2),
        moves=moves, collective=collective,
    )


def hidden_grads_kernel(cot_ref, slope_ref, silu_ref, w_ref, wd_ref, grads_ref, back_ref, total_ref):
    half, tile = pl.program_id(0), pl.program_id(1)
    rows = cot_ref.shape[0]
    here = pl.ds(pl.multiple_of(tile * rows, rows), rows)
    grad = dot(cot_ref[...], wd_ref[0], NT)
    gate_up = [grad * slope_ref[0].astype(F32), grad * silu_ref[0].astype(F32)]
    grads = jnp.concatenate(gate_up, axis=1).astype(BF16)
    grads_ref[0] = grads
    back = dot(grads, w_ref[0], NT)

    @pl.when(half == 0)
    def _():
        total_ref[here, :] = back

    @pl.when(half == 1)
    def _():
        back_ref[...] = (total_ref[here, :] + back).astype(BF16)


def hidden_grads(cot, slopes, silus, w, wd, moves, collective):
    tokens, features = cot.shape
    units = slopes.shape[2]
    some, weight, unit, _ = unit_specs(tokens, features, units)
    return compute(
        hidden_grads_kernel, "hidden_grads", (cot, slopes, silus, w, wd),
        [some, unit, unit, weight, pl.BlockSpec((1, units, features), lambda h, t: (h, 0, 0))],
        [
            pl.BlockSpec((1, tokens // 2, 2 * units), lambda h, t: (h, t, 0)),
            pl.BlockSpec((tokens // 2, features), lambda h, t: (h * t, 0)),
        ],
        [jax.ShapeDtypeStruct((2, tokens, 2 * units), BF16), jax.ShapeDtypeStruct(cot.shape, BF16)],
        45, grid=(2, 2), scratch=[pltpu.VMEM((tokens, features), F32)], moves=moves, collective=collective,
    )


def out_kernel(a_ref, b_ref, out_ref):
    grads = dot(a_ref[...], b_ref[0], TN).astype(BF16)
    wide = grads.shape[1] // 2
    for f in range(2):
        out_ref[0, f] = grads[:, f * wide:(f + 1) * wide]


def out_grads(a, b):
    planes = lax.axis_size("z")
    tokens, depth = a.shape
    features = b.shape[2]
    rows = max(depth // planes, TILE)
    grads = pl.pallas_call(
        out_kernel,
        name="out_grads",
        grid=(depth // rows,),
        in_specs=[
            pl.BlockSpec((tokens, rows), lambda i: (0, i)), pl.BlockSpec((1, tokens, features), lambda i: (0, 0, 0)),
        ],
        out_specs=pl.BlockSpec((1, 2, rows, features // 2), lambda i: (i, 0, 0, 0)),
        out_shape=jax.ShapeDtypeStruct((depth // rows, 2, rows, features // 2), BF16),
        compiler_params=pltpu.CompilerParams(vmem_limit_bytes=60 << 20),
        cost_estimate=cost(8),
    )(a, b)
    if rows * planes > depth:
        grads = grads.reshape(-1, 2, rows * planes // depth, depth // planes, features // 2).transpose(0, 2, 1, 3, 4)
    return grads.reshape(planes, 2, depth // planes, features // 2)


def weight_kernel(a_ref, b_ref, out_ref):
    out_ref[0, 0] = dot(a_ref[...], b_ref[0], TN).astype(BF16)


def weight_sums_kernel(a_ref, b_ref, sums_ref, out_ref):
    grads = dot(a_ref[...], b_ref[0], TN)
    wide = grads.shape[1]
    out_ref[0, 0, :, :wide - TILE] = grads[:, :wide - TILE].astype(BF16)
    once = jnp.where(pl.program_id(0) == 0, 1.0, 0.0)
    out_ref[0, 0, :, wide - TILE:] = (grads[:, wide - TILE:] + once * sums_ref[...]).astype(BF16)


def weight_grads(a, b, us, sums=None, moves=(), collective=None, after=()):
    planes = lax.axis_size("z")
    tokens, features = a.shape
    rows, columns = features // planes, b.shape[2]
    specs = [pl.BlockSpec((tokens, rows), lambda h, z: (0, z)), pl.BlockSpec((1, tokens, columns), lambda h, z: (h, 0, 0))]
    body, operands = weight_kernel, (a, b)
    if sums is not None:
        body, operands = weight_sums_kernel, (a, b, sums)
        specs.append(pl.BlockSpec((rows, TILE), lambda h, z: (z, 0)))
    out = compute(
        body, "weight_grads", operands, specs, [pl.BlockSpec((1, 1, rows, columns), lambda h, z: (z, h, 0, 0))],
        [jax.ShapeDtypeStruct((planes, 2, rows, columns), BF16)], us, grid=(2, planes),
        moves=moves, collective=collective, after=after,
    )
    return out if moves else out[0]


def down_kernel(hidden_ref, cot_ref, out_ref):
    grads = dot(hidden_ref[0], cot_ref[...], TN)
    rows = out_ref.shape[2]
    for z in range(out_ref.shape[0]):
        out_ref[z, 0] = grads[z * rows:(z + 1) * rows].astype(BF16)


def down_grads(hidden, cot):
    planes = lax.axis_size("z")
    tokens, features = cot.shape
    units = hidden.shape[2]
    wide = features // 2
    return pl.pallas_call(
        down_kernel,
        name="down_grads",
        grid=(2, 2),
        in_specs=[
            pl.BlockSpec((1, tokens, units), lambda h, i: (h, 0, 0)),
            pl.BlockSpec((tokens, wide), lambda h, i: (0, i)),
        ],
        out_specs=pl.BlockSpec((planes, 1, units // planes, wide), lambda h, i: (0, h, 0, i)),
        out_shape=jax.ShapeDtypeStruct((planes, 2, units // planes, features), BF16),
        compiler_params=pltpu.CompilerParams(vmem_limit_bytes=60 << 20),
        cost_estimate=cost(12),
    )(hidden, cot)


def input_kernel(grad_ref, w_ref, x_ref, out_ref, sums_ref):
    tile = pl.program_id(0)
    back = dot(grad_ref[0], w_ref[0], NT) + dot(grad_ref[1], w_ref[1], NT)
    out_ref[...] = back.astype(BF16)
    x = x_ref[...].astype(F32)
    xh = x * lax.rsqrt(jnp.mean(x * x, axis=1, keepdims=True) + EPSILON)
    sums = jnp.sum((back * xh).reshape(-1, 8, back.shape[1]), axis=0)
    sums_ref[...] = jnp.where(tile == 0, sums, sums_ref[...] + sums)


def input_grads(grad, w, x, moves, collective, after):
    tokens, features = x.shape
    rows = tokens // 4
    return compute(
        input_kernel, "input_grads", (grad, w, x),
        [
            pl.BlockSpec((2, rows, grad.shape[2]), lambda t: (0, t, 0)), pl.BlockSpec(w.shape, lambda t: (0, 0, 0)),
            pl.BlockSpec((rows, features), lambda t: (t, 0)),
        ],
        [pl.BlockSpec((rows, features), lambda t: (t, 0)), pl.BlockSpec((8, features), lambda t: (0, 0))],
        [jax.ShapeDtypeStruct(x.shape, BF16), jax.ShapeDtypeStruct((8, features), F32)],
        20, grid=(4,), moves=moves, collective=collective, after=after,
    )


def project_kernel(x_ref, gain_ref, w_ref, normed_ref, pre_ref):
    x = x_ref[...].astype(F32)
    ratio = lax.rsqrt(jnp.mean(x * x, axis=1, keepdims=True) + EPSILON)
    normed = (x * ratio * gain_ref[...]).astype(BF16)
    normed_ref[...] = normed
    for f in range(2):
        pre_ref[f] = dot(normed, w_ref[f], NN)


def project(x, gain, w, moves, collective):
    tokens, features = x.shape
    rows, columns = tokens // 4, w.shape[2]
    some = pl.BlockSpec((rows, features), lambda t: (t, 0))
    return compute(
        project_kernel, "project", (x, gain, w),
        [some, pl.BlockSpec((1, features), lambda t: (0, 0)), pl.BlockSpec(w.shape, lambda t: (0, 0, 0))],
        [some, pl.BlockSpec((2, rows, columns), lambda t: (0, t, 0))],
        [jax.ShapeDtypeStruct(x.shape, BF16), jax.ShapeDtypeStruct((2, tokens, columns), F32)],
        28, grid=(4,), moves=moves, collective=collective,
    )


def gather_planes(a):
    return lax.all_gather(a, ("c", "z"), axis=0, tiled=True).reshape((2, -1) + a.shape[1:])


def sum_planes(a):
    return lax.psum_scatter(a.reshape((-1,) + a.shape[2:]), ("z", "c"), scatter_dimension=0, tiled=True)[0]


def swap(a, axis):
    return lax.ppermute(a, axis, [(0, 1), (1, 0)])


def both_of(a, axis):
    other = swap(a, axis)
    return jnp.where(lax.axis_index(axis) == 0, jnp.stack([a, other]), jnp.stack([other, a]))


def scaled(features):
    return lax.rsqrt(jnp.mean(features * features, axis=-1, keepdims=True) + EPSILON)


def norm_back(grad, gain, features, ratio):
    u, xh = grad * gain, features * ratio
    return ratio * (u - xh * jnp.mean(u * xh, axis=-1, keepdims=True))


def body(inputs, starts, norm_attn, w_query, w_key, w_value, w_forget, gate_bias, w_out, norm_ffn, w_gate, w_up,
         w_down, cotangent):
    positions, features = inputs.shape[1:]
    depth = features // HEADS
    y, x, c, z = (lax.axis_index(name) for name in ("y", "x", "c", "z"))
    planes = lax.axis_size("z")
    head = y * 2 + x
    rows_here = w_query.shape[0]
    hidden_here = w_down.shape[0]

    def own_half(a, axis, at=c):
        return lax.dynamic_index_in_dim(a, at, axis, keepdims=False)

    bias_here = gate_bias.shape[0]

    def column(v):
        v = jnp.pad(v, (0, rows_here - v.shape[0]))
        return jnp.broadcast_to(v[None, :, None], (HEADS, rows_here, 1))

    forget = own_half(w_forget.reshape(rows_here, HEADS, 2, SLOTS // 2), 2).transpose(1, 0, 2)
    rest = jnp.concatenate([forget] + [column(v) for v in (norm_attn, norm_ffn, gate_bias)], axis=-1)
    rest = jnp.pad(rest, ((0, 0), (0, 0), (0, TILE - rest.shape[-1])))
    vectors = 3 * depth // 2 + SLOTS // 2
    width = vectors + 3

    def hidden_columns(w):
        w = own_half(w.reshape(rows_here, planes, 4, 2, hidden_here // 2), 3)
        return w.transpose(2, 0, 1, 3).reshape(4, rows_here, -1)

    x_here = inputs.reshape(positions, features)
    cot_here = cotangent.reshape(positions, features)
    out_half = own_half(w_out.reshape(2, rows_here // 2, features), 0)
    out_half = lax.all_gather(out_half, "z", axis=0)
    full_down = gather_planes(own_half(w_down.reshape(2, hidden_here // 2, features), 0))
    begins, x_rows, hidden_w, mixer_w = start_moves(1, (w_query, w_key, w_value), rest, (
        ("copy_homes", jnp.broadcast_to(starts, (8, positions))), ("copy_homes", x_here),
        ("columns", jnp.concatenate([hidden_columns(w_gate), hidden_columns(w_up)], axis=-1)),
    ))
    hidden_w = gather_planes(hidden_w.reshape(4 * rows_here, -1))
    mixer_w = mixer_w.reshape(2, features, -1)
    gain_attn, gain_ffn = (mixer_w[0, :, vectors + i].astype(F32) for i in range(2))
    bias = mixer_w[0, :, vectors + 2].reshape(4 * planes, rows_here)[:, :bias_here].reshape(-1).astype(F32)
    bias = lax.dynamic_slice_in_dim(bias, head * SLOTS, SLOTS)
    doc = jnp.cumsum(begins[:, 0].reshape(2, 2 * positions).astype(F32), axis=1)

    x_rows = x_rows.reshape(4 * positions, features)
    normed, pre, out_core = project(x_rows, gain_attn[None], mixer_w, [("copy_chips", out_half)], 13)
    z_total = pre[:, :, 3 * depth // 2:vectors].reshape(2, 2, 2 * positions, SLOTS // 2)
    z_total = z_total.transpose(2, 1, 0, 3).reshape(2 * positions, 2 * SLOTS) + jnp.tile(bias, 2)
    log_forget = jax.nn.log_sigmoid(z_total) / 8.0
    gain = -jnp.expm1(log_forget)
    mixed, scores, probs, paired, out_other, cot = mix_forward(
        pre, log_forget, gain, doc, [("swap_core", out_core), ("gather_near", cot_here)], 3
    )
    out_core, out_other = (a.reshape(features // 2, features) for a in (out_core, out_other))
    other = swap(own_half(mixed, 1, 1 - c), "c")
    own = own_half(mixed, 1)
    mixed_chips = jnp.where(c == 0, jnp.stack([own, other]), jnp.stack([other, own]))
    mixed_chips = mixed_chips.transpose(0, 1, 3, 2, 4).reshape(4 * positions, depth)
    (mixed,) = move(4, ("to_homes", mixed.reshape(4, 2 * positions, depth // 2)), us=14)
    mixed = mixed.reshape(2 * HEADS, positions, depth // 2).transpose(1, 0, 2)
    mixed = mixed.reshape(positions, planes, 4, 2, rows_here // 2).transpose(3, 0, 2, 1, 4)
    mixed = mixed.reshape(2, positions, features // 2)
    attended = (
        x_here.astype(F32) + jnp.dot(own_half(mixed, 0), out_core, preferred_element_type=F32)
        + jnp.dot(own_half(mixed, 0, 1 - c), out_other, preferred_element_type=F32)
    )

    ratio_f = scaled(attended)
    (normed_ffn,) = move(5, ("copy_chips", (attended * ratio_f * gain_ffn).astype(BF16)), us=38)
    normed_ffn = normed_ffn.reshape(4 * positions, features)
    hidden, slopes, silus, cot = hidden_units(normed_ffn, hidden_w, [("gather_far", cot)], 6)
    cot = cot.reshape(4 * positions, features)
    grad_down_w = down_grads(hidden, cot)
    block_out = jnp.einsum("ctf,cfd->td", hidden, full_down, preferred_element_type=F32).astype(BF16)
    block_out = block_out.reshape(2, 2, positions, features)
    grad_hidden, grad_normed_ffn, near = hidden_grads(
        cot, slopes, silus, hidden_w, full_down, [("reduce_near", block_out.reshape(4, positions, features))], 7
    )
    half = positions // 2
    own = [
        lax.dynamic_index_in_dim(block_out[:, :, :half], x, 1, keepdims=False),
        lax.dynamic_index_in_dim(block_out[:, :, half:], y, 0, keepdims=False),
    ]
    own = [jnp.where(at == 0, a[::-1], a) for at, a in zip((y, x), own)]
    near = jnp.stack(own).astype(F32) + near.astype(F32)
    grad_hidden_w, far = weight_grads(
        normed_ffn, grad_hidden, 22, moves=[("reduce_far", near[:, 0].astype(BF16))], collective=15
    )
    block_out = (near[:, 1] + far.astype(F32)).reshape(positions, features)
    output = (attended + block_out).astype(BF16)
    grad_normed_ffn = reduce_plane(
        8, grad_normed_ffn.reshape(4, positions, features), after=(grad_down_w, grad_hidden_w)
    )
    grad_down_w, grad_hidden_w = sum_planes(grad_down_w), sum_planes(grad_hidden_w)
    grad_gain_ffn = jnp.sum(grad_normed_ffn * attended * ratio_f, axis=0)
    grad_attended = cot_here.astype(F32) + norm_back(grad_normed_ffn, gain_ffn, attended, ratio_f)

    grad_branch = grad_attended.astype(BF16)
    grad_mixed = [
        jnp.einsum("te,de->td", grad_branch, w, preferred_element_type=F32).astype(BF16) for w in (out_core, out_other)
    ]
    grad_mixed = jnp.where(c == 0, jnp.stack(grad_mixed), jnp.stack(grad_mixed[::-1]))
    grad_mixed = grad_mixed.reshape(2, positions, 4, planes, rows_here // 2).transpose(1, 3, 2, 0, 4)
    grad_mixed = grad_mixed.reshape(positions, HEADS, 2, depth // 2).transpose(1, 2, 0, 3)
    (grad_mixed,) = move(
        9, ("from_homes", grad_mixed.reshape(4, 2 * positions, depth // 2)), after=(grad_down_w,), us=14
    )
    grad_mixed = grad_mixed.reshape(2, 2, 2, positions, depth // 2)
    rate = jax.nn.sigmoid(-z_total) / 8.0
    grad_pre, grad_bias, branch_chips = mix_backward(
        pre, grad_mixed, log_forget, gain, rate, doc, scores, probs, paired, [("copy_chips", grad_branch)], 10
    )
    grad_bias = jnp.sum(grad_bias[0].reshape(2, SLOTS), axis=0)
    grad_out_w = out_grads(mixed_chips, branch_chips.reshape(1, 4 * positions, features))
    grad_normed, sums, grad_hidden_w = input_grads(
        grad_pre, mixer_w, x_rows, [("spread", grad_hidden_w.reshape(1, 4, rows_here, -1))], 14, (grad_out_w,)
    )
    grad_bias = jnp.zeros((HEADS, SLOTS), F32).at[head].set(grad_bias).reshape(4 * planes, bias_here)
    grad_bias = jnp.pad(grad_bias, ((0, 0), (0, rows_here - bias_here))).reshape(-1)
    sums = jnp.stack([jnp.sum(sums, axis=0), grad_gain_ffn, grad_bias], axis=-1)
    first_sum = vectors + TILE - mixer_w.shape[-1]
    sums = jnp.pad(sums, ((0, 0), (first_sum, TILE - first_sum - 3)))
    grad_mixer_w = weight_grads(normed, grad_pre, 15, sums=sums)
    grad_out_w = sum_planes(grad_out_w)
    grad_normed, grad_out_w = move(
        11, ("to_homes", grad_normed.reshape(4, positions, features)), ("keep", grad_out_w), after=(grad_mixer_w,), us=48
    )
    grad_mixer_w = sum_planes(grad_mixer_w)
    grad_normed_here = jnp.sum(grad_normed.astype(F32), axis=0)
    x_here = x_here.astype(F32)
    ratio_a = scaled(x_here)
    grad_input = grad_attended + norm_back(grad_normed_here, gain_attn, x_here, ratio_a)

    grad_hidden_w = grad_hidden_w.reshape(2, 4, rows_here, 2, planes, hidden_here // 2)
    grad_hidden_w = grad_hidden_w.transpose(3, 2, 4, 1, 0, 5).reshape(2, rows_here, -1)
    grad_gate_w, grad_up_w = grad_hidden_w[0].astype(F32), grad_hidden_w[1].astype(F32)
    blocks = 4 * planes
    grad_out_w = lax.ppermute(
        grad_out_w, ("z", "y", "x"), [(at, at % 4 * planes + at // 4) for at in range(blocks)]
    )
    grad_out_w = both_of(grad_out_w, "c").transpose(1, 0, 2).reshape(rows_here, features).astype(F32)
    grad_down_w = both_of(grad_down_w, "c").reshape(hidden_here, features).astype(F32)
    (grad_mixer_w,) = move(12, ("spread", grad_mixer_w.reshape(1, 4, rows_here, -1)), us=18)
    grad_mixer_w = grad_mixer_w[:, :, 0]
    sums = jnp.sum(grad_mixer_w[0, :, :, vectors:width].astype(F32), axis=0)
    grad_mixer_w = grad_mixer_w.transpose(2, 1, 0, 3)
    grad_w = [
        grad_mixer_w[..., i * depth // 2:(i + 1) * depth // 2].reshape(rows_here, features).astype(F32) for i in range(3)
    ]
    grad_forget_w = grad_mixer_w[..., 3 * depth // 2:vectors].reshape(rows_here, HEADS * SLOTS).astype(F32)
    return (
        output.reshape(inputs.shape), grad_input.reshape(inputs.shape), sums[:, 0], grad_w[0], grad_w[1], grad_w[2],
        grad_forget_w, sums[:bias_here, 2], grad_out_w, sums[:, 1], grad_gate_w, grad_up_w, grad_down_w,
    )


def solution(mesh):
    planes = mesh.shape["dp"] // 4
    fine = Mesh(mesh.devices.reshape(planes, 2, 2, 2), ("z", "y", "x", "c"))
    dp = ("z", "y", "x")
    tokens, vector, matrix = P(dp, "c", None), P(dp), P(dp, None)
    in_specs = (
        tokens, P(dp, "c"), vector, matrix, matrix, matrix, matrix, vector, matrix, vector, matrix, matrix, matrix, tokens
    )
    out_specs = (
        tokens, tokens, vector, matrix, matrix, matrix, matrix, vector, matrix, vector, matrix, matrix, matrix
    )
    return jax.shard_map(body, mesh=fine, in_specs=in_specs, out_specs=out_specs, check_vma=False)
```

```python
import functools

import jax
import jax.numpy as jnp
from jax import lax
from jax.sharding import Mesh
from jax.sharding import PartitionSpec as P
from jax.experimental import pallas as pl
from jax.experimental.pallas import tpu as pltpu

HEADS = 4
SLOTS = 64
DEPTH = 512
TILE = 128
EPSILON = 1e-06
F32, BF16 = jnp.float32, jnp.bfloat16
NN = (((1,), (0,)), ((), ()))
NT = (((1,), (1,)), ((), ()))
TN = (((0,), (0,)), ((), ()))
HALVES = (64, 32, 16, 8, 4, 2, 1)
MESH = pl.DeviceIdType.MESH


def cost(us):
    return pl.CostEstimate(flops=0, bytes_accessed=us * 3_000_000, transcendentals=0)


def routes(kind, i, y, x, c):
    chip = {"y": i // 2 % 2, "x": i % 2}
    if kind == "to_homes":
        return {"y": c, "x": i // 2, "c": i % 2}, {**chip, "c": y}, y * 2 + x
    if kind in ("from_homes", "copy_homes"):
        return {**chip, "c": y}, {"y": c, "x": i // 2, "c": i % 2}, x * 2 + c
    return {**chip, "c": c}, {**chip, "c": c}, y * 2 + x


def enter_plane(y, x, c, more=(), greeted=0):
    barrier = pltpu.get_barrier_semaphore()
    peers = list(more)
    for flip in range(1, 8):
        peers.append({
            "y": lax.rem(y + flip // 4, 2), "x": lax.rem(x + (flip // 2) % 2, 2), "c": lax.rem(c + flip % 2, 2)
        })
    for peer in peers:
        pl.semaphore_signal(barrier, inc=1, device_id=peer, device_id_type=MESH)
    pl.semaphore_wait(barrier, len(peers) + greeted)


def swap_kernel_sems(count):
    return [pltpu.SemaphoreType.DMA((count,)), pltpu.SemaphoreType.DMA((count,))]


def remote(source, target, send, recv, peer):
    return pltpu.make_async_remote_copy(
        src_ref=source, dst_ref=target, send_sem=send, recv_sem=recv, device_id=peer, device_id_type=MESH
    )


class Stay:
    def __init__(self, source, target, sem, buffer):
        self.load = pltpu.make_async_copy(source, buffer, sem)
        self.store = pltpu.make_async_copy(buffer, target, sem)

    def start(self):
        self.load.start()
        self.load.wait()
        self.store.start()

    def wait(self):
        self.store.wait()


class GatherNear:
    def __init__(self, a_ref, out_ref, y, x, send, recv, *local):
        to_x, to_y = {"x": 1 - x}, {"y": 1 - y}
        here = y * 2 + x
        parts = halves_at(a_ref.shape[0])

        def copy(part, n, peer):
            return remote(a_ref.at[parts[part]], out_ref.at[here, parts[part]], send.at[n], recv.at[n], peer)

        self.own = Stay(a_ref, out_ref.at[here], *local)
        self.first, self.second = [copy(0, 0, to_x), copy(1, 1, to_y)], [copy(1, 2, to_x), copy(0, 3, to_y)]
        self.all = self.first + self.second

    def start(self):
        for copy in self.all + [self.own]:
            copy.start()

    def wait(self):
        for copy in self.all:
            copy.wait()
        self.own.wait()


class GatherFar:
    def __init__(self, out_ref, y, x, send, recv):
        at_x, at_y = y * 2 + 1 - x, (1 - y) * 2 + x
        parts = halves_at(out_ref.shape[1])

        def copy(place, part, n, peer):
            block = out_ref.at[place, parts[part]]
            return remote(block, block, send.at[n], recv.at[n], peer)

        self.all = [copy(at_x, 0, 0, {"y": 1 - y}), copy(at_y, 1, 1, {"x": 1 - x})]

    def start(self):
        for copy in self.all:
            copy.start()

    def wait(self):
        for copy in self.all:
            copy.wait()


def halves_at(rows):
    return [pl.ds(0, rows // 2), pl.ds(rows // 2, rows // 2)]


class Gather:
    def __init__(self, a_ref, out_ref, y, x, send, recv, *local):
        self.near = GatherNear(a_ref, out_ref, y, x, send, recv, *local)
        self.far = GatherFar(out_ref, y, x, send.at[pl.ds(4, 2)], recv.at[pl.ds(4, 2)])

    def start(self):
        self.near.start()

    def wait(self):
        for copy, onward in zip(self.near.first, self.far.all):
            copy.wait_recv()
            onward.start()
        for copy in self.near.second + self.far.all:
            copy.wait_recv()
        for copy in self.near.all + self.far.all:
            copy.wait_send()
        self.near.own.wait()


class ReduceNear:
    def __init__(self, a_ref, out_ref, y, x, send, recv):
        parts = halves_at(a_ref.shape[1])
        self.all = []
        for i, (at_y, at_x) in enumerate(((1 - y, 1 - x), (y, x))):
            blocks = (at_y * 2 + 1 - x, (1 - y) * 2 + at_x)
            for part, peer in enumerate(({"x": 1 - x}, {"y": 1 - y})):
                n = 2 * part + i
                self.all.append(
                    remote(a_ref.at[blocks[part], parts[part]], out_ref.at[part, i], send.at[n], recv.at[n], peer)
                )

    def start(self):
        for copy in self.all:
            copy.start()

    def wait(self):
        for copy in self.all:
            copy.wait()


class ReduceFar:
    def __init__(self, a_ref, out_ref, y, x, send, recv):
        self.all = [
            remote(a_ref.at[n], out_ref.at[n], send.at[n], recv.at[n], peer)
            for n, peer in enumerate(({"y": 1 - y}, {"x": 1 - x}))
        ]

    def start(self):
        for copy in self.all:
            copy.start()

    def wait(self):
        for copy in self.all:
            copy.wait()


def home_of_rows(y, x, z, planes):
    chip = y * 2 + x
    here = z * 4 + chip
    return here, chip * planes + z, lax.rem(here, planes) * 4 + here // planes


def device(block, core):
    return {"z": block // 4, "y": lax.rem(block, 4) // 2, "x": lax.rem(block, 2), "c": core}


def greet_homes(y, x, c, z, planes):
    here, goal, origin = home_of_rows(y, x, z, planes)

    @pl.when(goal != here)
    def _():
        for block in (goal, origin):
            pl.semaphore_signal(
                pltpu.get_barrier_semaphore(), inc=1, device_id=device(block, c), device_id_type=MESH
            )

    return jnp.where(goal != here, 2, 0)


class Swap:
    def __init__(self, a_ref, out_ref, c, send, recv):
        self.copy = remote(a_ref, out_ref, send.at[0], recv.at[0], {"c": 1 - c})

    def start(self):
        self.copy.start()

    def wait(self):
        self.copy.wait()


class Moves:
    def __init__(self, kind, source, target, y, x, c, send, recv, *local):
        self.copies = []
        for i in range(4):
            peer, giver, slot = routes(kind, i, y, x, c)
            to_me, from_me = (
                (at["y"] == y) & (at["x"] == x) & (at["c"] == c) for at in (peer, giver)
            )
            self.copies.append((
                to_me, from_me,
                Stay(source(i), target(slot), *local),
                remote(source(i), target(slot), send.at[i], recv.at[slot], peer),
                Stay(source(i), target(i), *local),
                remote(source(i), target(i), send.at[i], recv.at[i], peer),
            ))

    def start(self):
        for to_me, _, _, there, _, _ in self.copies:
            pl.when(jnp.logical_not(to_me))(there.start)
        for to_me, _, here, _, _, _ in self.copies:
            pl.when(to_me)(here.start)

    def wait(self):
        for to_me, from_me, _, _, here, there in self.copies:
            pl.when(jnp.logical_not(to_me))(there.wait_send)
            pl.when(jnp.logical_not(from_me))(there.wait_recv)
            pl.when(from_me)(here.wait)


class Spread:
    def __init__(self, a_ref, out_ref, y, x, c, send, recv, *local):
        here, other = y * 2 + x, {"c": 1 - c}
        self.own = Stay(a_ref.at[:, here], out_ref.at[c, here], *local)
        self.across = [remote(a_ref.at[:, here], out_ref.at[c, here], send.at[0], recv.at[0], other)]
        self.sent = []
        for flip in (1, 2, 3):
            peer = {"y": lax.rem(y + flip // 2, 2), "x": lax.rem(x + flip % 2, 2)}
            chip = peer["y"] * 2 + peer["x"]
            self.sent.append(remote(a_ref.at[:, chip], out_ref.at[c, here], send.at[flip], recv.at[flip], peer))
            self.across.append(
                remote(out_ref.at[c, chip], out_ref.at[c, chip], send.at[3 + flip], recv.at[3 + flip], other)
            )

    def start(self):
        for copy in self.sent + [self.across[0], self.own]:
            copy.start()

    def wait(self):
        for copy, onward in zip(self.sent, self.across[1:]):
            copy.wait_recv()
            onward.start()
        for copy in self.across:
            copy.wait()
        for copy in self.sent:
            copy.wait_send()
        self.own.wait()


def move_scratch(kind, a):
    sems = swap_kernel_sems({"spread": 7, "copy_chips": 6}.get(kind, 4)) + [pltpu.SemaphoreType.DMA]
    if kind in ("copy_homes", "copy_chips", "gather_near", "keep"):
        block = a.shape
    elif kind == "spread":
        block = a.shape[:1] + a.shape[2:]
    else:
        block = a.shape[1:] if kind in ("to_homes", "from_homes", "columns") else (16, TILE)
    return sems + [pltpu.VMEM(block, a.dtype)]


def moved(kind, a):
    if kind == "spread":
        return jax.ShapeDtypeStruct((2, 4, a.shape[0]) + a.shape[2:], a.dtype)
    if kind == "reduce_near":
        return jax.ShapeDtypeStruct((2, 2, a.shape[1] // 2) + a.shape[2:], a.dtype)
    if kind in ("swap_core", "keep", "gather_far", "reduce_far"):
        return jax.ShapeDtypeStruct(a.shape, a.dtype)
    block = a.shape if kind in ("copy_homes", "copy_chips", "gather_near") else a.shape[1:]
    return jax.ShapeDtypeStruct((4,) + block, a.dtype)


def one_move(kind, a_ref, out_ref, y, x, c, *sems):
    if kind == "spread":
        return Spread(a_ref, out_ref, y, x, c, *sems)
    if kind == "copy_chips":
        return Gather(a_ref, out_ref, y, x, *sems)
    if kind == "gather_near":
        return GatherNear(a_ref, out_ref, y, x, *sems)
    if kind == "gather_far":
        return GatherFar(out_ref, y, x, *sems[:2])
    if kind in ("reduce_near", "reduce_far"):
        return (ReduceNear if kind == "reduce_near" else ReduceFar)(a_ref, out_ref, y, x, *sems[:2])
    if kind == "swap_core":
        return Swap(a_ref, out_ref, c, *sems[:2])
    if kind == "keep":
        return Stay(a_ref, out_ref, *sems[2:])

    def source(i):
        return a_ref if kind == "copy_homes" else a_ref.at[i]

    return Moves(kind, source, lambda slot: out_ref.at[slot], y, x, c, *sems)


def all_moves(kinds, sources, results, sems, y, x, c):
    return [one_move(kind, sources[n], results[n], y, x, c, *sems[4 * n:4 * n + 4]) for n, kind in enumerate(kinds)]


def compute_body(counts, kinds, grid, body, *refs):
    refs, parts = list(refs), []
    for count in counts:
        parts.append(refs[:count])
        refs = refs[count:]
    operands, sources, _, outs, results, scratch, sems = parts
    if kinds:
        y, x, c = (lax.axis_index(name) for name in ("y", "x", "c"))
        moves = all_moves(kinds, sources, results, sems, y, x, c)
        first, last = True, True
        for axis, size in enumerate(grid):
            first, last = first & (pl.program_id(axis) == 0), last & (pl.program_id(axis) == size - 1)

        def start():
            enter_plane(y, x, c)
            for one in moves:
                one.start()

        def finish():
            for one in moves:
                one.wait()

        pl.when(first)(start) if grid else start()
    body(*operands, *outs, *scratch)
    if kinds:
        pl.when(last)(finish) if grid else finish()


def compute(body, name, operands, in_specs, out_specs, out_shape, us, grid=(), scratch=(), moves=(), collective=None, after=()):
    any_place = pl.BlockSpec(memory_space=pl.ANY)
    kinds = tuple(kind for kind, _ in moves)
    sems = [sem for kind, a in moves for sem in move_scratch(kind, a)]
    counts = (len(operands), len(moves), len(after), len(out_shape), len(moves), len(scratch), len(sems))
    params = {"collective_id": collective, "has_side_effects": True} if moves else {}
    aliases = {len(operands) + n: len(out_shape) + n for n, kind in enumerate(kinds) if kind == "gather_far"}
    return pl.pallas_call(
        functools.partial(compute_body, counts, kinds, grid, body),
        name=name,
        grid=grid,
        in_specs=list(in_specs) + [any_place] * (len(moves) + len(after)),
        out_specs=list(out_specs) + [any_place] * len(moves),
        out_shape=list(out_shape) + [moved(kind, a) for kind, a in moves],
        scratch_shapes=list(scratch) + sems,
        input_output_aliases=aliases,
        compiler_params=pltpu.CompilerParams(vmem_limit_bytes=60 << 20, **params),
        cost_estimate=cost(us),
    )(*operands, *(a for _, a in moves), *after)


def move_kernel(kinds, waits, *refs):
    count = len(kinds)
    sources, results, sems = refs[:count], refs[count + waits:2 * count + waits], refs[2 * count + waits:]
    y, x, c = (lax.axis_index(name) for name in ("y", "x", "c"))
    enter_plane(y, x, c)
    moves = all_moves(kinds, sources, results, sems, y, x, c)
    for one in moves:
        one.start()
    for one in moves:
        one.wait()


def move(collective, *items, after=(), us=48):
    kinds = tuple(kind for kind, _ in items)
    any_place = pl.BlockSpec(memory_space=pl.ANY)
    return pl.pallas_call(
        functools.partial(move_kernel, kinds, len(after)),
        name=kinds[0],
        out_shape=[moved(kind, a) for kind, a in items],
        in_specs=[any_place] * (len(items) + len(after)),
        out_specs=[any_place] * len(items),
        scratch_shapes=[sem for kind, a in items for sem in move_scratch(kind, a)],
        compiler_params=pltpu.CompilerParams(collective_id=collective, has_side_effects=True),
        cost_estimate=cost(us),
    )(*(a for _, a in items), *after)


def hidden_columns(core, planes, weights, out_ref):
    for chip in range(4):
        pieces = []
        for w_ref in weights:
            piece = w_ref.shape[1] // (8 * planes)
            for z in range(planes):
                start = (z * 4 + chip) * 2 * piece
                both = w_ref[:, start:start + 2 * piece].astype(F32)
                pieces.append(jnp.where(core == 0, both[:, :piece], both[:, piece:]))
        out_ref[chip] = jnp.concatenate(pieces, axis=1).astype(BF16)


def start_kernel(kinds, planes, *refs):
    count = len(kinds)
    projections, rest_ref, gate_ref, up_ref, sources = refs[:3], refs[3], refs[4], refs[5], refs[6:6 + count]
    results, h_ref, m_ref = refs[6 + count:6 + 2 * count], refs[6 + 2 * count], refs[7 + 2 * count]
    hidden_ref, gate_room, up_room, load, *sems = refs[8 + 2 * count:]
    y, x, c, z = (lax.axis_index(name) for name in ("y", "x", "c", "z"))
    up, down = lax.rem(z + 1, planes), lax.rem(z + planes - 1, planes)
    wide = DEPTH // 2
    loads = [
        pltpu.make_async_copy(w_ref, room, load.at[n]) for n, (w_ref, room) in enumerate(((gate_ref, gate_room), (up_ref, up_room)))
    ]
    for copy in loads:
        copy.start()
    enter_plane(y, x, c, [{"z": up}, {"z": down}])
    moves = all_moves(kinds, sources, results, sems, y, x, c)
    sems = sems[4 * count:]
    moves.append(one_move("columns", hidden_ref, h_ref, y, x, c, *sems[:4]))
    sems = sems[4:]

    def part(n, source, columns):
        return Moves(
            "columns", source, lambda slot: m_ref.at[c, z, slot, :, columns], y, x, c, *sems[4 * n:4 * n + 4]
        )

    def columns_of(w_ref):
        return lambda i: w_ref.at[:, pl.ds(pl.multiple_of((2 * i + c) * wide, wide), wide)]

    parts = [part(n, columns_of(w_ref), pl.ds(n * wide, wide)) for n, w_ref in enumerate(projections)]
    parts.append(part(3, lambda i: rest_ref.at[i], pl.ds(3 * wide, TILE)))
    m_send, m_recv, core_send, core_recv = sems[16:]

    def block(step):
        return m_ref.at[c, lax.rem(z + planes - step, planes)]

    ring = [
        remote(block(step), block(step), m_send.at[step], m_recv.at[step], {"z": up}) for step in range(planes - 1)
    ]
    across = [
        remote(block(step), block(step), core_send.at[step], core_recv.at[step], {"c": 1 - c}) for step in range(planes)
    ]
    for one in parts:
        one.start()
    for copy in loads:
        copy.wait()
    hidden_columns(c, planes, (gate_room, up_room), hidden_ref)
    for one in parts:
        one.wait()
    ring[0].start()
    across[0].start()
    for one in moves:
        one.start()
    for step in range(planes - 1):
        ring[step].wait_recv()
        if step < planes - 2:
            ring[step + 1].start()
        across[step + 1].start()
    for one in moves:
        one.wait()
    for copy in across:
        copy.wait()
    for copy in ring:
        copy.wait_send()


def start_moves(collective, projections, rest, gate, up, items):
    planes = lax.axis_size("z")
    kinds = tuple(kind for kind, _ in items)
    any_place = pl.BlockSpec(memory_space=pl.ANY)
    shapes = [moved(kind, a) for kind, a in items]
    hidden = jax.ShapeDtypeStruct((4, gate.shape[0], gate.shape[1] // 4), BF16)
    shapes.append(hidden)
    shapes.append(jax.ShapeDtypeStruct((2, planes, 4, rest.shape[1], 3 * DEPTH // 2 + TILE), BF16))
    sems = [pltpu.VMEM(hidden.shape, BF16), pltpu.VMEM(gate.shape, BF16), pltpu.VMEM(up.shape, BF16), pltpu.SemaphoreType.DMA((2,))]
    sems += [sem for kind, a in items for sem in move_scratch(kind, a)] + move_scratch("columns", hidden)
    part = jax.ShapeDtypeStruct((4, rest.shape[1], DEPTH // 2), BF16)
    sems += [sem for a in (part, part, part, rest) for sem in move_scratch("columns", a)]
    sems += swap_kernel_sems(planes) + swap_kernel_sems(planes)
    return pl.pallas_call(
        functools.partial(start_kernel, kinds, planes),
        name="start_moves",
        out_shape=shapes,
        in_specs=[any_place] * (6 + len(items)),
        out_specs=[any_place] * len(shapes),
        scratch_shapes=sems,
        compiler_params=pltpu.CompilerParams(collective_id=collective, has_side_effects=True, vmem_limit_bytes=60 << 20),
        cost_estimate=cost(85),
    )(*projections, rest, gate, up, *(a for _, a in items))


class PlaneSum:
    def __init__(self, a_ref, rooms, y, x):
        self.near_ref, self.onward_ref, self.far_ref, *sems = rooms
        self.near = ReduceNear(a_ref, self.near_ref, y, x, *sems[:2])
        self.far = ReduceFar(self.onward_ref, self.far_ref, y, x, *sems[2:])

    def start(self):
        self.near.start()

    def go_on(self, own):
        self.near.wait()
        for part in range(2):
            self.onward_ref[part] = (own(part, 0).astype(F32) + self.near_ref[part, 0].astype(F32)).astype(BF16)
        self.far.start()

    def total(self, own, part, some):
        return (
            own(part, 1)[some, :].astype(F32) + self.near_ref[part, 1, some, :].astype(F32)
            + self.far_ref[part, some, :].astype(F32)
        )


def sum_rooms(rows, features):
    half = (rows // 2, features)
    sem = pltpu.SemaphoreType.DMA
    return [
        pltpu.VMEM((2, 2) + half, BF16), pltpu.VMEM((2,) + half, BF16), pltpu.VMEM((2,) + half, BF16),
        sem((4,)), sem((4,)), sem((2,)), sem((2,)),
    ]


def end_kernel(planes, g_ref, gn_ref, block_ref, w_ref, grad_attended_ref, x_ref, gain_ref, attended_ref, *refs):
    outs, w_out_ref, grad_ref, output_ref, refs = refs[:4], refs[4], refs[5], refs[6], refs[7:]
    own_ref, core_ref, ring_ref, sum_ref, land_ref, w_land_ref, shares_ref, mine_ref, refs = *refs[:8], refs[8:]
    load, core_send, core_recv, ring_send, ring_recv, spread_send, spread_recv, w_send, w_recv, w_local = refs[:10]
    mine_load, shares_load, shares_send, shares_recv, *rooms = refs[10:]
    y, x, c, z = (lax.axis_index(name) for name in ("y", "x", "c", "z"))
    chip, other = y * 2 + x, {"c": 1 - c}
    up, down = {"z": lax.rem(z + 1, planes)}, {"z": lax.rem(z + planes - 1, planes)}
    here, goal, _ = home_of_rows(y, x, z, planes)
    enter_plane(y, x, c, [up, down], greet_homes(y, x, c, z, planes))
    rows = own_ref.shape[1]
    half, size = rows // 2, rows // 4
    parts = [pl.ds(0, half), pl.ds(half, half)]
    blocks = [[(1 - y) * 2 + x, chip], [y * 2 + 1 - x, chip]]
    token_parts = halves_at(block_ref.shape[1])

    def place(step):
        return lax.rem(z + 2 * planes - 1 - step, planes)

    loads = [pltpu.make_async_copy(g_ref.at[place(s), c], own_ref.at[s], load.at[s]) for s in range(planes)]
    across = [
        remote(g_ref.at[place(s), 1 - c], core_ref.at[s], core_send.at[s], core_recv.at[s], other) for s in range(planes)
    ]
    shares_across = [
        remote(gn_ref.at[2 * i + 1 - c], shares_ref.at[2 * c + i], shares_send.at[i], shares_recv.at[i], other)
        for i in range(2)
    ]
    shares_own = [
        pltpu.make_async_copy(gn_ref.at[2 * i + c], shares_ref.at[2 * c + i], shares_load.at[i]) for i in range(2)
    ]
    mine = [
        pltpu.make_async_copy(
            block_ref.at[blocks[part][i], token_parts[part]], mine_ref.at[part, i], mine_load.at[2 * part + i]
        ) for part in range(2) for i in range(2)
    ]
    out_sum = PlaneSum(block_ref, rooms[:7], y, x)
    in_sum = PlaneSum(shares_ref, rooms[7:], y, x)
    out_sum.start()
    for s in range(planes):
        across[s].start()
        loads[s].start()
        if s == 0:
            for copy in shares_across + shares_own + mine:
                copy.start()
    w_stay = pltpu.make_async_copy(w_ref, w_land_ref.at[c], w_local)
    w_sent = remote(w_ref, w_land_ref.at[c], w_send.at[0], w_recv.at[0], device(goal, c))
    w_passed = remote(w_land_ref.at[c], w_land_ref.at[c], w_send.at[1], w_recv.at[1], other)
    pl.when(goal == here)(w_stay.start)

    def ring(s, part):
        return remote(
            sum_ref.at[s, parts[part]], ring_ref.at[s, parts[part]], ring_send.at[s, part], ring_recv.at[s, part], up
        )

    def out_own(part, i):
        return mine_ref.at[part, i][...]

    def in_own(part, i):
        return shares_ref[blocks[part][i], token_parts[part], :]

    for s in range(planes):
        if s == 1:
            for copy in mine:
                copy.wait()
            out_sum.go_on(out_own)
            pl.when(goal != here)(w_sent.start)
        if s == planes - 1:
            in_sum.go_on(in_own)
        across[s].wait_recv()
        loads[s].wait()
        for part in range(2):
            total = own_ref[s, parts[part], :].astype(F32) + core_ref[s, parts[part], :].astype(F32)
            if s > 0:
                ring(s - 1, part).wait_recv()
                total = total + ring_ref[s - 1, parts[part], :].astype(F32)
            sum_ref[s, parts[part], :] = total.astype(BF16)
            if s < planes - 1:
                ring(s, part).start()
        if s == 0:
            for copy in shares_across:
                copy.wait_recv()
            for copy in shares_own:
                copy.wait()
            in_sum.start()

    sent, passed = [], []
    for flip in range(4):
        peer = {"y": lax.rem(y + flip // 2, 2), "x": lax.rem(x + flip % 2, 2)}
        at = peer["y"] * 2 + peer["x"]
        some = sum_ref.at[planes - 1, pl.ds(pl.multiple_of(at * size, size), size)]
        if flip:
            sent.append(remote(some, land_ref.at[c, chip], spread_send.at[flip], spread_recv.at[flip], peer))
            sent[-1].start()
        source = land_ref.at[c, at] if flip else some
        passed.append(remote(source, land_ref.at[c, at], spread_send.at[4 + flip], spread_recv.at[4 + flip], other))
    passed[0].start()
    land_ref[c, chip] = sum_ref[planes - 1, pl.ds(pl.multiple_of(chip * size, size), size), :]
    pl.when(goal == here)(w_stay.wait)
    pl.when(goal != here)(w_sent.wait)
    w_passed.start()
    out_sum.far.wait()
    tokens = output_ref.shape[0] // 2
    some = slice(0, tokens)
    for part in range(2):
        here_rows = slice(part * tokens, (part + 1) * tokens)
        output_ref[here_rows, :] = (attended_ref[here_rows, :] + out_sum.total(out_own, part, some)).astype(BF16)
    for copy, onward in zip(sent, passed[1:]):
        copy.wait_recv()
        onward.start()
    in_sum.far.wait()
    for part in range(2):
        here_rows = slice(part * tokens, (part + 1) * tokens)
        input_back(in_sum.total(in_own, part, some), here_rows, grad_attended_ref, x_ref, gain_ref, grad_ref)
    for copy in passed:
        copy.wait_recv()
    wide = DEPTH // 2
    for at in range(4):
        for core in range(2):
            block = land_ref[core, at].astype(F32)
            columns = pl.ds((2 * at + core) * wide, wide)
            for n in range(3):
                outs[n][:, columns] = block[:, n * wide:(n + 1) * wide]
            outs[3][core, at] = block[:, 3 * wide:]
    w_passed.wait()
    wide = w_land_ref.shape[2]
    for core in range(2):
        w_out_ref[:, core * wide:(core + 1) * wide] = w_land_ref[core].astype(F32)
    for copy in sent + passed + across + shares_across:
        copy.wait_send()
    for s in range(planes - 1):
        for part in range(2):
            ring(s, part).wait_send()


def input_back(grad, some, attended_ref, x_ref, gain_ref, out_ref):
    x = x_ref[some, :].astype(F32)
    ratio = lax.rsqrt(jnp.mean(x * x, axis=1, keepdims=True) + EPSILON)
    u, xh = grad * gain_ref[...], x * ratio
    back = ratio * (u - xh * jnp.mean(u * xh, axis=1, keepdims=True))
    out_ref[some, :] = attended_ref[some, :] + back


def end_moves(collective, grads, gn, block_out, w, grad_attended, x, gain, attended):
    planes, _, rows, columns = grads.shape
    here, features = rows // 4, x.shape[1]
    any_place, in_vmem = pl.BlockSpec(memory_space=pl.ANY), pl.BlockSpec(memory_space=pltpu.VMEM)
    matrix = jax.ShapeDtypeStruct((here, features), F32)
    blocks = pltpu.VMEM((planes, rows, columns), BF16)
    sem = pltpu.SemaphoreType.DMA
    half = (x.shape[0] // 2, features)
    return pl.pallas_call(
        functools.partial(end_kernel, planes),
        name="end_moves",
        out_shape=[
            matrix, matrix, matrix, jax.ShapeDtypeStruct((2, 4, here, TILE), F32), matrix,
            jax.ShapeDtypeStruct(x.shape, F32), jax.ShapeDtypeStruct(x.shape, BF16),
        ],
        in_specs=[any_place] * 4 + [in_vmem] * 4,
        out_specs=[in_vmem] * 7,
        scratch_shapes=[
            blocks, blocks, pltpu.VMEM((planes - 1, rows, columns), BF16), blocks,
            pltpu.VMEM((2, 4, here, columns), BF16), pltpu.VMEM((2,) + w.shape, BF16), pltpu.VMEM(gn.shape, gn.dtype),
            pltpu.VMEM((2, 2) + half, BF16),
            sem((planes,)), sem((planes,)), sem((planes,)), sem((planes - 1, 2)), sem((planes - 1, 2)), sem((8,)), sem((8,)),
            sem((2,)), sem((2,)), sem, sem((4,)), sem((2,)), sem((2,)), sem((2,)),
        ] + sum_rooms(*x.shape) + sum_rooms(*x.shape),
        compiler_params=pltpu.CompilerParams(collective_id=collective, has_side_effects=True, vmem_limit_bytes=60 << 20),
        cost_estimate=cost(95),
    )(grads, gn, block_out, w, grad_attended, x, gain, attended)


def dot(a, b, dims):
    return lax.dot_general(a, b, dims, preferred_element_type=F32)


def parts_of(a):
    high = a.astype(BF16)
    return high, (a - high.astype(F32)).astype(BF16)


def dot_parts(a, b, dims):
    return dot(a[0], b[0], dims) + (dot(a[1], b[0], dims) + dot(a[0], b[1], dims))


def dot_ones(ones, a):
    high = a.astype(BF16)
    rest = a - high.astype(F32)
    middle = rest.astype(BF16)
    low = (rest - middle.astype(F32)).astype(BF16)
    return dot(ones, high, NN) + (dot(ones, middle, NN) + dot(ones, low, NN))


def places():
    shape = (TILE, TILE)
    return lax.broadcasted_iota(jnp.int32, shape, 0), lax.broadcasted_iota(jnp.int32, shape, 1)


def ones_where(mask):
    return jnp.where(mask, 1.0, 0.0).astype(BF16)


def steps_to_middle(half):
    t, s = places()
    block = 2 * half
    same = (t // block) == (s // block)
    t_right, s_right = (t % block) >= half, (s % block) >= half
    right = t_right & s_right & (s <= t)
    left = jnp.logical_not(t_right | s_right) & (s > t)
    return ones_where(same & (right | left))


def pair_mask(half, turned=False):
    t, s = places()
    if turned:
        t, s = s, t
    block = 2 * half
    return ((t // block) == (s // block)) & ((t % block) >= half) & ((s % block) < half)


def first_row(rows):
    return lax.broadcasted_iota(jnp.int32, (rows, 2 * SLOTS), 1) < SLOTS


def row_sums(a, first):
    return (
        jnp.sum(jnp.where(first, a, 0.0), axis=1, keepdims=True),
        jnp.sum(jnp.where(first, 0.0, a), axis=1, keepdims=True),
    )


def tile_rows(j):
    return pl.ds(pl.multiple_of(j * TILE, TILE), TILE)


def prepare(lf_ref, decay_ref, reach_ref, e_ref, tiles):
    t, s = places()

    @pl.loop(0, tiles)
    def _(j):
        rows = tile_rows(j)
        lf = lf_ref[rows, :]
        decay_ref[rows, :] = dot_ones(ones_where(s <= t), lf)
        reach_ref[rows, :] = dot_ones(ones_where(s > t), lf)
        for level, half in enumerate(HALVES):
            e_ref[level, rows, :] = jnp.exp(dot_ones(steps_to_middle(half), lf))


def far_pairs(tiles):
    out, half = [], tiles // 2
    while half >= 1:
        for start in range(0, tiles, 2 * half):
            out.append((start + half, start, half))
        half //= 2
    return out


def far_decays(right, left, half, decay_ref, reach_ref):
    after, total = [], None
    for j in range(right, right + half):
        part = decay_ref[j * TILE:(j + 1) * TILE, :]
        after.append(jnp.exp(part if total is None else part + total))
        last = part[TILE - 1:TILE, :]
        total = last if total is None else total + last
    before, total = [], None
    for j in range(left + half - 1, left - 1, -1):
        part = reach_ref[j * TILE:(j + 1) * TILE, :]
        before.append(jnp.exp(part if total is None else part + total))
        whole = decay_ref[(j + 1) * TILE - 1:(j + 1) * TILE, :]
        total = whole if total is None else total + whole
    if half == 1:
        return after[0], before[0]
    return jnp.concatenate(after, axis=0), jnp.concatenate(before[::-1], axis=0)


def diagonal_of(block):
    t, s = places()
    return jnp.sum(jnp.where(t == s, block, 0.0), axis=1, keepdims=True)


def weighted_sums(a_ref, out_ref, gain_ref, decay_ref, reach_ref, e_ref, tiles):
    first = first_row(TILE)

    @pl.loop(0, tiles)
    def _(j):
        rows = tile_rows(j)
        gain = gain_ref[rows, :]
        blocks = [a_ref[r, rows, rows] for r in range(2)]
        total = jnp.where(first, diagonal_of(blocks[0]), diagonal_of(blocks[1])) * gain
        for level, half in enumerate(HALVES):
            e = e_ref[level, rows, :]
            x = parts_of(e * gain)
            pairs = pair_mask(half)
            y = [dot_parts(parts_of(jnp.where(pairs, a, 0.0)), x, NN) for a in blocks]
            total = total + e * jnp.where(first, y[0], y[1])
        out_ref[rows, :] = total

    for right, left, half in far_pairs(tiles):
        after, before = far_decays(right, left, half, decay_ref, reach_ref)
        here = slice(right * TILE, (right + half) * TILE)
        there = slice(left * TILE, (left + half) * TILE)
        x = parts_of(before * gain_ref[there, :])
        y = [dot_parts(parts_of(a_ref[r, here, there]), x, NN) for r in range(2)]
        out_ref[here, :] += after * jnp.where(first_row(half * TILE), y[0], y[1])


def split_rows(a, first):
    return parts_of(jnp.where(first, a, 0.0)), parts_of(jnp.where(first, 0.0, a))


def paired_weights(p_ref, out_ref, gain_ref, decay_ref, reach_ref, e_ref, tiles):
    first = first_row(TILE)
    t, s = places()

    @pl.loop(0, tiles)
    def _(j):
        rows = tile_rows(j)
        gain, p = gain_ref[rows, :], p_ref[rows, :]
        sums = row_sums(p * gain, first)
        total = [jnp.where(t == s, sums[r], 0.0) for r in range(2)]
        for level, half in enumerate(HALVES):
            e = e_ref[level, rows, :]
            x = parts_of(e * gain)
            pairs = pair_mask(half)
            pe = split_rows(p * e, first)
            total = [total[r] + jnp.where(pairs, dot_parts(pe[r], x, NT), 0.0) for r in range(2)]
        for r in range(2):
            out_ref[r, rows, rows] = total[r]

    for right, left, half in far_pairs(tiles):
        after, before = far_decays(right, left, half, decay_ref, reach_ref)
        here = slice(right * TILE, (right + half) * TILE)
        there = slice(left * TILE, (left + half) * TILE)
        x = parts_of(before * gain_ref[there, :])
        pe = split_rows(p_ref[here, :] * after, first_row(half * TILE))
        for r in range(2):
            out_ref[r, here, there] = dot_parts(pe[r], x, NT)
            out_ref[r, there, here] = jnp.zeros((half * TILE, half * TILE), F32)


def inner(a, b, r):
    return dot(a[0][r], b[0][r], NT) + dot(a[1][r], b[1][r], NT)


def sigmoid(v):
    return 1.0 / (1.0 + jnp.exp(-v))


def projections(pre_ref, which, length, act):
    depth = DEPTH // 2
    return [
        [act(pre_ref[f, r * length:(r + 1) * length, which * depth:(which + 1) * depth]) for r in range(2)]
        for f in range(2)
    ]


def silu_low(v):
    return (v * sigmoid(v)).astype(BF16)


def low(v):
    return v.astype(BF16)


def forward_kernel(pre_ref, lf_ref, gain_ref, dcol_ref, drow_ref,
                   mixed_ref, s_ref, p_ref, b_ref, a_ref, decay_ref, reach_ref, e_ref):
    length = lf_ref.shape[0]
    tiles = length // TILE
    scale = DEPTH ** -0.5
    q, k = projections(pre_ref, 0, length, silu_low), projections(pre_ref, 1, length, silu_low)
    for r in range(2):
        same = dcol_ref[r] == drow_ref[r]
        a_ref[r] = jnp.where(same, inner(q, k, r), 0.0)
    prepare(lf_ref, decay_ref, reach_ref, e_ref, tiles)
    weighted_sums(a_ref, s_ref, gain_ref, decay_ref, reach_ref, e_ref, tiles)
    first = first_row(length)
    logits = s_ref[...] * scale
    least = -jnp.inf
    top = jnp.where(
        first,
        jnp.max(jnp.where(first, logits, least), axis=1, keepdims=True),
        jnp.max(jnp.where(first, least, logits), axis=1, keepdims=True),
    )
    grown = jnp.exp(logits - top)
    sums = row_sums(grown, first)
    p_ref[...] = grown / jnp.where(first, sums[0], sums[1])
    paired_weights(p_ref, b_ref, gain_ref, decay_ref, reach_ref, e_ref, tiles)
    v = projections(pre_ref, 2, length, low)
    for r in range(2):
        b = jnp.where(dcol_ref[r] == drow_ref[r], b_ref[r], 0.0)
        b_ref[r] = b
        high, rest = parts_of(b)
        for f in range(2):
            mixed = (dot(high, v[f][r], NN) + dot(rest, v[f][r], NN)).astype(BF16)
            for place in range(2):
                mixed_ref[r, place, f] = mixed[place * length // 2:(place + 1) * length // 2]


def to_columns(r, f):
    t, s = places()
    half = SLOTS // 2
    return ones_where((s < half) & (t == s + r * SLOTS + f * half))


def backward_kernel(pre_ref, g_ref, lf_ref, gain_ref, rate_ref, dcol_ref, drow_ref, s_ref, p_ref, b_ref,
                    out_ref, bias_ref, a_ref, at_ref, dot_ref, h_ref, back_ref, decay_ref, reach_ref, e_ref):
    length = lf_ref.shape[0]
    tiles, depth = length // TILE, DEPTH // 2
    scale = DEPTH ** -0.5
    first_all, first = first_row(length), first_row(TILE)
    t, s = places()
    q, k = projections(pre_ref, 0, length, silu_low), projections(pre_ref, 1, length, silu_low)
    v = projections(pre_ref, 2, length, low)
    grads = [[g_ref[r, :, f].reshape(length, depth) for r in range(2)] for f in range(2)]
    for r in range(2):
        same = dcol_ref[r] == drow_ref[r]
        a_ref[r] = jnp.where(same, inner(grads, v, r), 0.0)
        at_ref[0, r] = jnp.where(same, inner(k, q, r), 0.0)
        at_ref[1, r] = jnp.where(same, inner(v, grads, r), 0.0)
    prepare(lf_ref, decay_ref, reach_ref, e_ref, tiles)
    weighted_sums(a_ref, dot_ref, gain_ref, decay_ref, reach_ref, e_ref, tiles)
    p, dots = p_ref[...], dot_ref[...]
    sums = row_sums(p * dots, first_all)
    h = scale * (p * (dots - jnp.where(first_all, sums[0], sums[1])))
    h_ref[...] = h
    dot_ref[...] = h * s_ref[...] + p * dots
    paired_weights(h_ref, a_ref, gain_ref, decay_ref, reach_ref, e_ref, tiles)
    @pl.loop(0, tiles)
    def _(j):
        rows = tile_rows(j)
        h, p = h_ref[rows, :], p_ref[rows, :]
        keys = [at_ref[0, r, rows, rows] for r in range(2)]
        values = [at_ref[1, r, rows, rows] for r in range(2)]
        total = (
            jnp.where(first, diagonal_of(keys[0]), diagonal_of(keys[1])) * h
            + jnp.where(first, diagonal_of(values[0]), diagonal_of(values[1])) * p
        )
        for level, half in enumerate(HALVES):
            e = e_ref[level, rows, :]
            he, pe = parts_of(h * e), parts_of(p * e)
            pairs = pair_mask(half, turned=True)
            y = [
                dot_parts(parts_of(jnp.where(pairs, keys[r], 0.0)), he, NN)
                + dot_parts(parts_of(jnp.where(pairs, values[r], 0.0)), pe, NN)
                for r in range(2)
            ]
            total = total + e * jnp.where(first, y[0], y[1])
        back_ref[rows, :] = total

    for right, left, half in far_pairs(tiles):
        after, before = far_decays(right, left, half, decay_ref, reach_ref)
        here = slice(right * TILE, (right + half) * TILE)
        there = slice(left * TILE, (left + half) * TILE)
        he, pe = parts_of(h_ref[here, :] * after), parts_of(p_ref[here, :] * after)
        y = [
            dot_parts(parts_of(at_ref[0, r, there, here]), he, NN)
            + dot_parts(parts_of(at_ref[1, r, there, here]), pe, NN)
            for r in range(2)
        ]
        back_ref[there, :] += before * jnp.where(first_row(half * TILE), y[0], y[1])

    for r in range(2):
        rows = slice(r * length, (r + 1) * length)
        c = parts_of(jnp.where(dcol_ref[r] == drow_ref[r], a_ref[r], 0.0))
        w = parts_of(b_ref[r])
        for f in range(2):
            gq = dot(c[0], k[f][r], NN) + dot(c[1], k[f][r], NN)
            out_ref[f, rows, :depth] = (gq * slope(pre_ref[f, rows, :depth])).astype(BF16)
            gk = dot(c[0], q[f][r], TN) + dot(c[1], q[f][r], TN)
            out_ref[f, rows, depth:2 * depth] = (gk * slope(pre_ref[f, rows, depth:2 * depth])).astype(BF16)
            gv = dot(w[0], grads[f][r], TN) + dot(w[1], grads[f][r], TN)
            out_ref[f, rows, 2 * depth:3 * depth] = gv.astype(BF16)
    carried = jnp.zeros((1, 2 * SLOTS), F32)
    for j in range(tiles - 1, -1, -1):
        rows = slice(j * TILE, (j + 1) * TILE)
        back = back_ref[rows, :]
        change = dot_ref[rows, :] - gain_ref[rows, :] * back
        upward = dot_ones(ones_where(s >= t), change) + carried
        h_ref[rows, :] = (upward - jnp.exp(lf_ref[rows, :]) * back) * rate_ref[rows, :]
        carried = upward[0:1, :]
    grad_z = h_ref[...]
    bias_ref[...] = jnp.broadcast_to(jnp.sum(grad_z, axis=0, keepdims=True), bias_ref.shape)
    for r in range(2):
        for f in range(2):
            out_ref[f, r * length:(r + 1) * length, 3 * depth:] = dot(grad_z.astype(BF16), to_columns(r, f), NN).astype(BF16)


def slope(v):
    s = sigmoid(v)
    return s * (1.0 + v * (1.0 - s))


def mix_forward(pre, lf, gain, doc, moves, collective):
    length = lf.shape[0]
    lanes = (length, 2 * SLOTS)
    square = (2, length, length)
    in_vmem = pl.BlockSpec(memory_space=pltpu.VMEM)
    return compute(
        forward_kernel, "mix_forward", (pre, lf, gain, doc[:, :, None], doc[:, None, :]), [in_vmem] * 5, [in_vmem] * 4,
        (
            jax.ShapeDtypeStruct((2, 2, 2, length // 2, DEPTH // 2), BF16), jax.ShapeDtypeStruct(lanes, F32),
            jax.ShapeDtypeStruct(lanes, F32), jax.ShapeDtypeStruct(square, F32),
        ),
        24, scratch=[
            pltpu.VMEM(square, F32), pltpu.VMEM(lanes, F32), pltpu.VMEM(lanes, F32),
            pltpu.VMEM((len(HALVES),) + lanes, F32),
        ],
        moves=moves, collective=collective,
    )


def mix_backward(pre, g, lf, gain, rate, doc, s, p, b, moves, collective):
    length = lf.shape[0]
    lanes = (length, 2 * SLOTS)
    square = (2, length, length)
    in_vmem = pl.BlockSpec(memory_space=pltpu.VMEM)
    return compute(
        backward_kernel, "mix_backward", (pre, g, lf, gain, rate, doc[:, :, None], doc[:, None, :], s, p, b),
        [in_vmem] * 10, [in_vmem] * 2,
        (jax.ShapeDtypeStruct(pre.shape, BF16), jax.ShapeDtypeStruct((8, 2 * SLOTS), F32)), 30,
        scratch=[pltpu.VMEM(square, F32), pltpu.VMEM((2,) + square, F32)] + [pltpu.VMEM(lanes, F32)] * 5
        + [pltpu.VMEM((len(HALVES),) + lanes, F32)],
        moves=moves, collective=collective,
    )


def hidden_kernel(nf_ref, w_ref, hidden_ref, slope_ref, silu_ref):
    units = hidden_ref.shape[2]
    both = dot(nf_ref[...], w_ref[0], NN)
    gate, up = both[:, :units], both[:, units:]
    s = sigmoid(gate)
    silu = gate * s
    hidden_ref[0] = (silu * up).astype(BF16)
    slope_ref[0] = (up * (s * (1.0 + gate * (1.0 - s)))).astype(BF16)
    silu_ref[0] = silu.astype(BF16)


def unit_specs(tokens, features, units):
    rows = tokens // 2
    return (
        pl.BlockSpec((rows, features), lambda h, t: (t, 0)),
        pl.BlockSpec((1, features, 2 * units), lambda h, t: (h, 0, 0)),
        pl.BlockSpec((1, rows, units), lambda h, t: (h, t, 0)),
        jax.ShapeDtypeStruct((2, tokens, units), BF16),
    )


def hidden_units(nf, w, moves, collective):
    some, weight, unit, units_all = unit_specs(*nf.shape, w.shape[2] // 2)
    return compute(
        hidden_kernel, "hidden_units", (nf, w), [some, weight], [unit] * 3, [units_all] * 3, 22, grid=(2, 2),
        moves=moves, collective=collective,
    )


def hidden_grads_kernel(cot_ref, slope_ref, silu_ref, w_ref, wd_ref, grads_ref, back_ref, total_ref):
    half, tile = pl.program_id(0), pl.program_id(1)
    rows = cot_ref.shape[0]
    here = pl.ds(pl.multiple_of(tile * rows, rows), rows)
    grad = dot(cot_ref[...], wd_ref[0], NT)
    gate_up = [grad * slope_ref[0].astype(F32), grad * silu_ref[0].astype(F32)]
    grads = jnp.concatenate(gate_up, axis=1).astype(BF16)
    grads_ref[0] = grads
    back = dot(grads, w_ref[0], NT)

    @pl.when(half == 0)
    def _():
        total_ref[here, :] = back

    @pl.when(half == 1)
    def _():
        back_ref[...] = (total_ref[here, :] + back).astype(BF16)


def hidden_grads(cot, slopes, silus, w, wd):
    tokens, features = cot.shape
    units = slopes.shape[2]
    some, weight, unit, _ = unit_specs(tokens, features, units)
    return compute(
        hidden_grads_kernel, "hidden_grads", (cot, slopes, silus, w, wd),
        [some, unit, unit, weight, pl.BlockSpec((1, units, features), lambda h, t: (h, 0, 0))],
        [
            pl.BlockSpec((1, tokens // 2, 2 * units), lambda h, t: (h, t, 0)),
            pl.BlockSpec((tokens // 2, features), lambda h, t: (h * t, 0)),
        ],
        [jax.ShapeDtypeStruct((2, tokens, 2 * units), BF16), jax.ShapeDtypeStruct(cot.shape, BF16)],
        34, grid=(2, 2), scratch=[pltpu.VMEM((tokens, features), F32)],
    )


def out_kernel(own_ref, other_ref, grad_ref, out_ref):
    core = lax.axis_index("c")
    grads = None
    for a_ref, at_y in ((own_ref, core), (other_ref, 1 - core)):
        for x in range(2):
            part = dot(a_ref[x, 0], grad_ref[2 * at_y + x], TN)
            grads = part if grads is None else grads + part
    rows, wide = out_ref.shape[2:]
    for z in range(out_ref.shape[0]):
        for f in range(2):
            out_ref[z, f] = grads[z * rows:(z + 1) * rows, f * wide:(f + 1) * wide].astype(BF16)


def out_grads(own, other, grad):
    planes = lax.axis_size("z")
    features = grad.shape[2]
    wide = own.shape[3]
    rows = 2 * wide // planes
    some = pl.BlockSpec((2, 1) + own.shape[2:], lambda f: (0, f, 0, 0))
    return compute(
        out_kernel, "out_grads", (own, other, grad), [some, some, pl.BlockSpec(grad.shape, lambda f: (0, 0, 0))],
        [pl.BlockSpec((planes // 2, 2, rows, features // 2), lambda f: (f, 0, 0, 0))],
        [jax.ShapeDtypeStruct((planes, 2, rows, features // 2), BF16)], 8, grid=(2,),
    )[0]


def block_kernel(hidden_ref, wd_ref, out_ref):
    out_ref[...] = (dot(hidden_ref[0], wd_ref[0], NN) + dot(hidden_ref[1], wd_ref[1], NN)).astype(BF16)


def block_outputs(hidden, wd, moves, collective):
    tokens, features = hidden.shape[1], wd.shape[2]
    rows = tokens // 2
    return compute(
        block_kernel, "block_outputs", (hidden, wd),
        [pl.BlockSpec((2, rows, hidden.shape[2]), lambda t: (0, t, 0)), pl.BlockSpec(wd.shape, lambda t: (0, 0, 0))],
        [pl.BlockSpec((rows, features), lambda t: (t, 0))], [jax.ShapeDtypeStruct((tokens, features), BF16)],
        12, grid=(2,), moves=moves, collective=collective,
    )


def weight_kernel(a_ref, b_ref, out_ref):
    out_ref[0, 0] = dot(a_ref[...], b_ref[0], TN).astype(BF16)


def weight_grads(a, b, us, moves=(), collective=None):
    planes = lax.axis_size("z")
    tokens, features = a.shape
    rows, columns = features // planes, b.shape[2]
    return compute(
        weight_kernel, "weight_grads", (a, b),
        [pl.BlockSpec((tokens, rows), lambda h, z: (0, z)), pl.BlockSpec((1, tokens, columns), lambda h, z: (h, 0, 0))],
        [pl.BlockSpec((1, 1, rows, columns), lambda h, z: (z, h, 0, 0))],
        [jax.ShapeDtypeStruct((planes, 2, rows, columns), BF16)], us, grid=(2, planes), moves=moves, collective=collective,
    )


def mixer_weight_kernel(a_ref, b_ref, sums_ref, out_ref):
    grads = dot(a_ref[...], b_ref[0], TN)
    wide = grads.shape[1] - TILE
    out_ref[0, 0, :, :wide] = grads[:, :wide].astype(BF16)
    once = jnp.where(pl.program_id(0) == 0, 1.0, 0.0)
    out_ref[0, 0, :, wide:] = (grads[:, wide:] + once * sums_ref[...]).astype(BF16)


def mixer_weight_grads(a, b, sums, moves, collective):
    planes = lax.axis_size("z")
    tokens, features = a.shape
    rows, columns = features // planes, b.shape[2]
    return compute(
        mixer_weight_kernel, "mixer_weight_grads", (a, b, sums),
        [
            pl.BlockSpec((tokens, rows), lambda h, z: (0, z)), pl.BlockSpec((1, tokens, columns), lambda h, z: (h, 0, 0)),
            pl.BlockSpec((rows, TILE), lambda h, z: (z, 0)),
        ],
        [pl.BlockSpec((1, 1, rows, columns), lambda h, z: (z, h, 0, 0))],
        [jax.ShapeDtypeStruct((planes, 2, rows, columns), BF16)], 20, grid=(2, planes), moves=moves, collective=collective,
    )


def down_kernel(hidden_ref, cot_ref, out_ref):
    grads = dot(hidden_ref[0], cot_ref[...], TN)
    rows = out_ref.shape[2]
    for z in range(out_ref.shape[0]):
        out_ref[z, 0] = grads[z * rows:(z + 1) * rows].astype(BF16)


def down_grads(hidden, cot):
    planes = lax.axis_size("z")
    tokens, features = cot.shape
    units = hidden.shape[2]
    wide = features // 2
    return pl.pallas_call(
        down_kernel,
        name="down_grads",
        grid=(2, 2),
        in_specs=[
            pl.BlockSpec((1, tokens, units), lambda h, i: (h, 0, 0)),
            pl.BlockSpec((tokens, wide), lambda h, i: (0, i)),
        ],
        out_specs=pl.BlockSpec((planes, 1, units // planes, wide), lambda h, i: (0, h, 0, i)),
        out_shape=jax.ShapeDtypeStruct((planes, 2, units // planes, features), BF16),
        compiler_params=pltpu.CompilerParams(vmem_limit_bytes=60 << 20),
        cost_estimate=cost(12),
    )(hidden, cot)


def input_kernel(grad_ref, w_ref, x_ref, out_ref, sums_ref):
    tile = pl.program_id(0)
    back = dot(grad_ref[0], w_ref[0], NT) + dot(grad_ref[1], w_ref[1], NT)
    out_ref[...] = back.astype(BF16)
    x = x_ref[...].astype(F32)
    xh = x * lax.rsqrt(jnp.mean(x * x, axis=1, keepdims=True) + EPSILON)
    sums = jnp.sum((back * xh).reshape(-1, 8, back.shape[1]), axis=0)
    sums_ref[...] = jnp.where(tile == 0, sums, sums_ref[...] + sums)


def input_grads(grad, w, x):
    tokens, features = x.shape
    rows = tokens // 4
    return compute(
        input_kernel, "input_grads", (grad, w, x),
        [
            pl.BlockSpec((2, rows, grad.shape[2]), lambda t: (0, t, 0)), pl.BlockSpec(w.shape, lambda t: (0, 0, 0)),
            pl.BlockSpec((rows, features), lambda t: (t, 0)),
        ],
        [pl.BlockSpec((rows, features), lambda t: (t, 0)), pl.BlockSpec((8, features), lambda t: (0, 0))],
        [jax.ShapeDtypeStruct(x.shape, BF16), jax.ShapeDtypeStruct((8, features), F32)],
        14, grid=(4,),
    )


def project_kernel(x_ref, gain_ref, w_ref, normed_ref, pre_ref):
    x = x_ref[...].astype(F32)
    ratio = lax.rsqrt(jnp.mean(x * x, axis=1, keepdims=True) + EPSILON)
    normed = (x * ratio * gain_ref[...]).astype(BF16)
    normed_ref[...] = normed
    for f in range(2):
        pre_ref[f] = dot(normed, w_ref[f], NN)


def project(x, gain, w, moves, collective):
    tokens, features = x.shape
    rows, columns = tokens // 4, w.shape[2]
    some = pl.BlockSpec((rows, features), lambda t: (t, 0))
    return compute(
        project_kernel, "project", (x, gain, w),
        [some, pl.BlockSpec((1, features), lambda t: (0, 0)), pl.BlockSpec(w.shape, lambda t: (0, 0, 0))],
        [some, pl.BlockSpec((2, rows, columns), lambda t: (0, t, 0))],
        [jax.ShapeDtypeStruct(x.shape, BF16), jax.ShapeDtypeStruct((2, tokens, columns), F32)],
        28, grid=(4,), moves=moves, collective=collective,
    )


def hidden_rows_kernel(planes, a_ref, gate_ref, up_ref):
    piece = gate_ref.shape[1] // (8 * planes)
    for core in range(2):
        for chip in range(4):
            block = a_ref[core, chip].astype(F32)
            for n, out_ref in enumerate((gate_ref, up_ref)):
                for z in range(planes):
                    start = ((z * 4 + chip) * 2 + core) * piece
                    out_ref[:, start:start + piece] = block[:, (n * planes + z) * piece:(n * planes + z + 1) * piece]


def hidden_rows(a, columns):
    rows = a.shape[2]
    in_vmem = pl.BlockSpec(memory_space=pltpu.VMEM)
    return compute(
        functools.partial(hidden_rows_kernel, lax.axis_size("z")), "hidden_rows", (a,), [in_vmem], [in_vmem] * 2,
        [jax.ShapeDtypeStruct((rows, columns), F32)] * 2, 6,
    )


def gather_planes(a):
    return lax.all_gather(a, ("c", "z"), axis=0, tiled=True).reshape((2, -1) + a.shape[1:])


def sum_planes(a):
    return lax.psum_scatter(a.reshape((-1,) + a.shape[2:]), ("z", "c"), scatter_dimension=0, tiled=True)[0]


def swap(a, axis):
    return lax.ppermute(a, axis, [(0, 1), (1, 0)])


def both_of(a, axis):
    other = swap(a, axis)
    return jnp.where(lax.axis_index(axis) == 0, jnp.stack([a, other]), jnp.stack([other, a]))


def scaled(features):
    return lax.rsqrt(jnp.mean(features * features, axis=-1, keepdims=True) + EPSILON)


def norm_back(grad, gain, features, ratio):
    u, xh = grad * gain, features * ratio
    return ratio * (u - xh * jnp.mean(u * xh, axis=-1, keepdims=True))


def body(inputs, starts, norm_attn, w_query, w_key, w_value, w_forget, gate_bias, w_out, norm_ffn, w_gate, w_up,
         w_down, cotangent):
    positions, features = inputs.shape[1:]
    depth = features // HEADS
    y, x, c, z = (lax.axis_index(name) for name in ("y", "x", "c", "z"))
    planes = lax.axis_size("z")
    head = y * 2 + x
    rows_here = w_query.shape[0]
    hidden_here = w_down.shape[0]

    def own_half(a, axis, at=c):
        return lax.dynamic_index_in_dim(a, at, axis, keepdims=False)

    bias_here = gate_bias.shape[0]

    def column(v):
        v = jnp.pad(v, (0, rows_here - v.shape[0]))
        return jnp.broadcast_to(v[None, :, None], (HEADS, rows_here, 1))

    forget = own_half(w_forget.reshape(rows_here, HEADS, 2, SLOTS // 2), 2).transpose(1, 0, 2)
    rest = jnp.concatenate([forget] + [column(v) for v in (norm_attn, norm_ffn, gate_bias)], axis=-1)
    rest = jnp.pad(rest, ((0, 0), (0, 0), (0, TILE - rest.shape[-1])))
    vectors = 3 * depth // 2 + SLOTS // 2
    width = vectors + 3

    x_here = inputs.reshape(positions, features)
    cot_here = cotangent.reshape(positions, features)
    out_half = own_half(w_out.reshape(2, rows_here // 2, features), 0)
    out_half = lax.all_gather(out_half, "z", axis=0)
    full_down = gather_planes(own_half(w_down.reshape(2, hidden_here // 2, features), 0))
    begins, x_rows, hidden_w, mixer_w = start_moves(
        1, (w_query, w_key, w_value), rest, w_gate, w_up,
        (("copy_homes", jnp.broadcast_to(starts, (8, positions))), ("copy_homes", x_here)),
    )
    hidden_w = gather_planes(hidden_w.reshape(4 * rows_here, -1))
    mixer_w = mixer_w.reshape(2, features, -1)
    gain_attn, gain_ffn = (mixer_w[0, :, vectors + i].astype(F32) for i in range(2))
    bias = mixer_w[0, :, vectors + 2].reshape(4 * planes, rows_here)[:, :bias_here].reshape(-1).astype(F32)
    bias = lax.dynamic_slice_in_dim(bias, head * SLOTS, SLOTS)
    doc = jnp.cumsum(begins[:, 0].reshape(2, 2 * positions).astype(F32), axis=1)

    x_rows = x_rows.reshape(4 * positions, features)
    normed, pre, out_core = project(x_rows, gain_attn[None], mixer_w, [("copy_chips", out_half)], 13)
    z_total = pre[:, :, 3 * depth // 2:vectors].reshape(2, 2, 2 * positions, SLOTS // 2)
    z_total = z_total.transpose(2, 1, 0, 3).reshape(2 * positions, 2 * SLOTS) + jnp.tile(bias, 2)
    log_forget = jax.nn.log_sigmoid(z_total) / 8.0
    gain = -jnp.expm1(log_forget)
    mixed, scores, probs, paired, out_other, cot = mix_forward(
        pre, log_forget, gain, doc, [("swap_core", out_core), ("gather_near", cot_here)], 3
    )
    out_core, out_other = (a.reshape(features // 2, features) for a in (out_core, out_other))
    mixed_own = own_half(mixed, 1)
    mixed, mixed_other = move(
        4, ("to_homes", mixed.reshape(4, 2 * positions, depth // 2)), ("swap_core", own_half(mixed, 1, 1 - c)), us=14
    )
    mixed = mixed.reshape(2 * HEADS, positions, depth // 2).transpose(1, 0, 2)
    mixed = mixed.reshape(positions, planes, 4, 2, rows_here // 2).transpose(3, 0, 2, 1, 4)
    mixed = mixed.reshape(2, positions, features // 2)
    attended = (
        x_here.astype(F32) + jnp.dot(own_half(mixed, 0), out_core, preferred_element_type=F32)
        + jnp.dot(own_half(mixed, 0, 1 - c), out_other, preferred_element_type=F32)
    )

    ratio_f = scaled(attended)
    (normed_ffn,) = move(5, ("copy_chips", (attended * ratio_f * gain_ffn).astype(BF16)), us=38)
    normed_ffn = normed_ffn.reshape(4 * positions, features)
    hidden, slopes, silus, cot = hidden_units(normed_ffn, hidden_w, [("gather_far", cot)], 6)
    cot = cot.reshape(4 * positions, features)
    grad_down_w = down_grads(hidden, cot)
    grad_hidden, shares = hidden_grads(cot, slopes, silus, hidden_w, full_down)
    shares = shares.reshape(2, 2, positions, features)
    grad_hidden_w, near = weight_grads(
        normed_ffn, grad_hidden, 24, [("reduce_near", shares.reshape(4, positions, features))], 7
    )
    half = positions // 2
    own = [
        lax.dynamic_index_in_dim(shares[:, :, :half], x, 1, keepdims=False),
        lax.dynamic_index_in_dim(shares[:, :, half:], y, 0, keepdims=False),
    ]
    own = [jnp.where(at == 0, a[::-1], a) for at, a in zip((y, x), own)]
    near = jnp.stack(own).astype(F32) + near.astype(F32)
    block_out, far = block_outputs(hidden, full_down, [("reduce_far", near[:, 0].astype(BF16))], 8)
    grad_normed_ffn = (near[:, 1] + far.astype(F32)).reshape(positions, features)
    grad_down_w, grad_hidden_w = sum_planes(grad_down_w), sum_planes(grad_hidden_w)
    grad_gain_ffn = jnp.sum(grad_normed_ffn * attended * ratio_f, axis=0)
    grad_attended = cot_here.astype(F32) + norm_back(grad_normed_ffn, gain_ffn, attended, ratio_f)

    grad_branch = grad_attended.astype(BF16)
    grad_mixed = [
        jnp.einsum("te,de->td", grad_branch, w, preferred_element_type=F32).astype(BF16) for w in (out_core, out_other)
    ]
    grad_mixed = jnp.where(c == 0, jnp.stack(grad_mixed), jnp.stack(grad_mixed[::-1]))
    grad_mixed = grad_mixed.reshape(2, positions, 4, planes, rows_here // 2).transpose(1, 3, 2, 0, 4)
    grad_mixed = grad_mixed.reshape(positions, HEADS, 2, depth // 2).transpose(1, 2, 0, 3)
    (grad_mixed,) = move(
        9, ("from_homes", grad_mixed.reshape(4, 2 * positions, depth // 2)), after=(grad_down_w,), us=14
    )
    grad_mixed = grad_mixed.reshape(2, 2, 2, positions, depth // 2)
    rate = jax.nn.sigmoid(-z_total) / 8.0
    grad_pre, grad_bias, branch_chips = mix_backward(
        pre, grad_mixed, log_forget, gain, rate, doc, scores, probs, paired, [("copy_chips", grad_branch)], 10
    )
    grad_bias = jnp.sum(grad_bias[0].reshape(2, SLOTS), axis=0)
    grad_out_w = out_grads(mixed_own, mixed_other, branch_chips)
    grad_normed, sums = input_grads(grad_pre, mixer_w, x_rows)
    grad_bias = jnp.zeros((HEADS, SLOTS), F32).at[head].set(grad_bias).reshape(4 * planes, bias_here)
    grad_bias = jnp.pad(grad_bias, ((0, 0), (0, rows_here - bias_here))).reshape(-1)
    sums = jnp.stack([jnp.sum(sums, axis=0), grad_gain_ffn, grad_bias], axis=-1)
    first_sum = vectors + TILE - mixer_w.shape[-1]
    sums = jnp.pad(sums, ((0, 0), (first_sum, TILE - first_sum - 3)))
    grad_mixer_w, grad_hidden_w = mixer_weight_grads(
        normed, grad_pre, sums, [("spread", grad_hidden_w.reshape(1, 4, rows_here, -1))], 14
    )
    grad_out_w = sum_planes(grad_out_w)
    grad_gate_w, grad_up_w = hidden_rows(grad_hidden_w[:, :, 0], w_gate.shape[1])
    *grad_w, rest, grad_out_w, grad_input, output = end_moves(
        11, grad_mixer_w, grad_normed.reshape(4, positions, features), block_out.reshape(4, positions, features),
        grad_out_w, grad_attended, x_here, gain_attn[None], attended,
    )

    columns = SLOTS // 2
    sums = jnp.sum(rest[0, :, :, columns:columns + 3], axis=0)
    grad_forget_w = rest[..., :columns].transpose(2, 1, 0, 3).reshape(rows_here, HEADS * SLOTS)
    grad_down_w = both_of(grad_down_w, "c").reshape(hidden_here, features).astype(F32)
    return (
        output.reshape(inputs.shape), grad_input.reshape(inputs.shape), sums[:, 0], grad_w[0], grad_w[1], grad_w[2],
        grad_forget_w, sums[:bias_here, 2], grad_out_w, sums[:, 1], grad_gate_w, grad_up_w, grad_down_w,
    )


def solution(mesh):
    planes = mesh.shape["dp"] // 4
    fine = Mesh(mesh.devices.reshape(planes, 2, 2, 2), ("z", "y", "x", "c"))
    dp = ("z", "y", "x")
    tokens, vector, matrix = P(dp, "c", None), P(dp), P(dp, None)
    in_specs = (
        tokens, P(dp, "c"), vector, matrix, matrix, matrix, matrix, vector, matrix, vector, matrix, matrix, matrix, tokens
    )
    out_specs = (
        tokens, tokens, vector, matrix, matrix, matrix, matrix, vector, matrix, vector, matrix, matrix, matrix
    )
    return jax.shard_map(body, mesh=fine, in_specs=in_specs, out_specs=out_specs, check_vma=False)
```

```python
import functools

import jax
import jax.numpy as jnp
from jax import lax
from jax.sharding import Mesh
from jax.sharding import PartitionSpec as P
from jax.experimental import pallas as pl
from jax.experimental.pallas import tpu as pltpu

HEADS = 4
SLOTS = 64
DEPTH = 512
TILE = 128
EPSILON = 1e-06
F32, BF16 = jnp.float32, jnp.bfloat16
NN = (((1,), (0,)), ((), ()))
NT = (((1,), (1,)), ((), ()))
TN = (((0,), (0,)), ((), ()))
HALVES = (64, 32, 16, 8, 4, 2, 1)
MESH = pl.DeviceIdType.MESH


def cost(us):
    return pl.CostEstimate(flops=0, bytes_accessed=us * 3_000_000, transcendentals=0)


def routes(kind, i, y, x, c):
    chip = {"y": i // 2 % 2, "x": i % 2}
    if kind == "to_homes":
        return {"y": c, "x": i // 2, "c": i % 2}, {**chip, "c": y}, y * 2 + x
    if kind in ("from_homes", "copy_homes"):
        return {**chip, "c": y}, {"y": c, "x": i // 2, "c": i % 2}, x * 2 + c
    return {**chip, "c": c}, {**chip, "c": c}, y * 2 + x


def enter_plane(y, x, c, more=(), greeted=0):
    barrier = pltpu.get_barrier_semaphore()
    peers = list(more)
    for flip in range(1, 8):
        peers.append({
            "y": lax.rem(y + flip // 4, 2), "x": lax.rem(x + (flip // 2) % 2, 2), "c": lax.rem(c + flip % 2, 2)
        })
    for peer in peers:
        pl.semaphore_signal(barrier, inc=1, device_id=peer, device_id_type=MESH)
    pl.semaphore_wait(barrier, len(peers) + greeted)


def swap_kernel_sems(count):
    return [pltpu.SemaphoreType.DMA((count,)), pltpu.SemaphoreType.DMA((count,))]


def remote(source, target, send, recv, peer):
    return pltpu.make_async_remote_copy(
        src_ref=source, dst_ref=target, send_sem=send, recv_sem=recv, device_id=peer, device_id_type=MESH
    )


class Stay:
    def __init__(self, source, target, sem, buffer):
        self.load = pltpu.make_async_copy(source, buffer, sem)
        self.store = pltpu.make_async_copy(buffer, target, sem)

    def start(self):
        self.load.start()
        self.load.wait()
        self.store.start()

    def wait(self):
        self.store.wait()


class GatherNear:
    def __init__(self, a_ref, out_ref, y, x, send, recv, *local):
        to_x, to_y = {"x": 1 - x}, {"y": 1 - y}
        here = y * 2 + x
        parts = halves_at(a_ref.shape[0])

        def copy(part, n, peer):
            return remote(a_ref.at[parts[part]], out_ref.at[here, parts[part]], send.at[n], recv.at[n], peer)

        self.own = Stay(a_ref, out_ref.at[here], *local)
        self.first, self.second = [copy(0, 0, to_x), copy(1, 1, to_y)], [copy(1, 2, to_x), copy(0, 3, to_y)]
        self.all = self.first + self.second

    def start(self):
        for copy in self.all + [self.own]:
            copy.start()

    def wait(self):
        for copy in self.all:
            copy.wait()
        self.own.wait()


class GatherFar:
    def __init__(self, out_ref, y, x, send, recv):
        at_x, at_y = y * 2 + 1 - x, (1 - y) * 2 + x
        parts = halves_at(out_ref.shape[1])

        def copy(place, part, n, peer):
            block = out_ref.at[place, parts[part]]
            return remote(block, block, send.at[n], recv.at[n], peer)

        self.all = [copy(at_x, 0, 0, {"y": 1 - y}), copy(at_y, 1, 1, {"x": 1 - x})]

    def start(self):
        for copy in self.all:
            copy.start()

    def wait(self):
        for copy in self.all:
            copy.wait()


def halves_at(rows):
    return [pl.ds(0, rows // 2), pl.ds(rows // 2, rows // 2)]


class Gather:
    def __init__(self, a_ref, out_ref, y, x, send, recv, *local):
        self.near = GatherNear(a_ref, out_ref, y, x, send, recv, *local)
        self.far = GatherFar(out_ref, y, x, send.at[pl.ds(4, 2)], recv.at[pl.ds(4, 2)])

    def start(self):
        self.near.start()

    def wait(self):
        for copy, onward in zip(self.near.first, self.far.all):
            copy.wait_recv()
            onward.start()
        for copy in self.near.second + self.far.all:
            copy.wait_recv()
        for copy in self.near.all + self.far.all:
            copy.wait_send()
        self.near.own.wait()


class ReduceNear:
    def __init__(self, a_ref, out_ref, y, x, send, recv):
        parts = halves_at(a_ref.shape[1])
        self.all = []
        for i, (at_y, at_x) in enumerate(((1 - y, 1 - x), (y, x))):
            blocks = (at_y * 2 + 1 - x, (1 - y) * 2 + at_x)
            for part, peer in enumerate(({"x": 1 - x}, {"y": 1 - y})):
                n = 2 * part + i
                self.all.append(
                    remote(a_ref.at[blocks[part], parts[part]], out_ref.at[part, i], send.at[n], recv.at[n], peer)
                )

    def start(self):
        for copy in self.all:
            copy.start()

    def wait(self):
        for copy in self.all:
            copy.wait()


class ReduceFar:
    def __init__(self, a_ref, out_ref, y, x, send, recv):
        self.all = [
            remote(a_ref.at[n], out_ref.at[n], send.at[n], recv.at[n], peer)
            for n, peer in enumerate(({"y": 1 - y}, {"x": 1 - x}))
        ]

    def start(self):
        for copy in self.all:
            copy.start()

    def wait(self):
        for copy in self.all:
            copy.wait()


def home_of_rows(y, x, z, planes):
    chip = y * 2 + x
    here = z * 4 + chip
    return here, chip * planes + z, lax.rem(here, planes) * 4 + here // planes


def device(block, core):
    return {"z": block // 4, "y": lax.rem(block, 4) // 2, "x": lax.rem(block, 2), "c": core}


def greet_homes(y, x, c, z, planes):
    here, goal, origin = home_of_rows(y, x, z, planes)

    @pl.when(goal != here)
    def _():
        for block in (goal, origin):
            pl.semaphore_signal(
                pltpu.get_barrier_semaphore(), inc=1, device_id=device(block, c), device_id_type=MESH
            )

    return jnp.where(goal != here, 2, 0)


class Swap:
    def __init__(self, a_ref, out_ref, c, send, recv):
        self.copy = remote(a_ref, out_ref, send.at[0], recv.at[0], {"c": 1 - c})

    def start(self):
        self.copy.start()

    def wait(self):
        self.copy.wait()


class Moves:
    def __init__(self, kind, source, target, y, x, c, send, recv, *local):
        self.copies = []
        for i in range(4):
            peer, giver, slot = routes(kind, i, y, x, c)
            to_me, from_me = (
                (at["y"] == y) & (at["x"] == x) & (at["c"] == c) for at in (peer, giver)
            )
            self.copies.append((
                to_me, from_me,
                Stay(source(i), target(slot), *local),
                remote(source(i), target(slot), send.at[i], recv.at[slot], peer),
                Stay(source(i), target(i), *local),
                remote(source(i), target(i), send.at[i], recv.at[i], peer),
            ))

    def start(self):
        for to_me, _, _, there, _, _ in self.copies:
            pl.when(jnp.logical_not(to_me))(there.start)
        for to_me, _, here, _, _, _ in self.copies:
            pl.when(to_me)(here.start)

    def wait(self):
        for to_me, from_me, _, _, here, there in self.copies:
            pl.when(jnp.logical_not(to_me))(there.wait_send)
            pl.when(jnp.logical_not(from_me))(there.wait_recv)
            pl.when(from_me)(here.wait)


class Spread:
    def __init__(self, a_ref, out_ref, y, x, c, send, recv, *local):
        here, other = y * 2 + x, {"c": 1 - c}
        self.own = Stay(a_ref.at[:, here], out_ref.at[c, here], *local)
        self.across = [remote(a_ref.at[:, here], out_ref.at[c, here], send.at[0], recv.at[0], other)]
        self.sent = []
        for flip in (1, 2, 3):
            peer = {"y": lax.rem(y + flip // 2, 2), "x": lax.rem(x + flip % 2, 2)}
            chip = peer["y"] * 2 + peer["x"]
            self.sent.append(remote(a_ref.at[:, chip], out_ref.at[c, here], send.at[flip], recv.at[flip], peer))
            self.across.append(
                remote(out_ref.at[c, chip], out_ref.at[c, chip], send.at[3 + flip], recv.at[3 + flip], other)
            )

    def start(self):
        for copy in self.sent + [self.across[0], self.own]:
            copy.start()

    def wait(self):
        for copy, onward in zip(self.sent, self.across[1:]):
            copy.wait_recv()
            onward.start()
        for copy in self.across:
            copy.wait()
        for copy in self.sent:
            copy.wait_send()
        self.own.wait()


def move_scratch(kind, a):
    sems = swap_kernel_sems({"spread": 7, "copy_chips": 6}.get(kind, 4)) + [pltpu.SemaphoreType.DMA]
    if kind in ("copy_homes", "copy_chips", "gather_near", "keep"):
        block = a.shape
    elif kind == "spread":
        block = a.shape[:1] + a.shape[2:]
    else:
        block = a.shape[1:] if kind in ("to_homes", "from_homes", "columns") else (16, TILE)
    return sems + [pltpu.VMEM(block, a.dtype)]


def moved(kind, a):
    if kind == "spread":
        return jax.ShapeDtypeStruct((2, 4, a.shape[0]) + a.shape[2:], a.dtype)
    if kind == "reduce_near":
        return jax.ShapeDtypeStruct((2, 2, a.shape[1] // 2) + a.shape[2:], a.dtype)
    if kind == "swap_half":
        return jax.ShapeDtypeStruct(a.shape[:1] + a.shape[2:], a.dtype)
    if kind in ("swap_core", "keep", "gather_far", "reduce_far"):
        return jax.ShapeDtypeStruct(a.shape, a.dtype)
    block = a.shape if kind in ("copy_homes", "copy_chips", "gather_near") else a.shape[1:]
    return jax.ShapeDtypeStruct((4,) + block, a.dtype)


def one_move(kind, a_ref, out_ref, y, x, c, *sems):
    if kind == "spread":
        return Spread(a_ref, out_ref, y, x, c, *sems)
    if kind == "copy_chips":
        return Gather(a_ref, out_ref, y, x, *sems)
    if kind == "gather_near":
        return GatherNear(a_ref, out_ref, y, x, *sems)
    if kind == "gather_far":
        return GatherFar(out_ref, y, x, *sems[:2])
    if kind in ("reduce_near", "reduce_far"):
        return (ReduceNear if kind == "reduce_near" else ReduceFar)(a_ref, out_ref, y, x, *sems[:2])
    if kind == "swap_core":
        return Swap(a_ref, out_ref, c, *sems[:2])
    if kind == "swap_half":
        return Swap(a_ref.at[:, 1 - c], out_ref, c, *sems[:2])
    if kind == "keep":
        return Stay(a_ref, out_ref, *sems[2:])

    def source(i):
        return a_ref if kind == "copy_homes" else a_ref.at[i]

    return Moves(kind, source, lambda slot: out_ref.at[slot], y, x, c, *sems)


def all_moves(kinds, sources, results, sems, y, x, c):
    return [one_move(kind, sources[n], results[n], y, x, c, *sems[4 * n:4 * n + 4]) for n, kind in enumerate(kinds)]


def compute_body(counts, kinds, grid, body, *refs):
    refs, parts = list(refs), []
    for count in counts:
        parts.append(refs[:count])
        refs = refs[count:]
    operands, sources, _, outs, results, scratch, sems = parts
    if kinds:
        y, x, c = (lax.axis_index(name) for name in ("y", "x", "c"))
        moves = all_moves(kinds, sources, results, sems, y, x, c)
        first, last = True, True
        for axis, size in enumerate(grid):
            first, last = first & (pl.program_id(axis) == 0), last & (pl.program_id(axis) == size - 1)

        def start():
            enter_plane(y, x, c)
            for one in moves:
                one.start()

        def finish():
            for one in moves:
                one.wait()

        pl.when(first)(start) if grid else start()
    body(*operands, *outs, *scratch)
    if kinds:
        pl.when(last)(finish) if grid else finish()


def compute(body, name, operands, in_specs, out_specs, out_shape, us, grid=(), scratch=(), moves=(), collective=None, after=()):
    any_place = pl.BlockSpec(memory_space=pl.ANY)
    kinds = tuple(kind for kind, _ in moves)
    sems = [sem for kind, a in moves for sem in move_scratch(kind, a)]
    counts = (len(operands), len(moves), len(after), len(out_shape), len(moves), len(scratch), len(sems))
    params = {"collective_id": collective, "has_side_effects": True} if moves else {}
    aliases = {len(operands) + n: len(out_shape) + n for n, kind in enumerate(kinds) if kind == "gather_far"}
    return pl.pallas_call(
        functools.partial(compute_body, counts, kinds, grid, body),
        name=name,
        grid=grid,
        in_specs=list(in_specs) + [any_place] * (len(moves) + len(after)),
        out_specs=list(out_specs) + [any_place] * len(moves),
        out_shape=list(out_shape) + [moved(kind, a) for kind, a in moves],
        scratch_shapes=list(scratch) + sems,
        input_output_aliases=aliases,
        compiler_params=pltpu.CompilerParams(vmem_limit_bytes=60 << 20, **params),
        cost_estimate=cost(us),
    )(*operands, *(a for _, a in moves), *after)


def move_kernel(kinds, waits, *refs):
    count = len(kinds)
    sources, results, sems = refs[:count], refs[count + waits:2 * count + waits], refs[2 * count + waits:]
    y, x, c = (lax.axis_index(name) for name in ("y", "x", "c"))
    enter_plane(y, x, c)
    moves = all_moves(kinds, sources, results, sems, y, x, c)
    for one in moves:
        one.start()
    for one in moves:
        one.wait()


def move(collective, *items, after=(), us=48):
    kinds = tuple(kind for kind, _ in items)
    any_place = pl.BlockSpec(memory_space=pl.ANY)
    return pl.pallas_call(
        functools.partial(move_kernel, kinds, len(after)),
        name=kinds[0],
        out_shape=[moved(kind, a) for kind, a in items],
        in_specs=[any_place] * (len(items) + len(after)),
        out_specs=[any_place] * len(items),
        scratch_shapes=[sem for kind, a in items for sem in move_scratch(kind, a)],
        compiler_params=pltpu.CompilerParams(collective_id=collective, has_side_effects=True),
        cost_estimate=cost(us),
    )(*(a for _, a in items), *after)


def hidden_columns(core, planes, weights, out_ref):
    for chip in range(4):
        pieces = []
        for w_ref in weights:
            piece = w_ref.shape[1] // (8 * planes)
            for z in range(planes):
                start = (z * 4 + chip) * 2 * piece
                both = w_ref[:, start:start + 2 * piece].astype(F32)
                pieces.append(jnp.where(core == 0, both[:, :piece], both[:, piece:]))
        out_ref[chip] = jnp.concatenate(pieces, axis=1).astype(BF16)


def start_kernel(kinds, planes, *refs):
    count = len(kinds)
    projections, rest_ref, gate_ref, up_ref, sources = refs[:3], refs[3], refs[4], refs[5], refs[6:6 + count]
    results, h_ref, m_ref = refs[6 + count:6 + 2 * count], refs[6 + 2 * count], refs[7 + 2 * count]
    hidden_ref, gate_room, up_room, load, *sems = refs[8 + 2 * count:]
    y, x, c, z = (lax.axis_index(name) for name in ("y", "x", "c", "z"))
    up, down = lax.rem(z + 1, planes), lax.rem(z + planes - 1, planes)
    wide = DEPTH // 2
    loads = [
        pltpu.make_async_copy(w_ref, room, load.at[n]) for n, (w_ref, room) in enumerate(((gate_ref, gate_room), (up_ref, up_room)))
    ]
    for copy in loads:
        copy.start()
    enter_plane(y, x, c, [{"z": up}, {"z": down}])
    moves = all_moves(kinds, sources, results, sems, y, x, c)
    sems = sems[4 * count:]
    moves.append(one_move("columns", hidden_ref, h_ref, y, x, c, *sems[:4]))
    sems = sems[4:]

    def part(n, source, columns):
        return Moves(
            "columns", source, lambda slot: m_ref.at[c, z, slot, :, columns], y, x, c, *sems[4 * n:4 * n + 4]
        )

    def columns_of(w_ref):
        return lambda i: w_ref.at[:, pl.ds(pl.multiple_of((2 * i + c) * wide, wide), wide)]

    parts = [part(n, columns_of(w_ref), pl.ds(n * wide, wide)) for n, w_ref in enumerate(projections)]
    parts.append(part(3, lambda i: rest_ref.at[i], pl.ds(3 * wide, TILE)))
    m_send, m_recv, core_send, core_recv = sems[16:]

    def block(step):
        return m_ref.at[c, lax.rem(z + planes - step, planes)]

    ring = [
        remote(block(step), block(step), m_send.at[step], m_recv.at[step], {"z": up}) for step in range(planes - 1)
    ]
    across = [
        remote(block(step), block(step), core_send.at[step], core_recv.at[step], {"c": 1 - c}) for step in range(planes)
    ]
    for one in parts:
        one.start()
    for copy in loads:
        copy.wait()
    hidden_columns(c, planes, (gate_room, up_room), hidden_ref)
    for one in parts:
        one.wait()
    ring[0].start()
    across[0].start()
    for one in moves:
        one.start()
    for step in range(planes - 1):
        ring[step].wait_recv()
        if step < planes - 2:
            ring[step + 1].start()
        across[step + 1].start()
    for one in moves:
        one.wait()
    for copy in across:
        copy.wait()
    for copy in ring:
        copy.wait_send()


def start_moves(collective, projections, rest, gate, up, items):
    planes = lax.axis_size("z")
    kinds = tuple(kind for kind, _ in items)
    any_place = pl.BlockSpec(memory_space=pl.ANY)
    shapes = [moved(kind, a) for kind, a in items]
    hidden = jax.ShapeDtypeStruct((4, gate.shape[0], gate.shape[1] // 4), BF16)
    shapes.append(hidden)
    shapes.append(jax.ShapeDtypeStruct((2, planes, 4, rest.shape[1], 3 * DEPTH // 2 + TILE), BF16))
    sems = [pltpu.VMEM(hidden.shape, BF16), pltpu.VMEM(gate.shape, BF16), pltpu.VMEM(up.shape, BF16), pltpu.SemaphoreType.DMA((2,))]
    sems += [sem for kind, a in items for sem in move_scratch(kind, a)] + move_scratch("columns", hidden)
    part = jax.ShapeDtypeStruct((4, rest.shape[1], DEPTH // 2), BF16)
    sems += [sem for a in (part, part, part, rest) for sem in move_scratch("columns", a)]
    sems += swap_kernel_sems(planes) + swap_kernel_sems(planes)
    return pl.pallas_call(
        functools.partial(start_kernel, kinds, planes),
        name="start_moves",
        out_shape=shapes,
        in_specs=[any_place] * (6 + len(items)),
        out_specs=[any_place] * len(shapes),
        scratch_shapes=sems,
        compiler_params=pltpu.CompilerParams(collective_id=collective, has_side_effects=True, vmem_limit_bytes=60 << 20),
        cost_estimate=cost(85),
    )(*projections, rest, gate, up, *(a for _, a in items))


class PlaneSum:
    def __init__(self, a_ref, rooms, y, x):
        self.near_ref, self.onward_ref, self.far_ref, *sems = rooms
        self.near = ReduceNear(a_ref, self.near_ref, y, x, *sems[:2])
        self.far = ReduceFar(self.onward_ref, self.far_ref, y, x, *sems[2:])

    def start(self):
        self.near.start()

    def go_on(self, own):
        self.near.wait()
        for part in range(2):
            self.onward_ref[part] = (own(part, 0).astype(F32) + self.near_ref[part, 0].astype(F32)).astype(BF16)
        self.far.start()

    def total(self, own, part, some):
        return (
            own(part, 1)[some, :].astype(F32) + self.near_ref[part, 1, some, :].astype(F32)
            + self.far_ref[part, some, :].astype(F32)
        )


def sum_rooms(rows, features):
    half = (rows // 2, features)
    sem = pltpu.SemaphoreType.DMA
    return [
        pltpu.VMEM((2, 2) + half, BF16), pltpu.VMEM((2,) + half, BF16), pltpu.VMEM((2,) + half, BF16),
        sem((4,)), sem((4,)), sem((2,)), sem((2,)),
    ]


def end_kernel(planes, g_ref, gn_ref, block_ref, w_ref, grad_attended_ref, x_ref, gain_ref, attended_ref, *refs):
    land_ref, w_land_ref, grad_ref, output_ref, refs = *refs[:4], refs[4:]
    own_ref, core_ref, ring_ref, sum_ref, shares_ref, mine_ref, refs = *refs[:6], refs[6:]
    load, core_send, core_recv, ring_send, ring_recv, spread_send, spread_recv, w_send, w_recv, local = refs[:10]
    mine_load, shares_load, shares_send, shares_recv, *rooms = refs[10:]
    y, x, c, z = (lax.axis_index(name) for name in ("y", "x", "c", "z"))
    chip, other = y * 2 + x, {"c": 1 - c}
    up, down = {"z": lax.rem(z + 1, planes)}, {"z": lax.rem(z + planes - 1, planes)}
    here, goal, _ = home_of_rows(y, x, z, planes)
    enter_plane(y, x, c, [up, down], greet_homes(y, x, c, z, planes))
    rows = own_ref.shape[1]
    half, size = rows // 2, rows // 4
    parts = [pl.ds(0, half), pl.ds(half, half)]
    blocks = [[(1 - y) * 2 + x, chip], [y * 2 + 1 - x, chip]]
    token_parts = halves_at(block_ref.shape[1])

    def place(step):
        return lax.rem(z + 2 * planes - 1 - step, planes)

    loads = [pltpu.make_async_copy(g_ref.at[place(s), c], own_ref.at[s], load.at[s]) for s in range(planes)]
    across = [
        [
            remote(
                g_ref.at[place(s), 1 - c, parts[part]], core_ref.at[s, parts[part]], core_send.at[s, part],
                core_recv.at[s, part], other,
            ) for part in range(2)
        ] for s in range(planes)
    ]
    shares_across = [
        remote(gn_ref.at[2 * i + 1 - c], shares_ref.at[2 * c + i], shares_send.at[i], shares_recv.at[i], other)
        for i in range(2)
    ]
    shares_own = [
        pltpu.make_async_copy(gn_ref.at[2 * i + c], shares_ref.at[2 * c + i], shares_load.at[i]) for i in range(2)
    ]
    mine = [
        pltpu.make_async_copy(
            block_ref.at[blocks[part][i], token_parts[part]], mine_ref.at[part, i], mine_load.at[2 * part + i]
        ) for part in range(2) for i in range(2)
    ]
    out_sum = PlaneSum(block_ref, rooms[:7], y, x)
    in_sum = PlaneSum(shares_ref, rooms[7:], y, x)
    for copy in across[0] + loads[:1]:
        copy.start()
    out_sum.start()
    w_stay = pltpu.make_async_copy(w_ref, w_land_ref.at[c], local.at[0])
    w_sent = remote(w_ref, w_land_ref.at[c], w_send.at[0], w_recv.at[0], device(goal, c))
    w_passed = remote(w_land_ref.at[c], w_land_ref.at[c], w_send.at[1], w_recv.at[1], other)
    pl.when(goal == here)(w_stay.start)

    def ring(s, part):
        return remote(
            sum_ref.at[s, parts[part]], ring_ref.at[s, parts[part]], ring_send.at[s, part], ring_recv.at[s, part], up
        )

    def out_own(part, i):
        return mine_ref.at[part, i][...]

    def in_own(part, i):
        return shares_ref[blocks[part][i], token_parts[part], :]

    tokens = output_ref.shape[0] // 2
    every = slice(0, tokens)
    for s in range(planes):
        loads[s].wait()
        for part in range(2):
            across[s][part].wait_recv()
            total = own_ref[s, parts[part], :].astype(F32) + core_ref[s, parts[part], :].astype(F32)
            if s > 0:
                ring(s - 1, part).wait_recv()
                total = total + ring_ref[s - 1, parts[part], :].astype(F32)
            sum_ref[s, parts[part], :] = total.astype(BF16)
            if s < planes - 1:
                ring(s, part).start()
        if s == 0:
            for n in range(1, planes):
                for part in range(2):
                    across[n][part].start()
                loads[n].start()
            for copy in shares_across + shares_own + mine:
                copy.start()
            for copy in shares_across:
                copy.wait_recv()
            for copy in shares_own:
                copy.wait()
            in_sum.start()
        if s == 1:
            for copy in mine:
                copy.wait()
            out_sum.go_on(out_own)
            pl.when(goal != here)(w_sent.start)
        if s == planes - 2:
            in_sum.go_on(in_own)

    sent, passed = [], []
    for flip in range(4):
        peer = {"y": lax.rem(y + flip // 2, 2), "x": lax.rem(x + flip % 2, 2)}
        at = peer["y"] * 2 + peer["x"]
        some = sum_ref.at[planes - 1, pl.ds(pl.multiple_of(at * size, size), size)]
        if flip:
            sent.append(remote(some, land_ref.at[c, chip], spread_send.at[flip], spread_recv.at[flip], peer))
            sent[-1].start()
        source = land_ref.at[c, at] if flip else some
        passed.append(remote(source, land_ref.at[c, at], spread_send.at[4 + flip], spread_recv.at[4 + flip], other))
    passed[0].start()
    stay = pltpu.make_async_copy(
        sum_ref.at[planes - 1, pl.ds(pl.multiple_of(chip * size, size), size)], land_ref.at[c, chip], local.at[1]
    )
    stay.start()
    out_sum.far.wait()
    for part in range(2):
        here_rows = slice(part * tokens, (part + 1) * tokens)
        output_ref[here_rows, :] = (attended_ref[here_rows, :] + out_sum.total(out_own, part, every)).astype(BF16)
    pl.when(goal == here)(w_stay.wait)
    pl.when(goal != here)(w_sent.wait)
    w_passed.start()
    for copy, onward in zip(sent, passed[1:]):
        copy.wait_recv()
        onward.start()
    in_sum.far.wait()
    for part in range(2):
        here_rows = slice(part * tokens, (part + 1) * tokens)
        input_back(in_sum.total(in_own, part, every), here_rows, grad_attended_ref, x_ref, gain_ref, grad_ref)
    for copy in passed:
        copy.wait_recv()
    w_passed.wait()
    stay.wait()
    for copy in sent + passed + shares_across + [copy for both in across for copy in both]:
        copy.wait_send()
    for s in range(planes - 1):
        for part in range(2):
            ring(s, part).wait_send()


def input_back(grad, some, attended_ref, x_ref, gain_ref, out_ref):
    x = x_ref[some, :].astype(F32)
    ratio = lax.rsqrt(jnp.mean(x * x, axis=1, keepdims=True) + EPSILON)
    u, xh = grad * gain_ref[...], x * ratio
    back = ratio * (u - xh * jnp.mean(u * xh, axis=1, keepdims=True))
    out_ref[some, :] = attended_ref[some, :] + back


def end_moves(collective, grads, gn, block_out, w, grad_attended, x, gain, attended):
    planes, _, rows, columns = grads.shape
    here, features = rows // 4, x.shape[1]
    any_place, in_vmem = pl.BlockSpec(memory_space=pl.ANY), pl.BlockSpec(memory_space=pltpu.VMEM)
    blocks = pltpu.VMEM((planes, rows, columns), BF16)
    sem = pltpu.SemaphoreType.DMA
    half = (x.shape[0] // 2, features)
    return pl.pallas_call(
        functools.partial(end_kernel, planes),
        name="end_moves",
        out_shape=[
            jax.ShapeDtypeStruct((2, 4, here, columns), BF16), jax.ShapeDtypeStruct((2,) + w.shape, BF16),
            jax.ShapeDtypeStruct(x.shape, F32), jax.ShapeDtypeStruct(x.shape, BF16),
        ],
        in_specs=[any_place] * 4 + [in_vmem] * 4,
        out_specs=[any_place] * 2 + [in_vmem] * 2,
        scratch_shapes=[
            blocks, blocks, pltpu.VMEM((planes - 1, rows, columns), BF16), blocks,
            pltpu.VMEM(gn.shape, gn.dtype),
            pltpu.VMEM((2, 2) + half, BF16),
            sem((planes,)), sem((planes, 2)), sem((planes, 2)), sem((planes - 1, 2)), sem((planes - 1, 2)), sem((8,)), sem((8,)),
            sem((2,)), sem((2,)), sem((2,)), sem((4,)), sem((2,)), sem((2,)), sem((2,)),
        ] + sum_rooms(*x.shape) + sum_rooms(*x.shape),
        compiler_params=pltpu.CompilerParams(collective_id=collective, has_side_effects=True, vmem_limit_bytes=60 << 20),
        cost_estimate=cost(95),
    )(grads, gn, block_out, w, grad_attended, x, gain, attended)


def dot(a, b, dims):
    return lax.dot_general(a, b, dims, preferred_element_type=F32)


def parts_of(a):
    high = a.astype(BF16)
    return high, (a - high.astype(F32)).astype(BF16)


def dot_parts(a, b, dims):
    return dot(a[0], b[0], dims) + (dot(a[1], b[0], dims) + dot(a[0], b[1], dims))


def dot_ones(ones, a):
    high = a.astype(BF16)
    rest = a - high.astype(F32)
    middle = rest.astype(BF16)
    low = (rest - middle.astype(F32)).astype(BF16)
    return dot(ones, high, NN) + (dot(ones, middle, NN) + dot(ones, low, NN))


def places():
    shape = (TILE, TILE)
    return lax.broadcasted_iota(jnp.int32, shape, 0), lax.broadcasted_iota(jnp.int32, shape, 1)


def ones_where(mask):
    return jnp.where(mask, 1.0, 0.0).astype(BF16)


def steps_to_middle(half):
    t, s = places()
    block = 2 * half
    same = (t // block) == (s // block)
    t_right, s_right = (t % block) >= half, (s % block) >= half
    right = t_right & s_right & (s <= t)
    left = jnp.logical_not(t_right | s_right) & (s > t)
    return ones_where(same & (right | left))


def pair_mask(half, turned=False):
    t, s = places()
    if turned:
        t, s = s, t
    block = 2 * half
    return ((t // block) == (s // block)) & ((t % block) >= half) & ((s % block) < half)


def first_row(rows):
    return lax.broadcasted_iota(jnp.int32, (rows, 2 * SLOTS), 1) < SLOTS


def row_sums(a, first):
    return (
        jnp.sum(jnp.where(first, a, 0.0), axis=1, keepdims=True),
        jnp.sum(jnp.where(first, 0.0, a), axis=1, keepdims=True),
    )


def tile_rows(j):
    return pl.ds(pl.multiple_of(j * TILE, TILE), TILE)


def prepare(lf_ref, decay_ref, reach_ref, e_ref, tiles):
    t, s = places()

    @pl.loop(0, tiles)
    def _(j):
        rows = tile_rows(j)
        lf = lf_ref[rows, :]
        decay_ref[rows, :] = dot_ones(ones_where(s <= t), lf)
        reach_ref[rows, :] = dot_ones(ones_where(s > t), lf)
        for level, half in enumerate(HALVES):
            e_ref[level, rows, :] = jnp.exp(dot_ones(steps_to_middle(half), lf))


def far_pairs(tiles):
    out, half = [], tiles // 2
    while half >= 1:
        for start in range(0, tiles, 2 * half):
            out.append((start + half, start, half))
        half //= 2
    return out


def far_decays(right, left, half, decay_ref, reach_ref):
    after, total = [], None
    for j in range(right, right + half):
        part = decay_ref[j * TILE:(j + 1) * TILE, :]
        after.append(jnp.exp(part if total is None else part + total))
        last = part[TILE - 1:TILE, :]
        total = last if total is None else total + last
    before, total = [], None
    for j in range(left + half - 1, left - 1, -1):
        part = reach_ref[j * TILE:(j + 1) * TILE, :]
        before.append(jnp.exp(part if total is None else part + total))
        whole = decay_ref[(j + 1) * TILE - 1:(j + 1) * TILE, :]
        total = whole if total is None else total + whole
    if half == 1:
        return after[0], before[0]
    return jnp.concatenate(after, axis=0), jnp.concatenate(before[::-1], axis=0)


def diagonal_of(block):
    t, s = places()
    return jnp.sum(jnp.where(t == s, block, 0.0), axis=1, keepdims=True)


def weighted_sums(a_ref, out_ref, gain_ref, decay_ref, reach_ref, e_ref, tiles):
    first = first_row(TILE)

    @pl.loop(0, tiles)
    def _(j):
        rows = tile_rows(j)
        gain = gain_ref[rows, :]
        blocks = [a_ref[r, rows, rows] for r in range(2)]
        total = jnp.where(first, diagonal_of(blocks[0]), diagonal_of(blocks[1])) * gain
        for level, half in enumerate(HALVES):
            e = e_ref[level, rows, :]
            x = parts_of(e * gain)
            pairs = pair_mask(half)
            y = [dot_parts(parts_of(jnp.where(pairs, a, 0.0)), x, NN) for a in blocks]
            total = total + e * jnp.where(first, y[0], y[1])
        out_ref[rows, :] = total

    for right, left, half in far_pairs(tiles):
        after, before = far_decays(right, left, half, decay_ref, reach_ref)
        here = slice(right * TILE, (right + half) * TILE)
        there = slice(left * TILE, (left + half) * TILE)
        x = parts_of(before * gain_ref[there, :])
        y = [dot_parts(parts_of(a_ref[r, here, there]), x, NN) for r in range(2)]
        out_ref[here, :] += after * jnp.where(first_row(half * TILE), y[0], y[1])


def split_rows(a, first):
    return parts_of(jnp.where(first, a, 0.0)), parts_of(jnp.where(first, 0.0, a))


def paired_weights(p_ref, out_ref, gain_ref, decay_ref, reach_ref, e_ref, tiles):
    first = first_row(TILE)
    t, s = places()

    @pl.loop(0, tiles)
    def _(j):
        rows = tile_rows(j)
        gain, p = gain_ref[rows, :], p_ref[rows, :]
        sums = row_sums(p * gain, first)
        total = [jnp.where(t == s, sums[r], 0.0) for r in range(2)]
        for level, half in enumerate(HALVES):
            e = e_ref[level, rows, :]
            x = parts_of(e * gain)
            pairs = pair_mask(half)
            pe = split_rows(p * e, first)
            total = [total[r] + jnp.where(pairs, dot_parts(pe[r], x, NT), 0.0) for r in range(2)]
        for r in range(2):
            out_ref[r, rows, rows] = total[r]

    for right, left, half in far_pairs(tiles):
        after, before = far_decays(right, left, half, decay_ref, reach_ref)
        here = slice(right * TILE, (right + half) * TILE)
        there = slice(left * TILE, (left + half) * TILE)
        x = parts_of(before * gain_ref[there, :])
        pe = split_rows(p_ref[here, :] * after, first_row(half * TILE))
        for r in range(2):
            out_ref[r, here, there] = dot_parts(pe[r], x, NT)
            out_ref[r, there, here] = jnp.zeros((half * TILE, half * TILE), F32)


def inner(a, b, r):
    return dot(a[0][r], b[0][r], NT) + dot(a[1][r], b[1][r], NT)


def sigmoid(v):
    return 1.0 / (1.0 + jnp.exp(-v))


def projections(pre_ref, which, length, act):
    depth = DEPTH // 2
    return [
        [act(pre_ref[f, r * length:(r + 1) * length, which * depth:(which + 1) * depth]) for r in range(2)]
        for f in range(2)
    ]


def document_numbers(begins_ref, length):
    starts = [
        jnp.concatenate([begins_ref[2 * r, :1, :], begins_ref[2 * r + 1, :1, :]], axis=1).astype(F32) for r in range(2)
    ]
    place = lax.broadcasted_iota(jnp.int32, (8, length), 0)
    starts = jnp.where(place == 0, starts[0], jnp.where(place == 1, starts[1], 0.0)).astype(BF16)
    s = lax.broadcasted_iota(jnp.int32, (length, length), 0)
    t = lax.broadcasted_iota(jnp.int32, (length, length), 1)
    counts = dot(starts, ones_where(s <= t), NN)
    turned = counts.T
    return [(turned[:, r:r + 1], counts[r:r + 1, :]) for r in range(2)]


def silu_low(v):
    return (v * sigmoid(v)).astype(BF16)


def low(v):
    return v.astype(BF16)


def forward_kernel(pre_ref, lf_ref, gain_ref, begins_ref,
                   mixed_ref, s_ref, p_ref, b_ref, a_ref, decay_ref, reach_ref, e_ref):
    length = lf_ref.shape[0]
    tiles = length // TILE
    scale = DEPTH ** -0.5
    documents = document_numbers(begins_ref, length)
    q, k = projections(pre_ref, 0, length, silu_low), projections(pre_ref, 1, length, silu_low)
    for r in range(2):
        same = documents[r][0] == documents[r][1]
        a_ref[r] = jnp.where(same, inner(q, k, r), 0.0)
    prepare(lf_ref, decay_ref, reach_ref, e_ref, tiles)
    weighted_sums(a_ref, s_ref, gain_ref, decay_ref, reach_ref, e_ref, tiles)
    first = first_row(length)
    logits = s_ref[...] * scale
    least = -jnp.inf
    top = jnp.where(
        first,
        jnp.max(jnp.where(first, logits, least), axis=1, keepdims=True),
        jnp.max(jnp.where(first, least, logits), axis=1, keepdims=True),
    )
    grown = jnp.exp(logits - top)
    sums = row_sums(grown, first)
    p_ref[...] = grown / jnp.where(first, sums[0], sums[1])
    paired_weights(p_ref, b_ref, gain_ref, decay_ref, reach_ref, e_ref, tiles)
    v = projections(pre_ref, 2, length, low)
    for r in range(2):
        b = jnp.where(documents[r][0] == documents[r][1], b_ref[r], 0.0)
        b_ref[r] = b
        high, rest = parts_of(b)
        for f in range(2):
            mixed = (dot(high, v[f][r], NN) + dot(rest, v[f][r], NN)).astype(BF16)
            for place in range(2):
                mixed_ref[r, place, f] = mixed[place * length // 2:(place + 1) * length // 2]


def to_columns(r, f):
    t, s = places()
    half = SLOTS // 2
    return ones_where((s < half) & (t == s + r * SLOTS + f * half))


def backward_kernel(pre_ref, g_ref, lf_ref, gain_ref, rate_ref, begins_ref, s_ref, p_ref, b_ref,
                    out_ref, bias_ref, a_ref, at_ref, dot_ref, h_ref, back_ref, decay_ref, reach_ref, e_ref):
    length = lf_ref.shape[0]
    tiles, depth = length // TILE, DEPTH // 2
    scale = DEPTH ** -0.5
    first_all, first = first_row(length), first_row(TILE)
    t, s = places()
    documents = document_numbers(begins_ref, length)
    q, k = projections(pre_ref, 0, length, silu_low), projections(pre_ref, 1, length, silu_low)
    v = projections(pre_ref, 2, length, low)
    grads = [[g_ref[r, :, f].reshape(length, depth) for r in range(2)] for f in range(2)]
    for r in range(2):
        same = documents[r][0] == documents[r][1]
        a_ref[r] = jnp.where(same, inner(grads, v, r), 0.0)
        at_ref[0, r] = jnp.where(same, inner(k, q, r), 0.0)
        at_ref[1, r] = jnp.where(same, inner(v, grads, r), 0.0)
    prepare(lf_ref, decay_ref, reach_ref, e_ref, tiles)
    weighted_sums(a_ref, dot_ref, gain_ref, decay_ref, reach_ref, e_ref, tiles)
    p, dots = p_ref[...], dot_ref[...]
    sums = row_sums(p * dots, first_all)
    h = scale * (p * (dots - jnp.where(first_all, sums[0], sums[1])))
    h_ref[...] = h
    dot_ref[...] = h * s_ref[...] + p * dots
    paired_weights(h_ref, a_ref, gain_ref, decay_ref, reach_ref, e_ref, tiles)
    @pl.loop(0, tiles)
    def _(j):
        rows = tile_rows(j)
        h, p = h_ref[rows, :], p_ref[rows, :]
        keys = [at_ref[0, r, rows, rows] for r in range(2)]
        values = [at_ref[1, r, rows, rows] for r in range(2)]
        total = (
            jnp.where(first, diagonal_of(keys[0]), diagonal_of(keys[1])) * h
            + jnp.where(first, diagonal_of(values[0]), diagonal_of(values[1])) * p
        )
        for level, half in enumerate(HALVES):
            e = e_ref[level, rows, :]
            he, pe = parts_of(h * e), parts_of(p * e)
            pairs = pair_mask(half, turned=True)
            y = [
                dot_parts(parts_of(jnp.where(pairs, keys[r], 0.0)), he, NN)
                + dot_parts(parts_of(jnp.where(pairs, values[r], 0.0)), pe, NN)
                for r in range(2)
            ]
            total = total + e * jnp.where(first, y[0], y[1])
        back_ref[rows, :] = total

    for right, left, half in far_pairs(tiles):
        after, before = far_decays(right, left, half, decay_ref, reach_ref)
        here = slice(right * TILE, (right + half) * TILE)
        there = slice(left * TILE, (left + half) * TILE)
        he, pe = parts_of(h_ref[here, :] * after), parts_of(p_ref[here, :] * after)
        y = [
            dot_parts(parts_of(at_ref[0, r, there, here]), he, NN)
            + dot_parts(parts_of(at_ref[1, r, there, here]), pe, NN)
            for r in range(2)
        ]
        back_ref[there, :] += before * jnp.where(first_row(half * TILE), y[0], y[1])

    for r in range(2):
        rows = slice(r * length, (r + 1) * length)
        c = parts_of(jnp.where(documents[r][0] == documents[r][1], a_ref[r], 0.0))
        w = parts_of(b_ref[r])
        for f in range(2):
            gq = dot(c[0], k[f][r], NN) + dot(c[1], k[f][r], NN)
            out_ref[f, rows, :depth] = (gq * slope(pre_ref[f, rows, :depth])).astype(BF16)
            gk = dot(c[0], q[f][r], TN) + dot(c[1], q[f][r], TN)
            out_ref[f, rows, depth:2 * depth] = (gk * slope(pre_ref[f, rows, depth:2 * depth])).astype(BF16)
            gv = dot(w[0], grads[f][r], TN) + dot(w[1], grads[f][r], TN)
            out_ref[f, rows, 2 * depth:3 * depth] = gv.astype(BF16)
    carried = jnp.zeros((1, 2 * SLOTS), F32)
    for j in range(tiles - 1, -1, -1):
        rows = slice(j * TILE, (j + 1) * TILE)
        back = back_ref[rows, :]
        change = dot_ref[rows, :] - gain_ref[rows, :] * back
        upward = dot_ones(ones_where(s >= t), change) + carried
        h_ref[rows, :] = (upward - jnp.exp(lf_ref[rows, :]) * back) * rate_ref[rows, :]
        carried = upward[0:1, :]
    grad_z = h_ref[...]
    bias_ref[...] = jnp.broadcast_to(jnp.sum(grad_z, axis=0, keepdims=True), bias_ref.shape)
    for r in range(2):
        for f in range(2):
            out_ref[f, r * length:(r + 1) * length, 3 * depth:] = dot(grad_z.astype(BF16), to_columns(r, f), NN).astype(BF16)


def slope(v):
    s = sigmoid(v)
    return s * (1.0 + v * (1.0 - s))


def mix_forward(pre, lf, gain, begins, moves, collective):
    length = lf.shape[0]
    lanes = (length, 2 * SLOTS)
    square = (2, length, length)
    in_vmem = pl.BlockSpec(memory_space=pltpu.VMEM)
    return compute(
        forward_kernel, "mix_forward", (pre, lf, gain, begins), [in_vmem] * 4, [in_vmem] * 4,
        (
            jax.ShapeDtypeStruct((2, 2, 2, length // 2, DEPTH // 2), BF16), jax.ShapeDtypeStruct(lanes, F32),
            jax.ShapeDtypeStruct(lanes, F32), jax.ShapeDtypeStruct(square, F32),
        ),
        24, scratch=[
            pltpu.VMEM(square, F32), pltpu.VMEM(lanes, F32), pltpu.VMEM(lanes, F32),
            pltpu.VMEM((len(HALVES),) + lanes, F32),
        ],
        moves=moves, collective=collective,
    )


def mix_backward(pre, g, lf, gain, rate, begins, s, p, b, moves, collective):
    length = lf.shape[0]
    lanes = (length, 2 * SLOTS)
    square = (2, length, length)
    in_vmem = pl.BlockSpec(memory_space=pltpu.VMEM)
    return compute(
        backward_kernel, "mix_backward", (pre, g, lf, gain, rate, begins, s, p, b),
        [in_vmem] * 9, [in_vmem] * 2,
        (jax.ShapeDtypeStruct(pre.shape, BF16), jax.ShapeDtypeStruct((8, 2 * SLOTS), F32)), 30,
        scratch=[pltpu.VMEM(square, F32), pltpu.VMEM((2,) + square, F32)] + [pltpu.VMEM(lanes, F32)] * 5
        + [pltpu.VMEM((len(HALVES),) + lanes, F32)],
        moves=moves, collective=collective,
    )


def hidden_kernel(nf_ref, w_ref, hidden_ref, slope_ref, silu_ref):
    units = hidden_ref.shape[2]
    both = dot(nf_ref[...], w_ref[0], NN)
    gate, up = both[:, :units], both[:, units:]
    s = sigmoid(gate)
    silu = gate * s
    hidden_ref[0] = (silu * up).astype(BF16)
    slope_ref[0] = (up * (s * (1.0 + gate * (1.0 - s)))).astype(BF16)
    silu_ref[0] = silu.astype(BF16)


def unit_specs(tokens, features, units):
    rows = tokens // 2
    return (
        pl.BlockSpec((rows, features), lambda h, t: (t, 0)),
        pl.BlockSpec((1, features, 2 * units), lambda h, t: (h, 0, 0)),
        pl.BlockSpec((1, rows, units), lambda h, t: (h, t, 0)),
        jax.ShapeDtypeStruct((2, tokens, units), BF16),
    )


def hidden_units(nf, w, moves, collective):
    some, weight, unit, units_all = unit_specs(*nf.shape, w.shape[2] // 2)
    return compute(
        hidden_kernel, "hidden_units", (nf, w), [some, weight], [unit] * 3, [units_all] * 3, 22, grid=(2, 2),
        moves=moves, collective=collective,
    )


def hidden_grads_kernel(cot_ref, slope_ref, silu_ref, w_ref, wd_ref, grads_ref, back_ref, total_ref):
    half, tile = pl.program_id(0), pl.program_id(1)
    rows = cot_ref.shape[0]
    here = pl.ds(pl.multiple_of(tile * rows, rows), rows)
    grad = dot(cot_ref[...], wd_ref[0], NT)
    gate_up = [grad * slope_ref[0].astype(F32), grad * silu_ref[0].astype(F32)]
    grads = jnp.concatenate(gate_up, axis=1).astype(BF16)
    grads_ref[0] = grads
    back = dot(grads, w_ref[0], NT)

    @pl.when(half == 0)
    def _():
        total_ref[here, :] = back

    @pl.when(half == 1)
    def _():
        back_ref[...] = (total_ref[here, :] + back).astype(BF16)


def hidden_grads(cot, slopes, silus, w, wd):
    tokens, features = cot.shape
    units = slopes.shape[2]
    some, weight, unit, _ = unit_specs(tokens, features, units)
    return compute(
        hidden_grads_kernel, "hidden_grads", (cot, slopes, silus, w, wd),
        [some, unit, unit, weight, pl.BlockSpec((1, units, features), lambda h, t: (h, 0, 0))],
        [
            pl.BlockSpec((1, tokens // 2, 2 * units), lambda h, t: (h, t, 0)),
            pl.BlockSpec((tokens // 2, features), lambda h, t: (h * t, 0)),
        ],
        [jax.ShapeDtypeStruct((2, tokens, 2 * units), BF16), jax.ShapeDtypeStruct(cot.shape, BF16)],
        34, grid=(2, 2), scratch=[pltpu.VMEM((tokens, features), F32)],
    )


def out_kernel(mixed_ref, other_ref, grad_ref, out_ref):
    core = lax.axis_index("c")
    grads = None
    for x in range(2):
        part = dot(mixed_ref[x, core, 0], grad_ref[2 * core + x], TN) + dot(other_ref[x, 0], grad_ref[2 * (1 - core) + x], TN)
        grads = part if grads is None else grads + part
    rows, wide = out_ref.shape[2:]
    for z in range(out_ref.shape[0]):
        for f in range(2):
            out_ref[z, f] = grads[z * rows:(z + 1) * rows, f * wide:(f + 1) * wide].astype(BF16)


def out_grads(mixed, other, grad):
    planes = lax.axis_size("z")
    features = grad.shape[2]
    wide = mixed.shape[4]
    rows = 2 * wide // planes
    return compute(
        out_kernel, "out_grads", (mixed, other, grad),
        [
            pl.BlockSpec((2, 2, 1) + mixed.shape[3:], lambda f: (0, 0, f, 0, 0)),
            pl.BlockSpec((2, 1) + other.shape[2:], lambda f: (0, f, 0, 0)), pl.BlockSpec(grad.shape, lambda f: (0, 0, 0)),
        ],
        [pl.BlockSpec((planes // 2, 2, rows, features // 2), lambda f: (f, 0, 0, 0))],
        [jax.ShapeDtypeStruct((planes, 2, rows, features // 2), BF16)], 8, grid=(2,),
    )[0]


def block_kernel(hidden_ref, wd_ref, out_ref):
    out_ref[...] = (dot(hidden_ref[0], wd_ref[0], NN) + dot(hidden_ref[1], wd_ref[1], NN)).astype(BF16)


def block_outputs(hidden, wd, moves, collective):
    tokens, features = hidden.shape[1], wd.shape[2]
    rows = tokens // 2
    return compute(
        block_kernel, "block_outputs", (hidden, wd),
        [pl.BlockSpec((2, rows, hidden.shape[2]), lambda t: (0, t, 0)), pl.BlockSpec(wd.shape, lambda t: (0, 0, 0))],
        [pl.BlockSpec((rows, features), lambda t: (t, 0))], [jax.ShapeDtypeStruct((tokens, features), BF16)],
        12, grid=(2,), moves=moves, collective=collective,
    )


def weight_kernel(a_ref, b_ref, out_ref):
    out_ref[0, 0] = dot(a_ref[...], b_ref[0], TN).astype(BF16)


def weight_grads(a, b, us, moves=(), collective=None):
    planes = lax.axis_size("z")
    tokens, features = a.shape
    rows, columns = features // planes, b.shape[2]
    return compute(
        weight_kernel, "weight_grads", (a, b),
        [pl.BlockSpec((tokens, rows), lambda h, z: (0, z)), pl.BlockSpec((1, tokens, columns), lambda h, z: (h, 0, 0))],
        [pl.BlockSpec((1, 1, rows, columns), lambda h, z: (z, h, 0, 0))],
        [jax.ShapeDtypeStruct((planes, 2, rows, columns), BF16)], us, grid=(2, planes), moves=moves, collective=collective,
    )


def mixer_weight_kernel(a_ref, b_ref, sums_ref, out_ref):
    grads = dot(a_ref[...], b_ref[0], TN)
    wide = grads.shape[1] - TILE
    out_ref[0, 0, :, :wide] = grads[:, :wide].astype(BF16)
    once = jnp.where(pl.program_id(0) == 0, 1.0, 0.0)
    out_ref[0, 0, :, wide:] = (grads[:, wide:] + once * sums_ref[...]).astype(BF16)


def mixer_weight_grads(a, b, sums, moves, collective):
    planes = lax.axis_size("z")
    tokens, features = a.shape
    rows, columns = features // planes, b.shape[2]
    return compute(
        mixer_weight_kernel, "mixer_weight_grads", (a, b, sums),
        [
            pl.BlockSpec((tokens, rows), lambda h, z: (0, z)), pl.BlockSpec((1, tokens, columns), lambda h, z: (h, 0, 0)),
            pl.BlockSpec((rows, TILE), lambda h, z: (z, 0)),
        ],
        [pl.BlockSpec((1, 1, rows, columns), lambda h, z: (z, h, 0, 0))],
        [jax.ShapeDtypeStruct((planes, 2, rows, columns), BF16)], 20, grid=(2, planes), moves=moves, collective=collective,
    )


def down_kernel(hidden_ref, cot_ref, out_ref):
    grads = dot(hidden_ref[0], cot_ref[...], TN)
    rows = out_ref.shape[2]
    for z in range(out_ref.shape[0]):
        out_ref[z, 0] = grads[z * rows:(z + 1) * rows].astype(BF16)


def down_grads(hidden, cot):
    planes = lax.axis_size("z")
    tokens, features = cot.shape
    units = hidden.shape[2]
    wide = features // 2
    return pl.pallas_call(
        down_kernel,
        name="down_grads",
        grid=(2, 2),
        in_specs=[
            pl.BlockSpec((1, tokens, units), lambda h, i: (h, 0, 0)),
            pl.BlockSpec((tokens, wide), lambda h, i: (0, i)),
        ],
        out_specs=pl.BlockSpec((planes, 1, units // planes, wide), lambda h, i: (0, h, 0, i)),
        out_shape=jax.ShapeDtypeStruct((planes, 2, units // planes, features), BF16),
        compiler_params=pltpu.CompilerParams(vmem_limit_bytes=60 << 20),
        cost_estimate=cost(12),
    )(hidden, cot)


def input_kernel(grad_ref, w_ref, x_ref, out_ref, sums_ref):
    tile = pl.program_id(0)
    back = dot(grad_ref[0], w_ref[0], NT) + dot(grad_ref[1], w_ref[1], NT)
    out_ref[...] = back.astype(BF16)
    x = x_ref[...].astype(F32)
    xh = x * lax.rsqrt(jnp.mean(x * x, axis=1, keepdims=True) + EPSILON)
    sums = jnp.sum((back * xh).reshape(-1, 8, back.shape[1]), axis=0)
    sums_ref[...] = jnp.where(tile == 0, sums, sums_ref[...] + sums)


def input_grads(grad, w, x):
    tokens, features = x.shape
    rows = tokens // 4
    return compute(
        input_kernel, "input_grads", (grad, w, x),
        [
            pl.BlockSpec((2, rows, grad.shape[2]), lambda t: (0, t, 0)), pl.BlockSpec(w.shape, lambda t: (0, 0, 0)),
            pl.BlockSpec((rows, features), lambda t: (t, 0)),
        ],
        [pl.BlockSpec((rows, features), lambda t: (t, 0)), pl.BlockSpec((8, features), lambda t: (0, 0))],
        [jax.ShapeDtypeStruct(x.shape, BF16), jax.ShapeDtypeStruct((8, features), F32)],
        14, grid=(4,),
    )


def project_kernel(vectors, x_ref, w_ref, normed_ref, pre_ref, gains_ref):
    @pl.when(pl.program_id(0) == 0)
    def _():
        first = vectors // TILE * TILE
        columns = w_ref[0, :, first:first + TILE].astype(F32).T
        gains_ref[...] = columns[vectors - first:vectors - first + 8, :]

    x = x_ref[...].astype(F32)
    ratio = lax.rsqrt(jnp.mean(x * x, axis=1, keepdims=True) + EPSILON)
    normed = (x * ratio * gains_ref[0:1, :]).astype(BF16)
    normed_ref[...] = normed
    for f in range(2):
        pre_ref[f] = dot(normed, w_ref[f], NN)


def project(x, w, vectors, moves, collective):
    tokens, features = x.shape
    rows, columns = tokens // 4, w.shape[2]
    some = pl.BlockSpec((rows, features), lambda t: (t, 0))
    return compute(
        functools.partial(project_kernel, vectors), "project", (x, w),
        [some, pl.BlockSpec(w.shape, lambda t: (0, 0, 0))],
        [some, pl.BlockSpec((2, rows, columns), lambda t: (0, t, 0)), pl.BlockSpec((8, features), lambda t: (0, 0))],
        [
            jax.ShapeDtypeStruct(x.shape, BF16), jax.ShapeDtypeStruct((2, tokens, columns), F32),
            jax.ShapeDtypeStruct((8, features), F32),
        ],
        28, grid=(4,), moves=moves, collective=collective,
    )


def finish_kernel(planes, a_ref, mixer_ref, w_ref, gate_ref, up_ref, *refs):
    *mixer_out, forget_ref, w_out_ref, sums_ref = refs
    piece = gate_ref.shape[1] // (8 * planes)
    wide, slots = DEPTH // 2, SLOTS // 2
    sums = None
    for core in range(2):
        for chip in range(4):
            block = a_ref[core, chip].astype(F32)
            for n, out_ref in enumerate((gate_ref, up_ref)):
                for z in range(planes):
                    start = ((z * 4 + chip) * 2 + core) * piece
                    out_ref[:, start:start + piece] = block[:, (n * planes + z) * piece:(n * planes + z + 1) * piece]
            at = 2 * chip + core
            for n, out_ref in enumerate(mixer_out):
                out_ref[:, at * wide:(at + 1) * wide] = mixer_ref[core, chip, :, n * wide:(n + 1) * wide].astype(F32)
            last = mixer_ref[core, chip, :, 3 * wide:].astype(F32)
            forget_ref[:, at * slots:(at + 1) * slots] = last[:, :slots]
            if core == 0:
                sums = last if sums is None else sums + last
        columns = w_ref.shape[2]
        w_out_ref[:, core * columns:(core + 1) * columns] = w_ref[core].astype(F32)
    sums_ref[...] = sums.T[slots:slots + 8, :]


def finish(a, mixer, w, columns):
    rows = a.shape[2]
    in_vmem = pl.BlockSpec(memory_space=pltpu.VMEM)
    widths = [columns, columns] + [HEADS * DEPTH] * 3 + [HEADS * SLOTS, HEADS * DEPTH]
    return compute(
        functools.partial(finish_kernel, lax.axis_size("z")), "finish", (a, mixer, w), [in_vmem] * 3,
        [in_vmem] * 8, [jax.ShapeDtypeStruct((rows, width), F32) for width in widths] + [jax.ShapeDtypeStruct((8, rows), F32)],
        10,
    )


def gather_planes(a):
    return lax.all_gather(a, ("c", "z"), axis=0, tiled=True).reshape((2, -1) + a.shape[1:])


def sum_planes(a):
    return lax.psum_scatter(a.reshape((-1,) + a.shape[2:]), ("z", "c"), scatter_dimension=0, tiled=True)[0]


def swap(a, axis):
    return lax.ppermute(a, axis, [(0, 1), (1, 0)])


def both_of(a, axis):
    other = swap(a, axis)
    return jnp.where(lax.axis_index(axis) == 0, jnp.stack([a, other]), jnp.stack([other, a]))


def scaled(features):
    return lax.rsqrt(jnp.mean(features * features, axis=-1, keepdims=True) + EPSILON)


def norm_back(grad, gain, features, ratio):
    u, xh = grad * gain, features * ratio
    return ratio * (u - xh * jnp.mean(u * xh, axis=-1, keepdims=True))


def body(inputs, starts, norm_attn, w_query, w_key, w_value, w_forget, gate_bias, w_out, norm_ffn, w_gate, w_up,
         w_down, cotangent):
    positions, features = inputs.shape[1:]
    depth = features // HEADS
    y, x, c, z = (lax.axis_index(name) for name in ("y", "x", "c", "z"))
    planes = lax.axis_size("z")
    head = y * 2 + x
    rows_here = w_query.shape[0]
    hidden_here = w_down.shape[0]

    def own_half(a, axis, at=c):
        return lax.dynamic_index_in_dim(a, at, axis, keepdims=False)

    bias_here = gate_bias.shape[0]

    def column(v):
        v = jnp.pad(v, (0, rows_here - v.shape[0]))
        return jnp.broadcast_to(v[None, :, None], (HEADS, rows_here, 1))

    forget = own_half(w_forget.reshape(rows_here, HEADS, 2, SLOTS // 2), 2).transpose(1, 0, 2)
    rest = jnp.concatenate([forget] + [column(v) for v in (norm_attn, norm_ffn, gate_bias)], axis=-1)
    rest = jnp.pad(rest, ((0, 0), (0, 0), (0, TILE - rest.shape[-1])))
    vectors = 3 * depth // 2 + SLOTS // 2
    width = vectors + 3

    x_here = inputs.reshape(positions, features)
    cot_here = cotangent.reshape(positions, features)
    out_half = own_half(w_out.reshape(2, rows_here // 2, features), 0)
    out_half = lax.all_gather(out_half, "z", axis=0)
    full_down = gather_planes(own_half(w_down.reshape(2, hidden_here // 2, features), 0))
    begins, x_rows, hidden_w, mixer_w = start_moves(
        1, (w_query, w_key, w_value), rest, w_gate, w_up,
        (("copy_homes", jnp.broadcast_to(starts, (8, positions))), ("copy_homes", x_here)),
    )
    hidden_w = gather_planes(hidden_w.reshape(4 * rows_here, -1))
    mixer_w = mixer_w.reshape(2, features, -1)
    x_rows = x_rows.reshape(4 * positions, features)
    normed, pre, gains, out_core = project(x_rows, mixer_w, vectors, [("copy_chips", out_half)], 13)
    bias = gains[2].reshape(4 * planes, rows_here)[:, :bias_here].reshape(-1)
    bias = lax.dynamic_slice_in_dim(bias, head * SLOTS, SLOTS)
    z_total = pre[:, :, 3 * depth // 2:vectors].reshape(2, 2, 2 * positions, SLOTS // 2)
    z_total = z_total.transpose(2, 1, 0, 3).reshape(2 * positions, 2 * SLOTS) + jnp.tile(bias, 2)
    log_forget = jax.nn.log_sigmoid(z_total) / 8.0
    gain = -jnp.expm1(log_forget)
    mixed, scores, probs, paired, out_other, cot = mix_forward(
        pre, log_forget, gain, begins, [("swap_core", out_core), ("gather_near", cot_here)], 3
    )
    out_core, out_other = (a.reshape(features // 2, features) for a in (out_core, out_other))
    mixed_rows = mixed
    mixed, mixed_other = move(
        4, ("to_homes", mixed.reshape(4, 2 * positions, depth // 2)), ("swap_half", mixed), us=14
    )
    mixed = mixed.reshape(2 * HEADS, positions, depth // 2).transpose(1, 0, 2)
    mixed = mixed.reshape(positions, planes, 4, 2, rows_here // 2).transpose(3, 0, 2, 1, 4)
    mixed = mixed.reshape(2, positions, features // 2)
    attended = (
        x_here.astype(F32) + jnp.dot(own_half(mixed, 0), out_core, preferred_element_type=F32)
        + jnp.dot(own_half(mixed, 0, 1 - c), out_other, preferred_element_type=F32)
    )

    ratio_f = scaled(attended)
    (normed_ffn,) = move(5, ("copy_chips", (attended * ratio_f * gains[1]).astype(BF16)), us=38)
    normed_ffn = normed_ffn.reshape(4 * positions, features)
    hidden, slopes, silus, cot = hidden_units(normed_ffn, hidden_w, [("gather_far", cot)], 6)
    cot = cot.reshape(4 * positions, features)
    grad_down_w = down_grads(hidden, cot)
    grad_hidden, shares = hidden_grads(cot, slopes, silus, hidden_w, full_down)
    shares = shares.reshape(2, 2, positions, features)
    grad_hidden_w, near = weight_grads(
        normed_ffn, grad_hidden, 24, [("reduce_near", shares.reshape(4, positions, features))], 7
    )
    half = positions // 2
    own = [
        lax.dynamic_index_in_dim(shares[:, :, :half], x, 1, keepdims=False),
        lax.dynamic_index_in_dim(shares[:, :, half:], y, 0, keepdims=False),
    ]
    own = [jnp.where(at == 0, a[::-1], a) for at, a in zip((y, x), own)]
    near = jnp.stack(own).astype(F32) + near.astype(F32)
    block_out, far = block_outputs(hidden, full_down, [("reduce_far", near[:, 0].astype(BF16))], 8)
    grad_normed_ffn = (near[:, 1] + far.astype(F32)).reshape(positions, features)
    grad_down_w, grad_hidden_w = sum_planes(grad_down_w), sum_planes(grad_hidden_w)
    grad_gain_ffn = jnp.sum(grad_normed_ffn * attended * ratio_f, axis=0)
    grad_attended = cot_here.astype(F32) + norm_back(grad_normed_ffn, gains[1], attended, ratio_f)

    grad_branch = grad_attended.astype(BF16)
    grad_mixed = [
        jnp.einsum("te,de->td", grad_branch, w, preferred_element_type=F32).astype(BF16) for w in (out_core, out_other)
    ]
    grad_mixed = jnp.where(c == 0, jnp.stack(grad_mixed), jnp.stack(grad_mixed[::-1]))
    grad_mixed = grad_mixed.reshape(2, positions, 4, planes, rows_here // 2).transpose(1, 3, 2, 0, 4)
    grad_mixed = grad_mixed.reshape(positions, HEADS, 2, depth // 2).transpose(1, 2, 0, 3)
    (grad_mixed,) = move(
        9, ("from_homes", grad_mixed.reshape(4, 2 * positions, depth // 2)), after=(grad_down_w,), us=14
    )
    grad_mixed = grad_mixed.reshape(2, 2, 2, positions, depth // 2)
    rate = jax.nn.sigmoid(-z_total) / 8.0
    grad_pre, grad_bias, branch_chips = mix_backward(
        pre, grad_mixed, log_forget, gain, rate, begins, scores, probs, paired, [("copy_chips", grad_branch)], 10
    )
    grad_bias = jnp.sum(grad_bias[0].reshape(2, SLOTS), axis=0)
    grad_out_w = out_grads(mixed_rows, mixed_other, branch_chips)
    grad_normed, sums = input_grads(grad_pre, mixer_w, x_rows)
    grad_bias = jnp.zeros((HEADS, SLOTS), F32).at[head].set(grad_bias).reshape(4 * planes, bias_here)
    grad_bias = jnp.pad(grad_bias, ((0, 0), (0, rows_here - bias_here))).reshape(-1)
    sums = jnp.stack([jnp.sum(sums, axis=0), grad_gain_ffn, grad_bias], axis=-1)
    first_sum = vectors + TILE - mixer_w.shape[-1]
    sums = jnp.pad(sums, ((0, 0), (first_sum, TILE - first_sum - 3)))
    grad_mixer_w, grad_hidden_w = mixer_weight_grads(
        normed, grad_pre, sums, [("spread", grad_hidden_w.reshape(1, 4, rows_here, -1))], 14
    )
    grad_out_w = sum_planes(grad_out_w)
    mixer_rows, out_rows, grad_input, output = end_moves(
        11, grad_mixer_w, grad_normed.reshape(4, positions, features), block_out.reshape(4, positions, features),
        grad_out_w, grad_attended, x_here, gains[:1], attended,
    )
    grad_gate_w, grad_up_w, *grad_w, grad_forget_w, grad_out_w, sums = finish(
        grad_hidden_w[:, :, 0], mixer_rows, out_rows, w_gate.shape[1]
    )
    grad_down_w = both_of(grad_down_w, "c").reshape(hidden_here, features).astype(F32)
    return (
        output.reshape(inputs.shape), grad_input.reshape(inputs.shape), sums[0], grad_w[0], grad_w[1], grad_w[2],
        grad_forget_w, sums[2, :bias_here], grad_out_w, sums[1], grad_gate_w, grad_up_w, grad_down_w,
    )


def solution(mesh):
    planes = mesh.shape["dp"] // 4
    fine = Mesh(mesh.devices.reshape(planes, 2, 2, 2), ("z", "y", "x", "c"))
    dp = ("z", "y", "x")
    tokens, vector, matrix = P(dp, "c", None), P(dp), P(dp, None)
    in_specs = (
        tokens, P(dp, "c"), vector, matrix, matrix, matrix, matrix, vector, matrix, vector, matrix, matrix, matrix, tokens
    )
    out_specs = (
        tokens, tokens, vector, matrix, matrix, matrix, matrix, vector, matrix, vector, matrix, matrix, matrix
    )
    return jax.shard_map(body, mesh=fine, in_specs=in_specs, out_specs=out_specs, check_vma=False)
```
